32 devices in a mesh: groups: 2 (over y), row: 4 (over x, core), col: 4 (over z).
Axes of the slice: x: 2, y: 2, z: 4, core: 2. Of those that a mesh axis runs over, the one named last changes fastest.
Arguments:
- object_slab: float32 [2, 2, 2048, 2048], P(None, None, ('groups', 'row'), 'col'), parts along dimension 2, may hold values from -5 to 5
- probe_field: float32 [4, 256, 256], P('groups'), parts along dimension 0, may hold values from -6 to 6
- prop_phase: float32 [256, 256], replicated, may hold values from -3.140625 to 3.140625
- intensities: float32 [16, 1024, 256], P(('groups', 'row'), 'col'), parts along dimension 0, may hold values from 0.1 to 3
- corners: int32 [32, 4, 2], P(('groups', 'row'), 'col'), parts along dimension 0, may hold values from 0 to 256, as said below
- slot_source: int32 [16, 4], P(('groups', 'row'), 'col'), parts along dimension 0, may hold values from 0 to 3, as said below
Outputs:
- updated_slab: float32 [2, 2, 2048, 2048], P(None, None, ('groups', 'row'), 'col'), parts along dimension 2
- updated_probe: float32 [4, 256, 256], P('groups'), parts along dimension 0
The draws below stay inside these ranges and needn't reach their ends.
There are 2 independent parts, one for each index of `groups`. The reference program is written for one: setup_inputs(seed, part) draws one part's arguments, and reference() takes and returns one part's arrays. A program takes and returns all parts, laid end to end along the dimension named above; an argument that names none is the same for every part. Nothing has to cross between parts.
Inputs may be any that keep to these rules, and one draw needn't show every extreme that they name: `corners`: entry [t * 4 + d, c] gives the row and column, within tile (t, c), of the patch that scan owner d of column c may take from that tile; the row is below 256, the column at most 256. `slot_source`: entry [d * 2 + k, c] is the tile row of column c that holds slot k of scan owner (d, c); one owner's 2 entries differ; in each column no tile row is named more than 4 times, and some tile row exactly 4 times.
All inputs are finite; a program needn't handle non-finite values.
Results may differ from the reference program's by a relative error of at most 0.015.
The reference program's roundings to bfloat16 on the way count: a program that leaves them out, or rounds other values in their place, can miss the bound.
Values may be sent and summed in bfloat16 or wider, within the bound.
No kernel may reach another device: no remote copies, remote signals or barrier semaphores. Data moves between devices by JAX's collectives and lax.ppermute only.
A program may use at most 128 MiB of HBM per device.

```python
import math
import jax
import jax.numpy as jnp
from jax import lax

P_SIZE = 256
SLICES = 2
TH = 256
TW = 512
SLOTS = 2
OH = 1024
OW = 2048
N_ROW = 4
N_COL = 4


def draw_slot_source(key, part):
    key = jax.random.fold_in(key, 11)
    column_keys = jax.random.split(key, N_COL)
    orders = jax.vmap(lambda column_key: jax.random.permutation(column_key, N_ROW))(column_keys)
    owner_rows = jnp.arange(N_ROW, dtype=jnp.int32)
    starts = 2 * (owner_rows % max(N_ROW // 4, 1))
    places = (starts[:, None] + jnp.arange(SLOTS, dtype=jnp.int32)[None, :]) % N_ROW
    picked = orders[:, places]
    return jnp.transpose(picked, (1, 2, 0)).reshape(N_ROW * SLOTS, N_COL).astype(jnp.int32)


def draw_corners(key, part):
    key = jax.random.fold_in(key, 23)
    key_rows, key_cols = jax.random.split(key)
    row_part = jax.random.randint(key_rows, (N_ROW * N_ROW, N_COL, 1), 0, TH)
    col_part = jax.random.randint(key_cols, (N_ROW * N_ROW, N_COL, 1), 0, TW - P_SIZE + 1)
    return jnp.concatenate([row_part, col_part], axis=2).astype(jnp.int32)


def block_levels(own_key, shape, pieces, least, high):
    def one(axis_at, blocks):
        heights = jax.random.uniform(jax.random.fold_in(jax.random.fold_in(own_key, 6), axis_at), (blocks,), jnp.float32, least / len(pieces), high / len(pieces))
        return jnp.repeat(jnp.exp(heights), shape[axis_at] // blocks).reshape((-1,) + (1,) * (len(shape) - axis_at - 1))

    gain = one(*pieces[0])
    for cut in pieces[1:]:
        gain = gain * one(*cut)
    return gain


def bell_draw(stream_key, dims, spread, reach, cuts=(), kind=jnp.bfloat16):
    drawn = spread * jax.random.normal(stream_key, dims, jnp.float32)
    if cuts:
        drawn = drawn * block_levels(stream_key, dims, cuts, -0.22, 0.18)
    return jnp.clip(drawn, -reach, reach).astype(kind)


def setup_inputs(seed: int = 0, part: int = 0) -> dict:
    streams_of = jax.random.split(jax.random.key(seed), 7)
    part_keys = jax.random.split(jax.random.fold_in(streams_of[6], part), 7)
    return {
        "object_slab": bell_draw(part_keys[0], (SLICES, 2, OH, OW), 0.7, 5.0, ((2, 4), (3, 4)), jnp.float32),
        "probe_field": bell_draw(part_keys[1], (2, P_SIZE, P_SIZE), 1.0, 6.0, (), jnp.float32),
        "prop_phase": jnp.clip(jax.random.uniform(streams_of[2], (P_SIZE, P_SIZE), jnp.float32, -3.140625, 3.140625), -3.140625, 3.140625),
        "intensities": jnp.clip(jnp.exp(math.log(3.0) - 3.4011974 * jax.random.uniform(part_keys[3], (N_ROW * SLOTS, N_COL * P_SIZE, P_SIZE), jnp.float32) ** block_levels(part_keys[3], (N_ROW * SLOTS, N_COL * P_SIZE, P_SIZE), ((0, 4), (1, 4)), -0.2, 0.2)), 0.1, 3.0),
        "corners": draw_corners(jax.random.fold_in(jax.random.fold_in(streams_of[6], part), 71), part),
        "slot_source": draw_slot_source(jax.random.fold_in(jax.random.fold_in(streams_of[6], part), 71), part),
    }


step_object = 0.05
step_probe = 0.5

def dft_tables(length):
    index = jnp.arange(length, dtype=jnp.int32)
    phase_index = index[:, None] * index[None, :] % length
    angles = phase_index.astype(jnp.float32) * (2.0 * jnp.pi / length)
    scale_factor = 1.0 / jnp.sqrt(jnp.float32(length))
    table_re = (jnp.cos(angles) * scale_factor).astype(jnp.bfloat16)
    table_im = (-jnp.sin(angles) * scale_factor).astype(jnp.bfloat16)
    return (table_re, table_im)

def left_mult(table, field):
    return jnp.einsum('jk,bkl->bjl', table.astype(jnp.float32), field.astype(jnp.float32))

def right_mult(field, table):
    return jnp.einsum('bjk,kl->bjl', field.astype(jnp.float32), table.astype(jnp.float32))

def transform(real_part, imag_part, table_re, table_im):
    field_re = lax.optimization_barrier(real_part.astype(jnp.bfloat16))
    field_im = lax.optimization_barrier(imag_part.astype(jnp.bfloat16))
    middle_re = left_mult(table_re, field_re) - left_mult(table_im, field_im)
    middle_im = left_mult(table_re, field_im) + left_mult(table_im, field_re)
    middle_re = lax.optimization_barrier(middle_re.astype(jnp.bfloat16))
    middle_im = lax.optimization_barrier(middle_im.astype(jnp.bfloat16))
    out_re = right_mult(middle_re, table_re) - right_mult(middle_im, table_im)
    out_im = right_mult(middle_im, table_re) + right_mult(middle_re, table_im)
    return (out_re, out_im)

def patch_step(patches, probe_field, measured, table_re, table_im, kernel_re, kernel_im):
    slabs = patches.astype(jnp.float32)
    slab0_re, slab0_im = (slabs[:, 0, 0], slabs[:, 0, 1])
    slab1_re, slab1_im = (slabs[:, 1, 0], slabs[:, 1, 1])
    probe_re, probe_im = (probe_field[0], probe_field[1])
    front_re = probe_re * slab0_re - probe_im * slab0_im
    front_im = probe_re * slab0_im + probe_im * slab0_re
    freq_re, freq_im = transform(front_re, front_im, table_re, table_im)
    spread_re = kernel_re * freq_re - kernel_im * freq_im
    spread_im = kernel_re * freq_im + kernel_im * freq_re
    moved_re, moved_im = transform(spread_re, spread_im, table_re, -table_im)
    second_re = moved_re * slab1_re - moved_im * slab1_im
    second_im = moved_re * slab1_im + moved_im * slab1_re
    far_re, far_im = transform(second_re, second_im, table_re, table_im)
    misfit = far_re * far_re + far_im * far_im - measured
    weighted_re = misfit * far_re
    weighted_im = misfit * far_im
    back1_re, back1_im = transform(weighted_re, weighted_im, table_re, -table_im)
    grad1_re = moved_re * back1_re + moved_im * back1_im
    grad1_im = moved_re * back1_im - moved_im * back1_re
    carry_re = slab1_re * back1_re + slab1_im * back1_im
    carry_im = slab1_re * back1_im - slab1_im * back1_re
    echo_re, echo_im = transform(carry_re, carry_im, table_re, table_im)
    undo_re = kernel_re * echo_re + kernel_im * echo_im
    undo_im = kernel_re * echo_im - kernel_im * echo_re
    back0_re, back0_im = transform(undo_re, undo_im, table_re, -table_im)
    grad0_re = probe_re * back0_re + probe_im * back0_im
    grad0_im = probe_re * back0_im - probe_im * back0_re
    probe_grad_re = lax.optimization_barrier(jnp.sum(slab0_re * back0_re + slab0_im * back0_im, axis=0))
    probe_grad_im = lax.optimization_barrier(jnp.sum(slab0_re * back0_im - slab0_im * back0_re, axis=0))
    first_slice = jnp.stack([grad0_re, grad0_im], axis=1)
    second_slice = jnp.stack([grad1_re, grad1_im], axis=1)
    grad_patches = jnp.stack([first_slice, second_slice], axis=1).astype(jnp.bfloat16)
    return (grad_patches, jnp.stack([probe_grad_re, probe_grad_im], axis=0))

def reference(object_slab, probe_field, prop_phase, intensities, corners, slot_source):
    table_re, table_im = dft_tables(P_SIZE)
    kernel_re = jnp.cos(prop_phase)
    kernel_im = jnp.sin(prop_phase)
    padded = jnp.pad(object_slab, ((0, 0), (0, 0), (0, P_SIZE), (0, 0)))
    slot_index = jnp.arange(SLOTS, dtype=jnp.int32)

    def visit(carry, owner_index):
        grad_slab, grad_probe = carry
        owner_row = owner_index // N_COL
        owner_col = owner_index % N_COL
        sources = slot_source[owner_row * SLOTS + slot_index, owner_col]
        corner_y = corners[sources * N_ROW + owner_row, owner_col, 0]
        corner_x = corners[sources * N_ROW + owner_row, owner_col, 1]
        start_y = (sources * TH + corner_y).astype(jnp.int32)
        start_x = (owner_col * TW + corner_x).astype(jnp.int32)
        measured = lax.dynamic_slice(intensities, (owner_row * SLOTS, owner_col * P_SIZE, jnp.int32(0)), (SLOTS, P_SIZE, P_SIZE))

        def cut_patch(row_start, col_start):
            zero_index = jnp.int32(0)
            return lax.dynamic_slice(padded, (zero_index, zero_index, row_start, col_start), (SLICES, 2, P_SIZE, P_SIZE))
        patches = jax.vmap(cut_patch)(start_y, start_x).astype(jnp.bfloat16)
        grad_patches, probe_grad = patch_step(patches, probe_field, measured, table_re, table_im, kernel_re, kernel_im)
        for position in range(SLOTS):
            where = (jnp.int32(0), jnp.int32(0), start_y[position], start_x[position])
            piece = lax.dynamic_slice(grad_slab, where, (SLICES, 2, P_SIZE, P_SIZE))
            grad_slab = lax.dynamic_update_slice(grad_slab, piece + grad_patches[position].astype(jnp.float32), where)
        return ((grad_slab, grad_probe + probe_grad), None)
    start_carry = (jnp.zeros(padded.shape, jnp.float32), jnp.zeros(probe_field.shape, jnp.float32))
    finished, unused = lax.scan(visit, start_carry, jnp.arange(N_ROW * N_COL, dtype=jnp.int32))
    grad_slab, grad_probe = finished
    updated_slab = object_slab - step_object * grad_slab[:, :, :OH, :]
    updated_probe = probe_field - step_probe * grad_probe / (N_ROW * N_COL * SLOTS)
    return (updated_slab, updated_probe)
```

```python
import functools

import jax
import jax.numpy as jnp
from jax import lax
from jax.experimental import pallas as pl
from jax.experimental.pallas import tpu as pltpu
from jax.sharding import PartitionSpec as P

step_object = 0.05
step_probe = 0.5
VMEM_BYTES = 48 * 1024 * 1024


def permute_pairs(block, axis, partner):
    return lax.ppermute(block, axis, [(i, partner(i)) for i in range(lax.axis_size(axis))])


def from_behind(block, axis, distance):
    devices = range(lax.axis_size(axis))
    route = [(i - distance, i) for i in devices if i - distance in devices]
    return lax.ppermute(block, axis, route)


def dft_tables(length):
    index = jnp.arange(length, dtype=jnp.int32)
    phase_index = index[:, None] * index[None, :] % length
    angles = phase_index.astype(jnp.float32) * (2.0 * jnp.pi / length)
    scale_factor = 1.0 / jnp.sqrt(jnp.float32(length))
    table_re = (jnp.cos(angles) * scale_factor).astype(jnp.bfloat16)
    table_im = (-jnp.sin(angles) * scale_factor).astype(jnp.bfloat16)
    first = jnp.concatenate(
        [jnp.concatenate([table_re, -table_im], 1), jnp.concatenate([table_im, table_re], 1)], 0
    )
    second = jnp.concatenate(
        [jnp.concatenate([table_re, table_im], 1), jnp.concatenate([-table_im, table_re], 1)], 0
    )
    return first, second


def product(a, b):
    return jnp.dot(a, b, preferred_element_type=jnp.float32)


def transform(fields, left_table, right_table):
    count = len(fields)
    n = fields[0][0].shape[0]
    stacked = jnp.concatenate(
        [
            jnp.concatenate([f[0].astype(jnp.bfloat16) for f in fields], 1),
            jnp.concatenate([f[1].astype(jnp.bfloat16) for f in fields], 1),
        ],
        0,
    )
    middle = product(left_table, stacked).astype(jnp.bfloat16)
    middle = jnp.concatenate(
        [
            jnp.concatenate([middle[:n, p * n : (p + 1) * n], middle[n:, p * n : (p + 1) * n]], 1)
            for p in range(count)
        ],
        0,
    )
    out = product(middle, right_table)
    return [(out[p * n : (p + 1) * n, :n], out[p * n : (p + 1) * n, n:]) for p in range(count)]


def one_hot_rows(shape, offset):
    rows = lax.broadcasted_iota(jnp.int32, shape, 0)
    columns = lax.broadcasted_iota(jnp.int32, shape, 1)
    return (columns == rows + offset).astype(jnp.bfloat16)


def one_hot_columns(shape, offset):
    rows = lax.broadcasted_iota(jnp.int32, shape, 0)
    columns = lax.broadcasted_iota(jnp.int32, shape, 1)
    return (rows == columns + offset).astype(jnp.bfloat16)


def cut(own_ref, rim_ref, n, corner_y, corner_x):
    height = own_ref.shape[1] + rim_ref.shape[1]
    width = own_ref.shape[2]
    planes = jnp.concatenate(
        [jnp.concatenate([own_ref[c], rim_ref[c]], 0) for c in range(2)], 1
    )
    rows = product(one_hot_rows((n, height), corner_y), planes).astype(jnp.bfloat16)
    rows = jnp.concatenate([rows[:, :width], rows[:, width:]], 0)
    both = product(rows, one_hot_columns((width, n), corner_x))
    return both[:n], both[n:]


def first_kernel(corner_ref, own_ref, rim_ref, probe_ref, kernel_ref, first_ref, second_ref, patch_ref, moved_ref):
    count, _, n, _ = patch_ref.shape
    base = pl.program_id(0) * count
    fronts = []
    for p in range(count):
        o_re, o_im = cut(own_ref, rim_ref, n, corner_ref[base + p, 0], corner_ref[base + p, 1])
        patch_ref[p, 0] = o_re.astype(jnp.bfloat16)
        patch_ref[p, 1] = o_im.astype(jnp.bfloat16)
        q_re, q_im = probe_ref[0], probe_ref[1]
        fronts.append((q_re * o_re - q_im * o_im, q_re * o_im + q_im * o_re))
    freq = transform(fronts, first_ref[...], second_ref[...])
    k_re, k_im = kernel_ref[0], kernel_ref[1]
    spread = [(k_re * r - k_im * i, k_re * i + k_im * r) for r, i in freq]
    moved = transform(spread, second_ref[...], first_ref[...])
    for p in range(count):
        moved_ref[p, 0] = moved[p][0]
        moved_ref[p, 1] = moved[p][1]


def second_kernel(
    corner_ref, own_ref, rim_ref, probe_ref, kernel_ref, first_ref, second_ref, patch_ref, moved_ref, *rest
):
    measured_refs = rest[:-3]
    grad_ref, probe_grad_ref, measured_ref = rest[-3:]
    count, _, n, _ = patch_ref.shape
    base = pl.program_id(0) * count

    @pl.when(pl.program_id(0) == 0)
    def _():
        for s, ref in enumerate(measured_refs):
            measured_ref[s] = ref[...]
        probe_grad_ref[...] = jnp.zeros_like(probe_grad_ref)

    seconds, slabs = [], []
    for p in range(count):
        o_re, o_im = cut(own_ref, rim_ref, n, corner_ref[base + p, 0], corner_ref[base + p, 1])
        m_re, m_im = moved_ref[p, 0], moved_ref[p, 1]
        slabs.append((o_re, o_im))
        seconds.append((m_re * o_re - m_im * o_im, m_re * o_im + m_im * o_re))
    far = transform(seconds, first_ref[...], second_ref[...])
    weighted = []
    for p, (f_re, f_im) in enumerate(far):
        measured = measured_ref[base + p].astype(jnp.float32)
        misfit = jnp.where(measured < 0.0, 0.0, f_re * f_re + f_im * f_im - measured)
        weighted.append((misfit * f_re, misfit * f_im))
    back_one = transform(weighted, second_ref[...], first_ref[...])
    carry = []
    for p, (b_re, b_im) in enumerate(back_one):
        m_re, m_im = moved_ref[p, 0], moved_ref[p, 1]
        o_re, o_im = slabs[p]
        grad_ref[p, 2] = (m_re * b_re + m_im * b_im).astype(jnp.bfloat16)
        grad_ref[p, 3] = (m_re * b_im - m_im * b_re).astype(jnp.bfloat16)
        carry.append((o_re * b_re + o_im * b_im, o_re * b_im - o_im * b_re))
    echo = transform(carry, first_ref[...], second_ref[...])
    k_re, k_im = kernel_ref[0], kernel_ref[1]
    undo = [(k_re * r + k_im * i, k_re * i - k_im * r) for r, i in echo]
    back_zero = transform(undo, second_ref[...], first_ref[...])
    total_re, total_im = probe_grad_ref[0], probe_grad_ref[1]
    q_re, q_im = probe_ref[0], probe_ref[1]
    for p, (b_re, b_im) in enumerate(back_zero):
        grad_ref[p, 0] = (q_re * b_re + q_im * b_im).astype(jnp.bfloat16)
        grad_ref[p, 1] = (q_re * b_im - q_im * b_re).astype(jnp.bfloat16)
        o_re = patch_ref[p, 0].astype(jnp.float32)
        o_im = patch_ref[p, 1].astype(jnp.float32)
        total_re += o_re * b_re + o_im * b_im
        total_im += o_re * b_im - o_im * b_re
    probe_grad_ref[0] = total_re
    probe_grad_ref[1] = total_im


def place_kernel(corner_ref, grad_ref, slab_ref, part_ref, rim_ref):
    positions, _, n, _ = grad_ref.shape
    height, width = slab_ref.shape[1:]
    wide = []
    for p in range(positions):
        move = one_hot_rows((n, width), corner_ref[p, 1])
        wide.append(product(grad_ref[p, 0], move).astype(jnp.bfloat16))
    wide = jnp.concatenate(wide, 0)
    tall = jnp.concatenate(
        [one_hot_columns((height + n, n), corner_ref[p, 0]) for p in range(positions)], 1
    )
    total = product(tall, wide)
    part_ref[0] = slab_ref[0] - step_object * total[:height]
    rim_ref[0] = total[height:].astype(jnp.bfloat16)


def whole(shape):
    return pl.BlockSpec(shape, lambda *_: (0,) * len(shape))


def per_position(shape):
    return pl.BlockSpec(shape, lambda i, *_: (i,) + (0,) * (len(shape) - 1))


def sum_everywhere(value):
    rows, n = value.shape
    row_count, col_count = lax.axis_size("row"), lax.axis_size("col")
    me = lax.axis_index("row")
    core, chip = me % 2, me // 2
    chips = row_count // 2
    half = rows // 2
    piece = half // chips
    send = lax.dynamic_slice_in_dim(value, (1 - core) * half, half, 0).astype(jnp.bfloat16)
    keep = lax.dynamic_slice_in_dim(value, core * half, half, 0)
    keep = keep + permute_pairs(send, "row", lambda i: i ^ 1).astype(jnp.float32)
    total = lax.dynamic_slice_in_dim(keep, chip * piece, piece, 0)
    for s in range(1, chips):
        send = lax.dynamic_slice_in_dim(keep, (chip ^ s) * piece, piece, 0).astype(jnp.bfloat16)
        total = total + permute_pairs(send, "row", lambda i: i ^ (2 * s)).astype(jnp.float32)
    send = total.astype(jnp.bfloat16)
    for s in range(1, col_count):
        total = total + permute_pairs(send, "col", lambda i: i ^ s).astype(jnp.float32)
    total = total.astype(jnp.bfloat16)
    gathered = jnp.zeros((half, n), jnp.bfloat16)
    gathered = lax.dynamic_update_slice_in_dim(gathered, total, chip * piece, 0)
    for s in range(1, chips):
        other = permute_pairs(total, "row", lambda i: i ^ (2 * s))
        gathered = lax.dynamic_update_slice_in_dim(gathered, other, (chip ^ s) * piece, 0)
    other = permute_pairs(gathered, "row", lambda i: i ^ 1)
    low = jnp.where(core == 0, gathered, other)
    high = jnp.where(core == 0, other, gathered)
    return jnp.concatenate([low, high], 0).astype(jnp.float32)


def per_device(object_slab, probe_field, prop_phase, intensities, corners, slot_source):
    slice_count, pair_count, height, width = object_slab.shape
    n = probe_field.shape[-1]
    row_count = lax.axis_size("row")
    col_count = lax.axis_size("col")
    slot_count = intensities.shape[0]
    me = lax.axis_index("row")
    first, second = dft_tables(n)
    kernel = jnp.stack([jnp.cos(prop_phase), jnp.sin(prop_phase)], 0)

    own = [object_slab[s].astype(jnp.bfloat16) for s in range(slice_count)]
    rim = [from_behind(block[:, :n], "row", -1) for block in own]

    sources = slot_source[:, 0]

    def message(target):
        hit = sources == target
        chosen = lax.dynamic_index_in_dim(intensities, jnp.argmax(hit), 0, keepdims=False)
        return jnp.where(jnp.any(hit), chosen, -1.0).astype(jnp.bfloat16)

    measured = [message(me)]
    origins = [me]
    for s in range(1, row_count):
        measured.append(permute_pairs(message(me ^ s), "row", lambda i: i ^ s))
        origins.append(me ^ s)
    spots = jnp.take(corners[:, 0], jnp.stack(origins), axis=0)

    count = 2
    steps = row_count // count
    plane = (2, n, n)
    patch_block = per_position((count, 2, n, n))
    table_specs = [whole((2 * n, 2 * n))] * 2
    tile_specs = [whole((pair_count, height, width)), whole((pair_count, n, width))]
    params = pltpu.CompilerParams(vmem_limit_bytes=VMEM_BYTES)
    unit = 2 * n * n * n
    patches, moved = pl.pallas_call(
        first_kernel,
        grid_spec=pltpu.PrefetchScalarGridSpec(
            num_scalar_prefetch=1,
            grid=(steps,),
            in_specs=tile_specs + [whole(plane)] * 2 + table_specs,
            out_specs=[patch_block, patch_block],
        ),
        out_shape=[
            jax.ShapeDtypeStruct((row_count, 2, n, n), jnp.bfloat16),
            jax.ShapeDtypeStruct((row_count, 2, n, n), jnp.float32),
        ],
        compiler_params=params,
        cost_estimate=pl.CostEstimate(flops=row_count * 28 * unit, bytes_accessed=6 * 2**20, transcendentals=0),
        name="first_half",
    )(spots, own[0], rim[0], probe_field, kernel, first, second)
    grads, probe_grad = pl.pallas_call(
        second_kernel,
        grid_spec=pltpu.PrefetchScalarGridSpec(
            num_scalar_prefetch=1,
            grid=(steps,),
            in_specs=tile_specs
            + [whole(plane)] * 2
            + table_specs
            + [patch_block, patch_block]
            + [whole((n, n))] * row_count,
            out_specs=[per_position((count, 4, n, n)), whole(plane)],
            scratch_shapes=[pltpu.VMEM((row_count, n, n), jnp.bfloat16)],
        ),
        out_shape=[
            jax.ShapeDtypeStruct((row_count, 4, n, n), jnp.bfloat16),
            jax.ShapeDtypeStruct(plane, jnp.float32),
        ],
        compiler_params=params,
        cost_estimate=pl.CostEstimate(flops=row_count * 44 * unit, bytes_accessed=8 * 2**20, transcendentals=0),
        name="second_half",
    )(spots, own[1], rim[1], probe_field, kernel, first, second, patches, moved, *measured)

    planes = slice_count * pair_count
    part, rim_grad = pl.pallas_call(
        place_kernel,
        grid_spec=pltpu.PrefetchScalarGridSpec(
            num_scalar_prefetch=1,
            grid=(planes,),
            in_specs=[
                pl.BlockSpec((row_count, 1, n, n), lambda i, *_: (0, i, 0, 0)),
                per_position((1, height, width)),
            ],
            out_specs=[per_position((1, height, width)), per_position((1, n, width))],
        ),
        out_shape=[
            jax.ShapeDtypeStruct((planes, height, width), jnp.float32),
            jax.ShapeDtypeStruct((planes, n, width), jnp.bfloat16),
        ],
        compiler_params=params,
        cost_estimate=pl.CostEstimate(flops=row_count * 24 * unit, bytes_accessed=7 * 2**20, transcendentals=0),
        name="place",
    )(spots, grads, object_slab.reshape(planes, height, width))
    total_probe = sum_everywhere(probe_grad.reshape(2 * n, n)).reshape(probe_field.shape)
    rim_grad = from_behind(rim_grad, "row", 1).astype(jnp.float32)
    updated_slab = part.at[:, :n].add(-step_object * rim_grad).reshape(object_slab.shape)
    updated_probe = probe_field - step_probe * total_probe / (row_count * col_count * slot_count)
    return (updated_slab, updated_probe)


def solution(mesh):
    placed = (
        P(None, None, ("groups", "row"), "col"),
        P("groups", None, None),
        P(),
        P(("groups", "row"), "col", None),
        P(("groups", "row"), "col", None),
        P(("groups", "row"), "col"),
    )
    return jax.shard_map(
        per_device,
        mesh=mesh,
        in_specs=placed,
        out_specs=(P(None, None, ("groups", "row"), "col"), P("groups", None, None)),
        check_vma=False,
    )
```

```python
import functools

import jax
import jax.numpy as jnp
from jax import lax
from jax.experimental import pallas as pl
from jax.experimental.pallas import tpu as pltpu
from jax.sharding import PartitionSpec as P

step_object = 0.05
step_probe = 0.5
VMEM_BYTES = 48 * 1024 * 1024


def permute_pairs(block, axis, partner):
    return lax.ppermute(block, axis, [(i, partner(i)) for i in range(lax.axis_size(axis))])


def from_behind(block, axis, distance):
    devices = range(lax.axis_size(axis))
    route = [(i - distance, i) for i in devices if i - distance in devices]
    return lax.ppermute(block, axis, route)


def dft_tables(length):
    index = jnp.arange(length, dtype=jnp.int32)
    phase_index = index[:, None] * index[None, :] % length
    angles = phase_index.astype(jnp.float32) * (2.0 * jnp.pi / length)
    scale_factor = 1.0 / jnp.sqrt(jnp.float32(length))
    table_re = (jnp.cos(angles) * scale_factor).astype(jnp.bfloat16)
    table_im = (-jnp.sin(angles) * scale_factor).astype(jnp.bfloat16)
    first = jnp.concatenate(
        [jnp.concatenate([table_re, -table_im], 1), jnp.concatenate([table_im, table_re], 1)], 0
    )
    second = jnp.concatenate(
        [jnp.concatenate([table_re, table_im], 1), jnp.concatenate([-table_im, table_re], 1)], 0
    )
    return first, second


def product(a, b):
    return jnp.dot(a, b, preferred_element_type=jnp.float32)


def transform(fields, left_table, right_table):
    count = len(fields)
    n = fields[0][0].shape[0]
    stacked = jnp.concatenate(
        [
            jnp.concatenate([f[0].astype(jnp.bfloat16) for f in fields], 1),
            jnp.concatenate([f[1].astype(jnp.bfloat16) for f in fields], 1),
        ],
        0,
    )
    middle = product(left_table, stacked).astype(jnp.bfloat16)
    middle = jnp.concatenate(
        [
            jnp.concatenate([middle[:n, p * n : (p + 1) * n], middle[n:, p * n : (p + 1) * n]], 1)
            for p in range(count)
        ],
        0,
    )
    out = product(middle, right_table)
    return [(out[p * n : (p + 1) * n, :n], out[p * n : (p + 1) * n, n:]) for p in range(count)]


def one_hot_rows(shape, offset):
    rows = lax.broadcasted_iota(jnp.int32, shape, 0)
    columns = lax.broadcasted_iota(jnp.int32, shape, 1)
    return (columns == rows + offset).astype(jnp.bfloat16)


def one_hot_columns(shape, offset):
    rows = lax.broadcasted_iota(jnp.int32, shape, 0)
    columns = lax.broadcasted_iota(jnp.int32, shape, 1)
    return (rows == columns + offset).astype(jnp.bfloat16)


def cut(own_ref, rim_ref, n, corner_y, corner_x):
    height = own_ref.shape[1] + rim_ref.shape[1]
    width = own_ref.shape[2]
    planes = jnp.concatenate(
        [jnp.concatenate([own_ref[c], rim_ref[c]], 0) for c in range(2)], 1
    )
    rows = product(one_hot_rows((n, height), corner_y), planes).astype(jnp.bfloat16)
    rows = jnp.concatenate([rows[:, :width], rows[:, width:]], 0)
    both = product(rows, one_hot_columns((width, n), corner_x))
    return both[:n], both[n:]


def spot(me_ref, corner_ref, position):
    owner = me_ref[0] ^ position
    return corner_ref[owner, 0], corner_ref[owner, 1]


def first_prep_kernel(slab_ref, own_ref):
    own_ref[...] = slab_ref[...].astype(jnp.bfloat16)


def second_prep_kernel(me_ref, source_ref, slab_ref, intensity_ref, own_ref, *message_refs):
    own_ref[...] = slab_ref[...].astype(jnp.bfloat16)
    for s, message_ref in enumerate(message_refs):
        target = me_ref[0] ^ s
        slot = jnp.int32(-1)
        for k in range(intensity_ref.shape[0]):
            slot = jnp.where(source_ref[k] == target, k, slot)
        chosen = intensity_ref[jnp.maximum(slot, 0)]
        message_ref[...] = jnp.where(slot >= 0, chosen, -1.0).astype(jnp.bfloat16)


def first_kernel(me_ref, corner_ref, own_ref, rim_ref, probe_ref, kernel_ref, first_ref, second_ref, patch_ref, moved_ref):
    count, _, n, _ = patch_ref.shape
    base = pl.program_id(0) * count
    fronts = []
    for p in range(count):
        o_re, o_im = cut(own_ref, rim_ref, n, *spot(me_ref, corner_ref, base + p))
        patch_ref[p, 0] = o_re.astype(jnp.bfloat16)
        patch_ref[p, 1] = o_im.astype(jnp.bfloat16)
        q_re, q_im = probe_ref[0], probe_ref[1]
        fronts.append((q_re * o_re - q_im * o_im, q_re * o_im + q_im * o_re))
    freq = transform(fronts, first_ref[...], second_ref[...])
    k_re, k_im = kernel_ref[0], kernel_ref[1]
    spread = [(k_re * r - k_im * i, k_re * i + k_im * r) for r, i in freq]
    moved = transform(spread, second_ref[...], first_ref[...])
    for p in range(count):
        moved_ref[p, 0] = moved[p][0]
        moved_ref[p, 1] = moved[p][1]


def second_kernel(
    me_ref, corner_ref, own_ref, rim_ref, probe_ref, kernel_ref, first_ref, second_ref, patch_ref, moved_ref, *rest
):
    measured_refs = rest[:-3]
    grad_ref, probe_grad_ref, measured_ref = rest[-3:]
    count, _, n, _ = patch_ref.shape
    base = pl.program_id(0) * count

    @pl.when(pl.program_id(0) == 0)
    def _():
        for s, ref in enumerate(measured_refs):
            measured_ref[s] = ref[...]
        probe_grad_ref[...] = jnp.zeros_like(probe_grad_ref)

    seconds, slabs = [], []
    for p in range(count):
        o_re, o_im = cut(own_ref, rim_ref, n, *spot(me_ref, corner_ref, base + p))
        m_re, m_im = moved_ref[p, 0], moved_ref[p, 1]
        slabs.append((o_re, o_im))
        seconds.append((m_re * o_re - m_im * o_im, m_re * o_im + m_im * o_re))
    far = transform(seconds, first_ref[...], second_ref[...])
    weighted = []
    for p, (f_re, f_im) in enumerate(far):
        measured = measured_ref[base + p].astype(jnp.float32)
        misfit = jnp.where(measured < 0.0, 0.0, f_re * f_re + f_im * f_im - measured)
        weighted.append((misfit * f_re, misfit * f_im))
    back_one = transform(weighted, second_ref[...], first_ref[...])
    carry = []
    for p, (b_re, b_im) in enumerate(back_one):
        m_re, m_im = moved_ref[p, 0], moved_ref[p, 1]
        o_re, o_im = slabs[p]
        grad_ref[p, 2] = (m_re * b_re + m_im * b_im).astype(jnp.bfloat16)
        grad_ref[p, 3] = (m_re * b_im - m_im * b_re).astype(jnp.bfloat16)
        carry.append((o_re * b_re + o_im * b_im, o_re * b_im - o_im * b_re))
    echo = transform(carry, first_ref[...], second_ref[...])
    k_re, k_im = kernel_ref[0], kernel_ref[1]
    undo = [(k_re * r + k_im * i, k_re * i - k_im * r) for r, i in echo]
    back_zero = transform(undo, second_ref[...], first_ref[...])
    total_re, total_im = probe_grad_ref[0], probe_grad_ref[1]
    q_re, q_im = probe_ref[0], probe_ref[1]
    for p, (b_re, b_im) in enumerate(back_zero):
        grad_ref[p, 0] = (q_re * b_re + q_im * b_im).astype(jnp.bfloat16)
        grad_ref[p, 1] = (q_re * b_im - q_im * b_re).astype(jnp.bfloat16)
        o_re = patch_ref[p, 0].astype(jnp.float32)
        o_im = patch_ref[p, 1].astype(jnp.float32)
        total_re += o_re * b_re + o_im * b_im
        total_im += o_re * b_im - o_im * b_re
    probe_grad_ref[0] = total_re
    probe_grad_ref[1] = total_im


def placed_rows(me_ref, corner_ref, grad_ref, width, rows, first_row):
    positions, _, n, _ = grad_ref.shape
    wide, tall = [], []
    for p in range(positions):
        corner_y, corner_x = spot(me_ref, corner_ref, p)
        move = one_hot_rows((n, width), corner_x)
        wide.append(product(grad_ref[p, 0], move).astype(jnp.bfloat16))
        tall.append(one_hot_columns((rows, n), corner_y - first_row))
    return product(jnp.concatenate(tall, 1), jnp.concatenate(wide, 0))


def place_rim_kernel(me_ref, corner_ref, grad_ref, rim_ref, *, height):
    rows, width = rim_ref.shape[1:]
    rim_ref[0] = placed_rows(me_ref, corner_ref, grad_ref, width, rows, height).astype(jnp.bfloat16)


def place_own_kernel(me_ref, corner_ref, grad_ref, slab_ref, part_ref):
    rows, width = part_ref.shape[1:]
    part_ref[0] = slab_ref[0] - step_object * placed_rows(me_ref, corner_ref, grad_ref, width, rows, 0)


def whole(shape):
    return pl.BlockSpec(shape, lambda *_: (0,) * len(shape))


def per_position(shape):
    return pl.BlockSpec(shape, lambda i, *_: (i,) + (0,) * (len(shape) - 1))


def sum_everywhere(value):
    rows, n = value.shape
    row_count, col_count = lax.axis_size("row"), lax.axis_size("col")
    me = lax.axis_index("row")
    core, chip = me % 2, me // 2
    chips = row_count // 2
    half = rows // 2
    piece = half // chips
    send = lax.dynamic_slice_in_dim(value, (1 - core) * half, half, 0).astype(jnp.bfloat16)
    keep = lax.dynamic_slice_in_dim(value, core * half, half, 0)
    keep = keep + permute_pairs(send, "row", lambda i: i ^ 1).astype(jnp.float32)
    total = lax.dynamic_slice_in_dim(keep, chip * piece, piece, 0)
    for s in range(1, chips):
        send = lax.dynamic_slice_in_dim(keep, (chip ^ s) * piece, piece, 0).astype(jnp.bfloat16)
        total = total + permute_pairs(send, "row", lambda i: i ^ (2 * s)).astype(jnp.float32)
    send = total.astype(jnp.bfloat16)
    for s in range(1, col_count):
        total = total + permute_pairs(send, "col", lambda i: i ^ s).astype(jnp.float32)
    total = total.astype(jnp.bfloat16)
    gathered = jnp.zeros((half, n), jnp.bfloat16)
    gathered = lax.dynamic_update_slice_in_dim(gathered, total, chip * piece, 0)
    for s in range(1, chips):
        other = permute_pairs(total, "row", lambda i: i ^ (2 * s))
        gathered = lax.dynamic_update_slice_in_dim(gathered, other, (chip ^ s) * piece, 0)
    other = permute_pairs(gathered, "row", lambda i: i ^ 1)
    low = jnp.where(core == 0, gathered, other)
    high = jnp.where(core == 0, other, gathered)
    return jnp.concatenate([low, high], 0).astype(jnp.float32)


def per_device(object_slab, probe_field, prop_phase, intensities, corners, slot_source):
    slice_count, pair_count, height, width = object_slab.shape
    n = probe_field.shape[-1]
    row_count = lax.axis_size("row")
    col_count = lax.axis_size("col")
    slot_count = intensities.shape[0]
    me = lax.axis_index("row")
    first, second = dft_tables(n)
    kernel = jnp.stack([jnp.cos(prop_phase), jnp.sin(prop_phase)], 0)

    planes = slice_count * pair_count
    slab = object_slab.reshape(planes, height, width)
    params = pltpu.CompilerParams(vmem_limit_bytes=VMEM_BYTES)
    me_array = jnp.reshape(me, (1,)).astype(jnp.int32)
    spots = corners.reshape(row_count, 2)
    sources = slot_source.reshape(slot_count)
    smem = pl.BlockSpec(memory_space=pltpu.SMEM)
    tile = (pair_count, height, width)
    own_zero = pl.pallas_call(
        first_prep_kernel,
        grid=(pair_count,),
        in_specs=[pl.BlockSpec((1, height, width), lambda i: (i, 0, 0))],
        out_specs=pl.BlockSpec((1, height, width), lambda i: (i, 0, 0)),
        out_shape=jax.ShapeDtypeStruct(tile, jnp.bfloat16),
        compiler_params=params,
        name="prepare_zero",
    )(slab)
    rim_zero = from_behind(own_zero[:, :n], "row", -1)
    own_one, *messages = pl.pallas_call(
        second_prep_kernel,
        grid=(1,),
        in_specs=[
            smem,
            smem,
            pl.BlockSpec(tile, lambda i: (1, 0, 0)),
            pl.BlockSpec(intensities.shape, lambda i: (0, 0, 0)),
        ],
        out_specs=[pl.BlockSpec(tile, lambda i: (0, 0, 0))]
        + [pl.BlockSpec((n, n), lambda i: (0, 0))] * row_count,
        out_shape=[jax.ShapeDtypeStruct(tile, jnp.bfloat16)]
        + [jax.ShapeDtypeStruct((n, n), jnp.bfloat16)] * row_count,
        compiler_params=params,
        name="prepare_one",
    )(me_array, sources, slab, intensities)
    rim_one = from_behind(own_one[:, :n], "row", -1)
    own, rim = [own_zero, own_one], [rim_zero, rim_one]
    measured = [messages[0]]
    for s in range(1, row_count):
        measured.append(permute_pairs(messages[s], "row", lambda i: i ^ s))

    count = 2
    steps = row_count // count
    plane = (2, n, n)
    patch_block = per_position((count, 2, n, n))
    table_specs = [whole((2 * n, 2 * n))] * 2
    tile_specs = [whole((pair_count, height, width)), whole((pair_count, n, width))]
    unit = 2 * n * n * n
    patches, moved = pl.pallas_call(
        first_kernel,
        grid_spec=pltpu.PrefetchScalarGridSpec(
            num_scalar_prefetch=2,
            grid=(steps,),
            in_specs=tile_specs + [whole(plane)] * 2 + table_specs,
            out_specs=[patch_block, patch_block],
        ),
        out_shape=[
            jax.ShapeDtypeStruct((row_count, 2, n, n), jnp.bfloat16),
            jax.ShapeDtypeStruct((row_count, 2, n, n), jnp.float32),
        ],
        compiler_params=params,
        cost_estimate=pl.CostEstimate(flops=row_count * 28 * unit, bytes_accessed=6 * 2**20, transcendentals=0),
        name="first_half",
    )(me_array, spots, own[0], rim[0], probe_field, kernel, first, second)
    grads, probe_grad = pl.pallas_call(
        second_kernel,
        grid_spec=pltpu.PrefetchScalarGridSpec(
            num_scalar_prefetch=2,
            grid=(steps,),
            in_specs=tile_specs
            + [whole(plane)] * 2
            + table_specs
            + [patch_block, patch_block]
            + [whole((n, n))] * row_count,
            out_specs=[per_position((count, 4, n, n)), whole(plane)],
            scratch_shapes=[pltpu.VMEM((row_count, n, n), jnp.bfloat16)],
        ),
        out_shape=[
            jax.ShapeDtypeStruct((row_count, 4, n, n), jnp.bfloat16),
            jax.ShapeDtypeStruct(plane, jnp.float32),
        ],
        compiler_params=params,
        cost_estimate=pl.CostEstimate(flops=row_count * 44 * unit, bytes_accessed=8 * 2**20, transcendentals=0),
        name="second_half",
    )(me_array, spots, own[1], rim[1], probe_field, kernel, first, second, patches, moved, *measured)

    def place(body, block_rows, out_type, arrays, name):
        extra = [per_position((1, height, width))] * len(arrays)
        return pl.pallas_call(
            body,
            grid_spec=pltpu.PrefetchScalarGridSpec(
                num_scalar_prefetch=2,
                grid=(planes,),
                in_specs=[pl.BlockSpec((row_count, 1, n, n), lambda i, *_: (0, i, 0, 0))] + extra,
                out_specs=per_position((1, block_rows, width)),
            ),
            out_shape=jax.ShapeDtypeStruct((planes, block_rows, width), out_type),
            compiler_params=params,
            cost_estimate=pl.CostEstimate(flops=row_count * 16 * unit, bytes_accessed=4 * 2**20, transcendentals=0),
            name=name,
        )(me_array, spots, grads, *arrays)

    rim_grad = place(functools.partial(place_rim_kernel, height=height), n, jnp.bfloat16, [], "place_rim")
    part = place(place_own_kernel, height, jnp.float32, [slab], "place_own")
    total_probe = sum_everywhere(probe_grad.reshape(2 * n, n)).reshape(probe_field.shape)
    rim_grad = from_behind(rim_grad, "row", 1).astype(jnp.float32)
    updated_slab = part.at[:, :n].add(-step_object * rim_grad).reshape(object_slab.shape)
    updated_probe = probe_field - step_probe * total_probe / (row_count * col_count * slot_count)
    return (updated_slab, updated_probe)


def solution(mesh):
    placed = (
        P(None, None, ("groups", "row"), "col"),
        P("groups", None, None),
        P(),
        P(("groups", "row"), "col", None),
        P(("groups", "row"), "col", None),
        P(("groups", "row"), "col"),
    )
    return jax.shard_map(
        per_device,
        mesh=mesh,
        in_specs=placed,
        out_specs=(P(None, None, ("groups", "row"), "col"), P("groups", None, None)),
        check_vma=False,
    )
```

```python
import functools

import jax
import jax.numpy as jnp
import ml_dtypes
import numpy as np
from jax import lax
from jax.experimental import pallas as pl
from jax.experimental.pallas import tpu as pltpu
from jax.sharding import PartitionSpec as P

step_object = 0.05
step_probe = 0.5
SMALL_FLOPS = 2000000000
SMALL_VMEM = 8 * 1024 * 1024
LARGE_VMEM = 24 * 1024 * 1024
POSITIONS_AT_ONCE = 4


def permute_pairs(block, axis, partner):
    return lax.ppermute(block, axis, [(i, partner(i)) for i in range(lax.axis_size(axis))])


def from_behind(block, axis, distance):
    devices = range(lax.axis_size(axis))
    route = [(i - distance, i) for i in devices if i - distance in devices]
    return lax.ppermute(block, axis, route)


def dft_table(length):
    index = np.arange(length)
    angles = (index[:, None] * index[None, :] % length) * (2.0 * np.pi / length)
    scale_factor = 1.0 / np.sqrt(length)
    table_re = (np.cos(angles) * scale_factor).astype(np.float32).astype(ml_dtypes.bfloat16)
    table_im = (-np.sin(angles) * scale_factor).astype(np.float32).astype(ml_dtypes.bfloat16)
    return jnp.asarray(np.block([[table_re, -table_im], [table_im, table_re]]))


def product(a, b):
    return jnp.dot(a, b, preferred_element_type=jnp.float32)


def transform(table_ref, field_ref, middle_ref, out_ref, positions):
    n = field_ref.shape[1] // 2
    for p in positions:
        middle = product(table_ref[...], field_ref[p])
        middle_ref[p, :, n:] = middle[:n].astype(jnp.bfloat16)
        middle_ref[p, :, :n] = middle[n:].astype(jnp.bfloat16)
        out_ref[p] = product(middle_ref[p], table_ref[...])


def chunks(n):
    size = min(32, n)
    return [slice(a, a + size) for a in range(0, n, size)]


def put_forward(field_ref, p, rows, re, im):
    n = field_ref.shape[1] // 2
    field_ref[p, rows] = re.astype(jnp.bfloat16)
    field_ref[p, slice(n + rows.start, n + rows.stop)] = im.astype(jnp.bfloat16)


def put_backward(field_ref, p, rows, re, im):
    put_forward(field_ref, p, rows, im, re)


def get_forward(out_ref, p, rows):
    n = out_ref.shape[1]
    return out_ref[p, rows, n:], out_ref[p, rows, :n]


def get_backward(out_ref, p, rows):
    n = out_ref.shape[1]
    return out_ref[p, rows, :n], out_ref[p, rows, n:]


def one_hot_rows(shape, offset):
    rows = lax.broadcasted_iota(jnp.int32, shape, 0)
    columns = lax.broadcasted_iota(jnp.int32, shape, 1)
    return (columns == rows + offset).astype(jnp.bfloat16)


def one_hot_columns(shape, offset):
    rows = lax.broadcasted_iota(jnp.int32, shape, 0)
    columns = lax.broadcasted_iota(jnp.int32, shape, 1)
    return (rows == columns + offset).astype(jnp.bfloat16)


def spot(corner_ref, position):
    return corner_ref[position, 0, :1, :1], corner_ref[position, 1, :1, :1]


def cut(own_ref, rim_ref, patch_ref, corner_ref, base, count):
    n = patch_ref.shape[2]
    height = own_ref.shape[1] + rim_ref.shape[1]
    width = own_ref.shape[2]
    planes = jnp.concatenate([jnp.concatenate([own_ref[c], rim_ref[c]], 0) for c in range(2)], 1)
    for p in range(count):
        corner_y, corner_x = spot(corner_ref, base + p)
        rows = product(one_hot_rows((n, height), corner_y), planes).astype(jnp.bfloat16)
        rows = jnp.concatenate([rows[:, :width], rows[:, width:]], 0)
        both = product(rows, one_hot_columns((width, n), corner_x)).astype(jnp.bfloat16)
        patch_ref[p, 0] = both[:n]
        patch_ref[p, 1] = both[n:]


def pair(ref, p, rows):
    return ref[p, 0, rows].astype(jnp.float32), ref[p, 1, rows].astype(jnp.float32)


def first_prep_kernel(slab_ref, own_ref, wide_ref, sems):
    planes = own_ref.shape[0]
    copies = [pltpu.make_async_copy(slab_ref.at[c], wide_ref.at[c], sems.at[c]) for c in range(planes)]
    for copy in copies:
        copy.start()
    for c, copy in enumerate(copies):
        copy.wait()
        own_ref[c] = wide_ref[c].astype(jnp.bfloat16)


def second_prep_kernel(source_ref, slab_hbm, intensity_ref, own_ref, *rest):
    message_refs, wide_ref, sem = rest[:-2], rest[-2], rest[-1]
    copy = pltpu.make_async_copy(slab_hbm.at[pl.ds(own_ref.shape[0], own_ref.shape[0])], wide_ref, sem)
    copy.start()
    for s, message_ref in enumerate(message_refs):
        target = lax.axis_index("row") ^ s
        slot = jnp.int32(-1)
        for k in range(intensity_ref.shape[0]):
            slot = jnp.where(source_ref[k] == target, k, slot)
        chosen = intensity_ref[jnp.maximum(slot, 0)]
        message_ref[...] = jnp.where(slot >= 0, chosen, -1.0).astype(jnp.bfloat16)
    copy.wait()
    own_ref[...] = wide_ref[...].astype(jnp.bfloat16)


def third_prep_kernel(corner_ref, phase_ref, table_hbm, table_ref, kernel_ref, spot_ref, sem):
    copy = pltpu.make_async_copy(table_hbm, table_ref, sem)
    copy.start()
    for p in range(spot_ref.shape[0]):
        owner = lax.axis_index("row") ^ p
        for k in range(2):
            spot_ref[p, k] = jnp.full(spot_ref.shape[2:], corner_ref[owner, k], jnp.int32)
    for rows in chunks(phase_ref.shape[0]):
        kernel_ref[0, rows] = jnp.cos(phase_ref[rows])
        kernel_ref[1, rows] = jnp.sin(phase_ref[rows])
    copy.wait()


def first_kernel(
    corner_ref, own_ref, rim_ref, probe_ref, kernel_ref, table_ref, patch_ref, moved_ref,
    field_ref, middle_ref, out_ref,
):
    count, _, n, _ = patch_ref.shape
    cut(own_ref, rim_ref, patch_ref, corner_ref, pl.program_id(0) * count, count)
    for p in range(count):
        for rows in chunks(n):
            q_re, q_im = probe_ref[0, rows], probe_ref[1, rows]
            o_re, o_im = pair(patch_ref, p, rows)
            put_forward(field_ref, p, rows, q_re * o_re - q_im * o_im, q_re * o_im + q_im * o_re)
    transform(table_ref, field_ref, middle_ref, out_ref, range(count))
    for p in range(count):
        for rows in chunks(n):
            k_re, k_im = kernel_ref[0, rows], kernel_ref[1, rows]
            r, i = get_forward(out_ref, p, rows)
            put_backward(field_ref, p, rows, k_re * r - k_im * i, k_re * i + k_im * r)
    transform(table_ref, field_ref, middle_ref, moved_ref, range(count))


def second_kernel(
    corner_ref, own_ref, rim_ref, moved_ref, table_ref, patch_ref, far_ref, field_ref, middle_ref
):
    count, _, n, _ = patch_ref.shape
    cut(own_ref, rim_ref, patch_ref, corner_ref, pl.program_id(0) * count, count)
    for p in range(count):
        for rows in chunks(n):
            m_re, m_im = get_backward(moved_ref, p, rows)
            o_re, o_im = pair(patch_ref, p, rows)
            put_forward(field_ref, p, rows, m_re * o_re - m_im * o_im, m_re * o_im + m_im * o_re)
    transform(table_ref, field_ref, middle_ref, far_ref, range(count))


def third_kernel(corner_ref, probe_ref, kernel_ref, table_ref, zero_ref, one_ref, moved_ref, far_ref, *rest):
    measured_refs = rest[:-9]
    grad_ref, rim_ref, keep_ref, send_ref, probe_grad_ref, measured_ref = rest[-9:-3]
    field_ref, middle_ref, out_ref = rest[-3:]
    count, _, n, _ = zero_ref.shape
    planes = grad_ref.shape[0]
    base = pl.program_id(0) * count
    last = pl.program_id(0) == pl.num_programs(0) - 1

    @pl.when(pl.program_id(0) == 0)
    def _():
        for s, ref in enumerate(measured_refs):
            measured_ref[s] = ref[...]
        probe_grad_ref[...] = jnp.zeros_like(probe_grad_ref)

    for p in range(count):
        for rows in chunks(n):
            f_re, f_im = get_forward(far_ref, p, rows)
            measured = measured_ref[base + p, rows].astype(jnp.float32)
            misfit = jnp.where(measured < 0.0, 0.0, f_re * f_re + f_im * f_im - measured)
            put_backward(field_ref, p, rows, misfit * f_re, misfit * f_im)
    transform(table_ref, field_ref, middle_ref, out_ref, range(count))
    for p in range(count):
        for rows in chunks(n):
            b_re, b_im = get_backward(out_ref, p, rows)
            m_re, m_im = get_backward(moved_ref, p, rows)
            o_re, o_im = pair(one_ref, p, rows)
            grad_ref[2, base + p, rows] = (m_re * b_re + m_im * b_im).astype(jnp.bfloat16)
            grad_ref[3, base + p, rows] = (m_re * b_im - m_im * b_re).astype(jnp.bfloat16)
            put_forward(field_ref, p, rows, o_re * b_re + o_im * b_im, o_re * b_im - o_im * b_re)
    transform(table_ref, field_ref, middle_ref, out_ref, range(count))
    for p in range(count):
        for rows in chunks(n):
            k_re, k_im = kernel_ref[0, rows], kernel_ref[1, rows]
            r, i = get_forward(out_ref, p, rows)
            put_backward(field_ref, p, rows, k_re * r + k_im * i, k_re * i - k_im * r)
    transform(table_ref, field_ref, middle_ref, out_ref, range(count))
    for rows in chunks(n):
        total_re, total_im = probe_grad_ref[0, rows], probe_grad_ref[1, rows]
        q_re, q_im = probe_ref[0, rows], probe_ref[1, rows]
        for p in range(count):
            b_re, b_im = get_backward(out_ref, p, rows)
            o_re, o_im = pair(zero_ref, p, rows)
            grad_ref[0, base + p, rows] = (q_re * b_re + q_im * b_im).astype(jnp.bfloat16)
            grad_ref[1, base + p, rows] = (q_re * b_im - q_im * b_re).astype(jnp.bfloat16)
            total_re += o_re * b_re + o_im * b_im
            total_im += o_re * b_im - o_im * b_re
        probe_grad_ref[0, rows] = total_re
        probe_grad_ref[1, rows] = total_im

    @pl.when(last)
    def _():
        core = lax.axis_index("row") % 2
        keep_ref[...] = probe_grad_ref[core]
        send_ref[...] = probe_grad_ref[1 - core].astype(jnp.bfloat16)
        rows, width = rim_ref.shape[1:]
        moves, tall = placements(corner_ref, grad_ref.shape[1], n, width, rows, rows)
        for plane in range(planes):
            rim_ref[plane] = placed(grad_ref, plane, moves, tall).astype(jnp.bfloat16)


def placements(corner_ref, positions, n, width, rows, first_row):
    moves, tall = [], []
    for p in range(positions):
        corner_y, corner_x = spot(corner_ref, p)
        moves.append(one_hot_rows((n, width), corner_x))
        tall.append(one_hot_columns((rows, n), corner_y - first_row))
    return moves, jnp.concatenate(tall, 1)


def placed(grad_ref, plane, moves, tall):
    wide = [product(grad_ref[plane, p], move).astype(jnp.bfloat16) for p, move in enumerate(moves)]
    return product(tall, jnp.concatenate(wide, 0))


def place_kernel(corner_ref, grad_ref, slab_ref, part_ref):
    rows, width = part_ref.shape[1:]
    moves, tall = placements(corner_ref, grad_ref.shape[1], grad_ref.shape[2], width, rows, 0)
    for plane in range(grad_ref.shape[0]):
        part_ref[plane] = slab_ref[plane] - step_object * placed(grad_ref, plane, moves, tall)


def in_hbm(array):
    return pltpu.with_memory_space_constraint(array, pltpu.HBM)


def finish_kernel(part_ref, rim_ref, out_ref):
    rows = rim_ref.shape[1]
    out_ref[:, :rows] = part_ref[:, :rows] - step_object * rim_ref[...].astype(jnp.float32)
    if rows < part_ref.shape[1]:
        out_ref[:, rows:] = part_ref[:, rows:]


def whole(shape):
    return pl.BlockSpec(shape, lambda *_: (0,) * len(shape))


def per_position(shape):
    return pl.BlockSpec(shape, lambda i, *_: (i,) + (0,) * (len(shape) - 1))


def half_sum_kernel(keep_ref, other_ref, mine_ref, *rest):
    send_refs, total_ref = rest[:-1], rest[-1]
    chip = lax.axis_index("row") // 2
    piece = mine_ref.shape[0]
    total_ref[...] = keep_ref[...] + other_ref[...].astype(jnp.float32)
    mine_ref[...] = total_ref[pl.ds(pl.multiple_of(chip * piece, piece), piece)]
    for s, send_ref in enumerate(send_refs, 1):
        rows = pl.ds(pl.multiple_of((chip ^ s) * piece, piece), piece)
        send_ref[...] = total_ref[rows].astype(jnp.bfloat16)


def row_sum_kernel(mine_ref, *rest):
    other_refs, total_ref, send_ref = rest[:-2], rest[-2], rest[-1]
    total = mine_ref[...]
    for other_ref in other_refs:
        total += other_ref[...].astype(jnp.float32)
    total_ref[...] = total
    send_ref[...] = total.astype(jnp.bfloat16)


def full_sum_kernel(mine_ref, *rest):
    other_refs, total_ref = rest[:-1], rest[-1]
    total = mine_ref[...]
    for other_ref in other_refs:
        total += other_ref[...].astype(jnp.float32)
    total_ref[...] = total.astype(jnp.bfloat16)


def gather_kernel(mine_ref, *rest):
    other_refs, half_ref = rest[:-1], rest[-1]
    chip = lax.axis_index("row") // 2
    piece = mine_ref.shape[0]
    for s, ref in enumerate((mine_ref,) + other_refs):
        half_ref[pl.ds(pl.multiple_of((chip ^ s) * piece, piece), piece)] = ref[...]


def probe_kernel(probe_ref, mine_ref, other_ref, out_ref, *, scale):
    core = lax.axis_index("row") % 2
    out_ref[core] = probe_ref[core] - scale * mine_ref[...].astype(jnp.float32)
    out_ref[1 - core] = probe_ref[1 - core] - scale * other_ref[...].astype(jnp.float32)


def small_call(body, arrays, out_shape, name, scratch=()):
    return pl.pallas_call(
        body,
        in_specs=[pl.BlockSpec(memory_space=pltpu.VMEM)] * len(arrays),
        out_specs=[pl.BlockSpec(memory_space=pltpu.VMEM)] * len(out_shape),
        out_shape=out_shape,
        scratch_shapes=scratch,
        compiler_params=pltpu.CompilerParams(vmem_limit_bytes=SMALL_VMEM),
        cost_estimate=pl.CostEstimate(flops=SMALL_FLOPS, bytes_accessed=2**18, transcendentals=0),
        name=name,
    )(*arrays)


def probe_sum(keep, send, part):
    n = keep.shape[0]
    row_count, col_count = lax.axis_size("row"), lax.axis_size("col")
    chips = row_count // 2
    shape = (n // chips, n)
    wide, narrow = jax.ShapeDtypeStruct(shape, jnp.float32), jax.ShapeDtypeStruct(shape, jnp.bfloat16)
    other = permute_pairs(send, "row", lambda i: i ^ 1)
    mine, *sends = small_call(
        half_sum_kernel, [keep, other], [wide] + [narrow] * (chips - 1), "half_sum", [pltpu.VMEM((n, n), jnp.float32)]
    )
    others = [permute_pairs(sends[s - 1], "row", lambda i: i ^ (2 * s)) for s in range(1, chips)]
    total, send = small_call(row_sum_kernel, [mine, *others], [wide, narrow], "row_sum")
    others = [permute_pairs(send, "col", lambda i: i ^ s) for s in range(col_count - 1, 0, -1)]
    others, part = lax.optimization_barrier((others, part))
    (total,) = small_call(full_sum_kernel, [total, *others], [narrow], "full_sum")
    others = [permute_pairs(total, "row", lambda i: i ^ (2 * s)) for s in range(1, chips)]
    half = jax.ShapeDtypeStruct((n, n), jnp.bfloat16)
    (mine,) = small_call(gather_kernel, [total, *others], [half], "gather_half")
    return mine, permute_pairs(mine, "row", lambda i: i ^ 1), part


def per_device(object_slab, probe_field, prop_phase, intensities, corners, slot_source):
    slice_count, pair_count, height, width = object_slab.shape
    n = probe_field.shape[-1]
    row_count = lax.axis_size("row")
    col_count = lax.axis_size("col")
    slot_count = intensities.shape[0]
    me = lax.axis_index("row")

    planes = slice_count * pair_count
    slab = object_slab.reshape(planes, height, width)
    sources = slot_source.reshape(slot_count)
    smem = pl.BlockSpec(memory_space=pltpu.SMEM)
    hbm = pl.BlockSpec(memory_space=pltpu.HBM)
    vmem = pl.BlockSpec(memory_space=pltpu.VMEM)
    small = row_count <= POSITIONS_AT_ONCE

    def kept(shape, kind):
        return pltpu.VMEM(shape, kind) if small else jax.ShapeDtypeStruct(shape, kind)

    def near(array):
        return pltpu.with_memory_space_constraint(array, pltpu.VMEM) if small else array

    tile = (pair_count, height, width)
    own_zero = pl.pallas_call(
        first_prep_kernel,
        in_specs=[hbm],
        out_specs=vmem,
        out_shape=kept(tile, jnp.bfloat16),
        scratch_shapes=[pltpu.VMEM(tile, jnp.float32), pltpu.SemaphoreType.DMA((pair_count,))],
        compiler_params=pltpu.CompilerParams(vmem_limit_bytes=SMALL_VMEM),
        name="prepare_zero",
    )(in_hbm(slab))
    rim_zero = from_behind(own_zero[:, :n], "row", -1)
    own_one, *messages = pl.pallas_call(
        second_prep_kernel,
        in_specs=[smem, hbm, vmem],
        out_specs=[vmem] * (1 + row_count),
        out_shape=[kept(tile, jnp.bfloat16)] + [kept((n, n), jnp.bfloat16)] * row_count,
        scratch_shapes=[pltpu.VMEM(tile, jnp.float32), pltpu.SemaphoreType.DMA],
        compiler_params=pltpu.CompilerParams(vmem_limit_bytes=SMALL_VMEM),
        name="prepare_one",
    )(sources, in_hbm(slab), intensities)
    table, kernel, spots = pl.pallas_call(
        third_prep_kernel,
        in_specs=[smem, vmem, hbm],
        out_specs=[vmem] * 3,
        out_shape=[
            kept((2 * n, 2 * n), jnp.bfloat16),
            kept((2, n, n), jnp.float32),
            kept((row_count, 2, 8, 128), jnp.int32),
        ],
        scratch_shapes=[pltpu.SemaphoreType.DMA],
        compiler_params=pltpu.CompilerParams(vmem_limit_bytes=SMALL_VMEM),
        name="prepare_two",
    )(corners.reshape(row_count, 2), prop_phase, in_hbm(dft_table(n)))
    rim_one = from_behind(own_one[:, :n], "row", -1)
    measured = [messages[0]]
    for s in range(1, row_count):
        measured.append(permute_pairs(messages[s], "row", lambda i: i ^ s))

    count = min(POSITIONS_AT_ONCE, row_count)
    plane = (2, n, n)
    positions = (row_count, 2, n, n)
    block = per_position((count, 2, n, n))
    own_block, rim_block, tables = whole(tile), whole((pair_count, n, width)), whole((2 * n, 2 * n))
    wide = (row_count, n, 2 * n)
    wide_block = per_position((count, n, 2 * n))
    work = [
        pltpu.VMEM((count, 2 * n, n), jnp.bfloat16),
        pltpu.VMEM((count, n, 2 * n), jnp.bfloat16),
        pltpu.VMEM((count, n, 2 * n), jnp.float32),
    ]
    unit = 2 * n * n * n

    def call(body, in_specs, out_specs, out_shape, units, name, scratch=(), steps=row_count // count):
        return pl.pallas_call(
            body,
            grid=(steps,),
            in_specs=[whole((row_count, 2, 8, 128))] + in_specs,
            out_specs=out_specs,
            scratch_shapes=scratch,
            out_shape=out_shape,
            compiler_params=pltpu.CompilerParams(vmem_limit_bytes=LARGE_VMEM),
            cost_estimate=pl.CostEstimate(
                flops=row_count * units * unit, bytes_accessed=2**21, transcendentals=0
            ),
            name=name,
        )

    patch_zero, moved = call(
        first_kernel,
        [own_block, rim_block, whole(plane), whole(plane), tables],
        [block, wide_block],
        [kept(positions, jnp.bfloat16), kept(wide, jnp.float32)],
        28,
        "moved",
        scratch=work,
    )(near(spots), near(own_zero), near(rim_zero), probe_field, near(kernel), near(table))
    patch_one, far = call(
        second_kernel,
        [own_block, rim_block, wide_block, tables],
        [block, wide_block],
        [kept(positions, jnp.bfloat16), kept(wide, jnp.float32)],
        20,
        "far",
        scratch=work[:2],
    )(near(spots), near(own_one), near(rim_one), near(moved), near(table))
    grad_shape = (planes, row_count, n, n)
    grads, rim_grad, keep, send = call(
        third_kernel,
        [whole(plane), whole(plane), tables, block, block, wide_block, wide_block] + [whole((n, n))] * row_count,
        [whole(grad_shape), whole((planes, n, width)), whole((n, n)), whole((n, n))],
        [
            kept(grad_shape, jnp.bfloat16),
            kept((planes, n, width), jnp.bfloat16),
            kept((n, n), jnp.float32),
            kept((n, n), jnp.bfloat16),
        ],
        40,
        "gradients",
        scratch=[pltpu.VMEM(plane, jnp.float32), pltpu.VMEM((row_count, n, n), jnp.bfloat16)] + work,
    )(
        near(spots), probe_field, near(kernel), near(table), near(patch_zero), near(patch_one), near(moved), near(far),
        *[near(array) for array in measured],
    )
    (part,) = call(
        place_kernel,
        [whole(grad_shape), whole((planes, height, width))],
        [whole((planes, height, width))],
        [kept((planes, height, width), jnp.float32)],
        16,
        "place",
        steps=1,
    )(near(spots), near(grads), slab)

    rim_grad = from_behind(rim_grad, "row", 1)
    mine, other, part = probe_sum(keep, send, part)
    updated_slab = pl.pallas_call(
        finish_kernel,
        grid=(planes,),
        in_specs=[
            pl.BlockSpec((1, height, width), lambda i: (i, 0, 0)),
            pl.BlockSpec((1, n, width), lambda i: (i, 0, 0)),
        ],
        out_specs=pl.BlockSpec((1, height, width), lambda i: (i, 0, 0)),
        out_shape=jax.ShapeDtypeStruct((planes, height, width), jnp.float32),
        compiler_params=pltpu.CompilerParams(vmem_limit_bytes=SMALL_VMEM),
        name="finish",
    )(near(part), near(rim_grad)).reshape(object_slab.shape)
    (updated_probe,) = small_call(
        functools.partial(probe_kernel, scale=step_probe / (row_count * col_count * slot_count)),
        [probe_field, mine, other],
        [jax.ShapeDtypeStruct(probe_field.shape, jnp.float32)],
        "update_probe",
    )
    return (updated_slab, updated_probe)


def solution(mesh):
    placed = (
        P(None, None, ("groups", "row"), "col"),
        P("groups", None, None),
        P(),
        P(("groups", "row"), "col", None),
        P(("groups", "row"), "col", None),
        P(("groups", "row"), "col"),
    )
    return jax.shard_map(
        per_device,
        mesh=mesh,
        in_specs=placed,
        out_specs=(P(None, None, ("groups", "row"), "col"), P("groups", None, None)),
        check_vma=False,
    )
```

```python
import functools

import jax
import jax.numpy as jnp
import ml_dtypes
import numpy as np
from jax import lax
from jax.experimental import pallas as pl
from jax.experimental.pallas import tpu as pltpu
from jax.sharding import PartitionSpec as P

step_object = 0.05
step_probe = 0.5
SMALL_FLOPS = 4000000000
LATE_FROM = 99
SMALL_VMEM = 8 * 1024 * 1024
LARGE_VMEM = 24 * 1024 * 1024
POSITIONS_AT_ONCE = 4


def permute_pairs(block, axis, partner):
    return lax.ppermute(block, axis, [(i, partner(i)) for i in range(lax.axis_size(axis))])


def around(block, axis, distance):
    size = lax.axis_size(axis)
    return lax.ppermute(block, axis, [(i, (i + distance) % size) for i in range(size)])


def dft_table(length):
    index = np.arange(length)
    angles = (index[:, None] * index[None, :] % length) * (2.0 * np.pi / length)
    scale_factor = 1.0 / np.sqrt(length)
    table_re = (np.cos(angles) * scale_factor).astype(np.float32).astype(ml_dtypes.bfloat16)
    table_im = (-np.sin(angles) * scale_factor).astype(np.float32).astype(ml_dtypes.bfloat16)
    return jnp.asarray(np.block([[table_re, -table_im], [table_im, table_re]]))


def product(a, b):
    return jnp.dot(a, b, preferred_element_type=jnp.float32)


def transform(table_ref, field_ref, middle_ref, out_ref, positions):
    n = field_ref.shape[1] // 2
    for p in positions:
        middle = product(table_ref[...], field_ref[p])
        middle_ref[p, :, n:] = middle[:n].astype(jnp.bfloat16)
        middle_ref[p, :, :n] = middle[n:].astype(jnp.bfloat16)
        out_ref[p] = product(middle_ref[p], table_ref[...])


def chunks(n, size=32):
    size = min(size, n)
    return [slice(a, a + size) for a in range(0, n, size)]


def put_forward(field_ref, p, rows, re, im):
    n = field_ref.shape[1] // 2
    field_ref[p, rows] = re.astype(jnp.bfloat16)
    field_ref[p, slice(n + rows.start, n + rows.stop)] = im.astype(jnp.bfloat16)


def put_backward(field_ref, p, rows, re, im):
    put_forward(field_ref, p, rows, im, re)


def get_forward(out_ref, p, rows):
    n = out_ref.shape[1]
    return out_ref[p, rows, n:], out_ref[p, rows, :n]


def get_backward(out_ref, p, rows):
    n = out_ref.shape[1]
    return out_ref[p, rows, :n], out_ref[p, rows, n:]


def one_hot_rows(shape, offset):
    rows = lax.broadcasted_iota(jnp.int32, shape, 0)
    columns = lax.broadcasted_iota(jnp.int32, shape, 1)
    return (columns == rows + offset).astype(jnp.bfloat16)


def one_hot_columns(shape, offset):
    rows = lax.broadcasted_iota(jnp.int32, shape, 0)
    columns = lax.broadcasted_iota(jnp.int32, shape, 1)
    return (rows == columns + offset).astype(jnp.bfloat16)


def spot(corner_ref, position):
    return corner_ref[position, 0, :1, :1], corner_ref[position, 1, :1, :1]


def cut(own_ref, rim_ref, patch_ref, spot_ref, tile_ref, place_ref, sem, base, count):
    n = patch_ref.shape[2]
    height, width = own_ref.shape[1:]
    copy = pltpu.make_async_copy(spot_ref, place_ref, sem)
    copy.start()
    ends = lax.axis_index("row") == lax.axis_size("row") - 1
    for c in range(2):
        tile_ref[c, : height // 8] = own_ref[c].astype(jnp.float32).reshape(height // 8, 8, width)
        rim = jnp.where(ends, 0.0, rim_ref[c].astype(jnp.float32))
        tile_ref[c, height // 8 :] = rim.reshape(-1, 8, width)
    copy.wait()
    within = lax.broadcasted_iota(jnp.int32, (n // 8, 8, width), 1)
    for p in range(count):
        corner_y, corner_x = place_ref[base + p, 0], place_ref[base + p, 1]
        group = corner_y // 8
        shift = corner_y - group * 8
        rows = []
        for c in range(2):
            turned = pltpu.roll(tile_ref[c, pl.ds(group, n // 8 + 1)], 8 - shift, 1)
            rows.append(jnp.where(within < 8 - shift, turned[:-1], turned[1:]).reshape(n, width))
        rows = jnp.concatenate(rows, 0).astype(jnp.bfloat16)
        both = product(rows, one_hot_columns((width, n), corner_x)).astype(jnp.bfloat16)
        patch_ref[p, 0] = both[:n]
        patch_ref[p, 1] = both[n:]


def pair(ref, p, rows):
    return ref[p, 0, rows].astype(jnp.float32), ref[p, 1, rows].astype(jnp.float32)


def own_kernel(slab_hbm, own_ref, wide_ref, sems):
    parts = [(c, rows) for c in range(own_ref.shape[0]) for rows in chunks(own_ref.shape[1], 64)]
    copies = [
        pltpu.make_async_copy(slab_hbm.at[c, rows], wide_ref.at[c, rows], sems.at[i])
        for i, (c, rows) in enumerate(parts)
    ]
    for copy in copies:
        copy.start()
    for (c, rows), copy in zip(parts, copies):
        copy.wait()
        own_ref[c, rows] = wide_ref[c, rows].astype(jnp.bfloat16)


def prepare_kernel(
    corner_ref, source_ref, phase_ref, table_hbm, slab_hbm, intensity_ref,
    own_ref, table_ref, kernel_ref, vector_ref, spot_ref, *rest,
):
    message_refs, wide_ref, sems = rest[:-2], rest[-2], rest[-1]
    planes = own_ref.shape[0]
    slab_copy = pltpu.make_async_copy(slab_hbm.at[pl.ds(planes, planes)], wide_ref, sems.at[0])
    slab_copy.start()
    copy = pltpu.make_async_copy(table_hbm, table_ref, sems.at[1])
    copy.start()
    for s, message_ref in enumerate(message_refs):
        target = lax.axis_index("row") ^ s
        slot = jnp.int32(-1)
        for k in range(intensity_ref.shape[0]):
            slot = jnp.where(source_ref[k] == target, k, slot)
        chosen = intensity_ref[jnp.maximum(slot, 0)]
        message_ref[...] = jnp.where(slot >= 0, chosen, -1.0).astype(jnp.bfloat16)
    lane = lax.broadcasted_iota(jnp.int32, (1, spot_ref.shape[1]), 1)
    for p in range(vector_ref.shape[0]):
        owner = lax.axis_index("row") ^ p
        for k in range(2):
            vector_ref[p, k] = jnp.full(vector_ref.shape[2:], corner_ref[owner, k], jnp.int32)
        spot_ref[p : p + 1] = jnp.where(lane == 0, corner_ref[owner, 0], corner_ref[owner, 1])
    for rows in chunks(phase_ref.shape[0]):
        kernel_ref[0, rows] = jnp.cos(phase_ref[rows])
        kernel_ref[1, rows] = jnp.sin(phase_ref[rows])
    slab_copy.wait()
    own_ref[...] = wide_ref[...].astype(jnp.bfloat16)
    copy.wait()


def first_kernel(
    spot_ref, own_ref, rim_ref, probe_ref, kernel_ref, table_ref, patch_ref, moved_ref,
    tile_ref, place_ref, sem, field_ref, middle_ref, out_ref,
):
    count, _, n, _ = patch_ref.shape
    base = pl.program_id(0) * count
    cut(own_ref, rim_ref, patch_ref, spot_ref, tile_ref, place_ref, sem, base, count)
    for p in range(count):
        for rows in chunks(n):
            q_re, q_im = probe_ref[0, rows], probe_ref[1, rows]
            o_re, o_im = pair(patch_ref, p, rows)
            put_forward(field_ref, p, rows, q_re * o_re - q_im * o_im, q_re * o_im + q_im * o_re)
    transform(table_ref, field_ref, middle_ref, out_ref, range(count))
    for p in range(count):
        for rows in chunks(n):
            k_re, k_im = kernel_ref[0, rows], kernel_ref[1, rows]
            r, i = get_forward(out_ref, p, rows)
            put_backward(field_ref, p, rows, k_re * r - k_im * i, k_re * i + k_im * r)
    transform(table_ref, field_ref, middle_ref, moved_ref, range(count))


def second_kernel(
    spot_ref, own_ref, rim_ref, moved_ref, table_ref, patch_ref, far_ref,
    tile_ref, place_ref, sem, field_ref, middle_ref,
):
    count, _, n, _ = patch_ref.shape
    base = pl.program_id(0) * count
    cut(own_ref, rim_ref, patch_ref, spot_ref, tile_ref, place_ref, sem, base, count)
    for p in range(count):
        for rows in chunks(n):
            m_re, m_im = get_backward(moved_ref, p, rows)
            o_re, o_im = pair(patch_ref, p, rows)
            put_forward(field_ref, p, rows, m_re * o_re - m_im * o_im, m_re * o_im + m_im * o_re)
    transform(table_ref, field_ref, middle_ref, far_ref, range(count))


def third_kernel(probe_ref, kernel_ref, table_ref, zero_ref, one_ref, moved_ref, far_ref, *rest, steps):
    measured_refs = rest[:-8]
    grad_ref, keep_ref, send_ref, probe_grad_ref, measured_ref = rest[-8:-3]
    field_ref, middle_ref, out_ref = rest[-3:]
    count, _, n, _ = zero_ref.shape
    base = pl.program_id(0) * count if steps > 1 else 0

    def start():
        for s, ref in enumerate(measured_refs):
            measured_ref[s] = ref[...]
        probe_grad_ref[...] = jnp.zeros_like(probe_grad_ref)

    if steps > 1:
        pl.when(pl.program_id(0) == 0)(start)

    for p in range(count):
        for rows in chunks(n):
            f_re, f_im = get_forward(far_ref, p, rows)
            measured = measured_ref[base + p, rows] if steps > 1 else measured_refs[p][rows]
            measured = measured.astype(jnp.float32)
            misfit = jnp.where(measured < 0.0, 0.0, f_re * f_re + f_im * f_im - measured)
            put_backward(field_ref, p, rows, misfit * f_re, misfit * f_im)
    transform(table_ref, field_ref, middle_ref, out_ref, range(count))
    for p in range(count):
        for rows in chunks(n):
            b_re, b_im = get_backward(out_ref, p, rows)
            m_re, m_im = get_backward(moved_ref, p, rows)
            o_re, o_im = pair(one_ref, p, rows)
            grad_ref[2, base + p, rows] = (m_re * b_re + m_im * b_im).astype(jnp.bfloat16)
            grad_ref[3, base + p, rows] = (m_re * b_im - m_im * b_re).astype(jnp.bfloat16)
            put_forward(field_ref, p, rows, o_re * b_re + o_im * b_im, o_re * b_im - o_im * b_re)
    transform(table_ref, field_ref, middle_ref, out_ref, range(count))
    for p in range(count):
        for rows in chunks(n):
            k_re, k_im = kernel_ref[0, rows], kernel_ref[1, rows]
            r, i = get_forward(out_ref, p, rows)
            put_backward(field_ref, p, rows, k_re * r + k_im * i, k_re * i - k_im * r)
    transform(table_ref, field_ref, middle_ref, out_ref, range(count))
    for rows in chunks(n):
        total_re, total_im = (probe_grad_ref[0, rows], probe_grad_ref[1, rows]) if steps > 1 else (0.0, 0.0)
        q_re, q_im = probe_ref[0, rows], probe_ref[1, rows]
        for p in range(count):
            b_re, b_im = get_backward(out_ref, p, rows)
            o_re, o_im = pair(zero_ref, p, rows)
            grad_ref[0, base + p, rows] = (q_re * b_re + q_im * b_im).astype(jnp.bfloat16)
            grad_ref[1, base + p, rows] = (q_re * b_im - q_im * b_re).astype(jnp.bfloat16)
            total_re += o_re * b_re + o_im * b_im
            total_im += o_re * b_im - o_im * b_re
        probe_grad_ref[0, rows] = total_re
        probe_grad_ref[1, rows] = total_im

    def end():
        core = lax.axis_index("row") % 2
        keep_ref[...] = probe_grad_ref[core]
        send_ref[...] = probe_grad_ref[1 - core].astype(jnp.bfloat16)

    if steps > 1:
        pl.when(pl.program_id(0) == steps - 1)(end)
    else:
        end()


def placed(corner_ref, grad_ref, tall_ref, rows, width, first_row):
    planes, positions, n, _ = grad_ref.shape
    moves = []
    for p in range(positions):
        corner_y, corner_x = spot(corner_ref, p)
        moves.append(one_hot_rows((n, width), corner_x))
        every = jnp.concatenate([grad_ref[plane, p] for plane in range(planes)], 1)
        tall = product(one_hot_columns((rows, n), corner_y - first_row), every).astype(jnp.bfloat16)
        for plane in range(planes):
            tall_ref[plane, :, p * n : (p + 1) * n] = tall[:, plane * n : (plane + 1) * n]
    moves = jnp.concatenate(moves, 0)
    for plane in range(planes):
        yield plane, product(tall_ref[plane], moves)


def place_rim_kernel(corner_ref, grad_ref, rim_ref, tall_ref, *, height):
    rows, width = rim_ref.shape[1:]
    for plane, total in placed(corner_ref, grad_ref, tall_ref, rows, width, height):
        rim_ref[plane] = total.astype(jnp.bfloat16)


def place_kernel(corner_ref, grad_ref, slab_ref, part_ref, tall_ref):
    rows, width = part_ref.shape[1:]
    for plane, total in placed(corner_ref, grad_ref, tall_ref, rows, width, 0):
        part_ref[plane] = slab_ref[plane] - step_object * total


def in_hbm(array):
    return pltpu.with_memory_space_constraint(array, pltpu.HBM)


def finish_kernel(part_ref, rim_ref, out_hbm, sums_ref, sems):
    parts = [(c, rows) for c in range(part_ref.shape[0]) for rows in chunks(part_ref.shape[1], 128)]
    copies = []
    step = jnp.where(lax.axis_index("row") == 0, 0.0, step_object)
    for i, (c, rows) in enumerate(parts):
        value = part_ref[c, rows]
        if rows.start < rim_ref.shape[1]:
            value -= step * rim_ref[c, rows].astype(jnp.float32)
        sums_ref[c, rows] = value
        copies.append(pltpu.make_async_copy(sums_ref.at[c, rows], out_hbm.at[c, rows], sems.at[i]))
        copies[-1].start()
    for copy in copies:
        copy.wait()


def whole(shape):
    return pl.BlockSpec(shape, lambda *_: (0,) * len(shape))


def per_position(shape):
    return pl.BlockSpec(shape, lambda i, *_: (i,) + (0,) * (len(shape) - 1))


def half_sum_kernel(keep_ref, other_ref, mine_ref, *rest):
    send_refs, total_ref = rest[:-1], rest[-1]
    chip = lax.axis_index("row") // 2
    piece = mine_ref.shape[0]
    total_ref[...] = keep_ref[...] + other_ref[...].astype(jnp.float32)
    mine_ref[...] = total_ref[pl.ds(pl.multiple_of(chip * piece, piece), piece)]
    for s, send_ref in enumerate(send_refs, 1):
        rows = pl.ds(pl.multiple_of((chip ^ s) * piece, piece), piece)
        send_ref[...] = total_ref[rows].astype(jnp.bfloat16)


def row_sum_kernel(mine_ref, *rest):
    other_refs, total_ref, send_ref = rest[:-2], rest[-2], rest[-1]
    total = mine_ref[...]
    for other_ref in other_refs:
        total += other_ref[...].astype(jnp.float32)
    total_ref[...] = total
    send_ref[...] = total.astype(jnp.bfloat16)


def full_sum_kernel(mine_ref, *rest):
    other_refs, total_ref = rest[:-1], rest[-1]
    total = mine_ref[...]
    for other_ref in other_refs:
        total += other_ref[...].astype(jnp.float32)
    total_ref[...] = total.astype(jnp.bfloat16)


def gather_kernel(mine_ref, *rest):
    other_refs, half_ref = rest[:-1], rest[-1]
    chip = lax.axis_index("row") // 2
    piece = mine_ref.shape[0]
    for s, ref in enumerate((mine_ref,) + other_refs):
        half_ref[pl.ds(pl.multiple_of((chip ^ s) * piece, piece), piece)] = ref[...]


def probe_kernel(probe_ref, mine_ref, other_ref, out_ref, *, scale):
    core = lax.axis_index("row") % 2
    out_ref[core] = probe_ref[core] - scale * mine_ref[...].astype(jnp.float32)
    out_ref[1 - core] = probe_ref[1 - core] - scale * other_ref[...].astype(jnp.float32)


def small_call(body, arrays, out_shape, name, scratch=()):
    return pl.pallas_call(
        body,
        in_specs=[pl.BlockSpec(memory_space=pltpu.VMEM)] * len(arrays),
        out_specs=[pl.BlockSpec(memory_space=pltpu.VMEM)] * len(out_shape),
        out_shape=out_shape,
        scratch_shapes=scratch,
        compiler_params=pltpu.CompilerParams(vmem_limit_bytes=SMALL_VMEM),
        cost_estimate=pl.CostEstimate(flops=SMALL_FLOPS, bytes_accessed=2**18, transcendentals=0),
        name=name,
    )(*arrays)


def probe_sum(keep, send, rim_grad, part):
    n = keep.shape[0]
    row_count, col_count = lax.axis_size("row"), lax.axis_size("col")
    chips = row_count // 2
    shape = (n // chips, n)
    wide, narrow = jax.ShapeDtypeStruct(shape, jnp.float32), jax.ShapeDtypeStruct(shape, jnp.bfloat16)
    other = permute_pairs(send, "row", lambda i: i ^ 1)
    rim_grad = around(rim_grad, "row", 1)
    mine, *sends = small_call(
        half_sum_kernel, [keep, other], [wide] + [narrow] * (chips - 1), "half_sum", [pltpu.VMEM((n, n), jnp.float32)]
    )
    others = [permute_pairs(sends[s - 1], "row", lambda i: i ^ (2 * s)) for s in range(1, chips)]
    total, send = small_call(row_sum_kernel, [mine, *others], [wide, narrow], "row_sum")
    others = [permute_pairs(send, "col", lambda i: i ^ s) for s in range(col_count - 1, 0, -1)]
    others, part = lax.optimization_barrier((others, part))
    (total,) = small_call(full_sum_kernel, [total, *others], [narrow], "full_sum")
    others = [permute_pairs(total, "row", lambda i: i ^ (2 * s)) for s in range(1, chips)]
    half = jax.ShapeDtypeStruct((n, n), jnp.bfloat16)
    (mine,) = small_call(gather_kernel, [total, *others], [half], "gather_half")
    return mine, permute_pairs(mine, "row", lambda i: i ^ 1), rim_grad, part


def per_device(object_slab, probe_field, prop_phase, intensities, corners, slot_source):
    slice_count, pair_count, height, width = object_slab.shape
    n = probe_field.shape[-1]
    row_count = lax.axis_size("row")
    col_count = lax.axis_size("col")
    slot_count = intensities.shape[0]
    me = lax.axis_index("row")

    planes = slice_count * pair_count
    slab = object_slab.reshape(planes, height, width)
    sources = slot_source.reshape(slot_count)
    smem = pl.BlockSpec(memory_space=pltpu.SMEM)
    hbm = pl.BlockSpec(memory_space=pltpu.HBM)
    vmem = pl.BlockSpec(memory_space=pltpu.VMEM)
    small = row_count <= POSITIONS_AT_ONCE

    def kept(shape, kind):
        return pltpu.VMEM(shape, kind) if small else jax.ShapeDtypeStruct(shape, kind)

    def near(array):
        return pltpu.with_memory_space_constraint(array, pltpu.VMEM) if small else array

    tile = (pair_count, height, width)
    spot_shape = (-(-row_count // 8) * 8, 128)
    own_zero = pl.pallas_call(
        own_kernel,
        in_specs=[hbm],
        out_specs=vmem,
        out_shape=kept(tile, jnp.bfloat16),
        scratch_shapes=[
            pltpu.VMEM(tile, jnp.float32),
            pltpu.SemaphoreType.DMA((pair_count * len(chunks(height, 64)),)),
        ],
        compiler_params=pltpu.CompilerParams(vmem_limit_bytes=SMALL_VMEM),
        name="own_zero",
    )(in_hbm(slab))
    rim_zero = around(own_zero[:, :n], "row", -1)
    own_one, table, kernel, vectors, spots, *messages = pl.pallas_call(
        prepare_kernel,
        in_specs=[smem, smem, vmem, hbm, hbm, vmem],
        out_specs=[vmem] * (5 + row_count),
        out_shape=[
            kept(tile, jnp.bfloat16),
            kept((2 * n, 2 * n), jnp.bfloat16),
            kept((2, n, n), jnp.float32),
            kept((row_count, 2, 8, 128), jnp.int32),
            kept(spot_shape, jnp.int32),
        ]
        + [kept((n, n), jnp.bfloat16)] * row_count,
        scratch_shapes=[pltpu.VMEM(tile, jnp.float32), pltpu.SemaphoreType.DMA((2,))],
        compiler_params=pltpu.CompilerParams(vmem_limit_bytes=SMALL_VMEM),
        name="prepare",
    )(corners.reshape(row_count, 2), sources, prop_phase, in_hbm(dft_table(n)), in_hbm(slab), intensities)
    rim_one = around(own_one[:, :n], "row", -1)
    measured = {0: messages[0]}
    late = [s for s in range(1, row_count) if s >= LATE_FROM]
    for s in range(1, row_count):
        if s not in late:
            measured[s] = permute_pairs(messages[s], "row", lambda i: i ^ s)

    count = min(POSITIONS_AT_ONCE, row_count)
    plane = (2, n, n)
    positions = (row_count, 2, n, n)
    block = per_position((count, 2, n, n))
    own_block, rim_block, tables = whole(tile), whole((pair_count, n, width)), whole((2 * n, 2 * n))
    spot_block, vector_block = whole(spot_shape), whole((row_count, 2, 8, 128))
    cutting = [
        pltpu.VMEM((pair_count, (height + n) // 8, 8, width), jnp.float32),
        pltpu.SMEM(spot_shape, jnp.int32),
        pltpu.SemaphoreType.DMA,
    ]
    wide = (row_count, n, 2 * n)
    wide_block = per_position((count, n, 2 * n))
    work = [
        pltpu.VMEM((count, 2 * n, n), jnp.bfloat16),
        pltpu.VMEM((count, n, 2 * n), jnp.bfloat16),
        pltpu.VMEM((count, n, 2 * n), jnp.float32),
    ]
    unit = 2 * n * n * n

    def call(body, in_specs, out_specs, out_shape, units, name, scratch=(), steps=row_count // count):
        return pl.pallas_call(
            body,
            grid=(steps,),
            in_specs=in_specs,
            out_specs=out_specs,
            scratch_shapes=scratch,
            out_shape=out_shape,
            compiler_params=pltpu.CompilerParams(vmem_limit_bytes=LARGE_VMEM),
            cost_estimate=pl.CostEstimate(
                flops=row_count * units * unit, bytes_accessed=2**21, transcendentals=0
            ),
            name=name,
        )

    patch_zero, moved = call(
        first_kernel,
        [spot_block, own_block, rim_block, whole(plane), whole(plane), tables],
        [block, wide_block],
        [kept(positions, jnp.bfloat16), kept(wide, jnp.float32)],
        28,
        "moved",
        scratch=cutting + work,
    )(near(spots), near(own_zero), near(rim_zero), probe_field, near(kernel), near(table))
    moved, waiting = lax.optimization_barrier((moved, [messages[s] for s in late]))
    for s, message in zip(late, waiting):
        measured[s] = permute_pairs(message, "row", lambda i: i ^ s)
    patch_one, far = call(
        second_kernel,
        [spot_block, own_block, rim_block, wide_block, tables],
        [block, wide_block],
        [kept(positions, jnp.bfloat16), kept(wide, jnp.float32)],
        20,
        "far",
        scratch=cutting + work[:2],
    )(near(spots), near(own_one), near(rim_one), near(moved), near(table))
    grad_shape = (planes, row_count, n, n)
    grads, keep, send = call(
        functools.partial(third_kernel, steps=row_count // count),
        [whole(plane), whole(plane), tables, block, block, wide_block, wide_block] + [whole((n, n))] * row_count,
        [whole(grad_shape), whole((n, n)), whole((n, n))],
        [
            kept(grad_shape, jnp.bfloat16),
            kept((n, n), jnp.float32),
            kept((n, n), jnp.bfloat16),
        ],
        24,
        "gradients",
        scratch=[pltpu.VMEM(plane, jnp.float32), pltpu.VMEM((row_count, n, n), jnp.bfloat16)] + work,
    )(
        probe_field, near(kernel), near(table), near(patch_zero), near(patch_one), near(moved), near(far),
        *[near(measured[s]) for s in range(row_count)],
    )
    (rim_grad,) = call(
        functools.partial(place_rim_kernel, height=height),
        [vector_block, whole(grad_shape)],
        [whole((planes, n, width))],
        [kept((planes, n, width), jnp.bfloat16)],
        12,
        "place_rim",
        scratch=[pltpu.VMEM((planes, n, row_count * n), jnp.bfloat16)],
        steps=1,
    )(near(vectors), near(grads))
    (part,) = call(
        place_kernel,
        [vector_block, whole(grad_shape), whole((planes, height, width))],
        [whole((planes, height, width))],
        [kept((planes, height, width), jnp.float32)],
        12,
        "place",
        scratch=[pltpu.VMEM((planes, height, row_count * n), jnp.bfloat16)],
        steps=1,
    )(near(vectors), near(grads), slab)

    mine, other, rim_grad, part = probe_sum(keep, send, rim_grad, part)
    updated_slab = pl.pallas_call(
        finish_kernel,
        in_specs=[vmem, vmem],
        out_specs=hbm,
        out_shape=pltpu.HBM((planes, height, width), jnp.float32),
        scratch_shapes=[
            pltpu.VMEM((planes, height, width), jnp.float32),
            pltpu.SemaphoreType.DMA((planes * len(chunks(height, 128)),)),
        ],
        compiler_params=pltpu.CompilerParams(vmem_limit_bytes=SMALL_VMEM),
        name="finish",
    )(near(part), near(rim_grad)).reshape(object_slab.shape)
    other, updated_slab = lax.optimization_barrier((other, updated_slab))
    (updated_probe,) = small_call(
        functools.partial(probe_kernel, scale=step_probe / (row_count * col_count * slot_count)),
        [probe_field, mine, other],
        [jax.ShapeDtypeStruct(probe_field.shape, jnp.float32)],
        "update_probe",
    )
    return (updated_slab, updated_probe)


def solution(mesh):
    placed = (
        P(None, None, ("groups", "row"), "col"),
        P("groups", None, None),
        P(),
        P(("groups", "row"), "col", None),
        P(("groups", "row"), "col", None),
        P(("groups", "row"), "col"),
    )
    return jax.shard_map(
        per_device,
        mesh=mesh,
        in_specs=placed,
        out_specs=(P(None, None, ("groups", "row"), "col"), P("groups", None, None)),
        check_vma=False,
    )
```

```python
import functools

import jax
import jax.numpy as jnp
import ml_dtypes
import numpy as np
from jax import lax
from jax.experimental import pallas as pl
from jax.experimental.pallas import tpu as pltpu
from jax.sharding import PartitionSpec as P

step_object = 0.05
step_probe = 0.5
SMALL_FLOPS = 1000000000
LATE_FROM = 99
SMALL_VMEM = 8 * 1024 * 1024
LARGE_VMEM = 24 * 1024 * 1024
POSITIONS_AT_ONCE = 4


def permute_pairs(block, axis, partner):
    return lax.ppermute(block, axis, [(i, partner(i)) for i in range(lax.axis_size(axis))])


def around(block, axis, distance):
    size = lax.axis_size(axis)
    return lax.ppermute(block, axis, [(i, (i + distance) % size) for i in range(size)])


def dft_table(length):
    index = np.arange(length)
    angles = (index[:, None] * index[None, :] % length) * (2.0 * np.pi / length)
    scale_factor = 1.0 / np.sqrt(length)
    table_re = (np.cos(angles) * scale_factor).astype(np.float32).astype(ml_dtypes.bfloat16)
    table_im = (-np.sin(angles) * scale_factor).astype(np.float32).astype(ml_dtypes.bfloat16)
    return jnp.asarray(np.block([[table_re, -table_im], [table_im, table_re]]))


def product(a, b):
    return jnp.dot(a, b, preferred_element_type=jnp.float32)


def transform(table_ref, field_ref, middle_ref, out_ref, positions):
    n = field_ref.shape[1] // 2
    for p in positions:
        middle = product(table_ref[...], field_ref[p])
        middle_ref[p, :, n:] = middle[:n].astype(jnp.bfloat16)
        middle_ref[p, :, :n] = middle[n:].astype(jnp.bfloat16)
    for p in positions:
        out_ref[p] = product(middle_ref[p], table_ref[...])


def chunks(n, size=32):
    size = min(size, n)
    return [slice(a, a + size) for a in range(0, n, size)]


def put_forward(field_ref, p, rows, re, im):
    n = field_ref.shape[1] // 2
    field_ref[p, rows] = re.astype(jnp.bfloat16)
    field_ref[p, slice(n + rows.start, n + rows.stop)] = im.astype(jnp.bfloat16)


def put_backward(field_ref, p, rows, re, im):
    put_forward(field_ref, p, rows, im, re)


def get_forward(out_ref, p, rows):
    n = out_ref.shape[1]
    return out_ref[p, rows, n:], out_ref[p, rows, :n]


def get_backward(out_ref, p, rows):
    n = out_ref.shape[1]
    return out_ref[p, rows, :n], out_ref[p, rows, n:]


def one_hot_rows(shape, offset):
    rows = lax.broadcasted_iota(jnp.int32, shape, 0)
    columns = lax.broadcasted_iota(jnp.int32, shape, 1)
    return (columns == rows + offset).astype(jnp.bfloat16)


def one_hot_columns(shape, offset):
    rows = lax.broadcasted_iota(jnp.int32, shape, 0)
    columns = lax.broadcasted_iota(jnp.int32, shape, 1)
    return (rows == columns + offset).astype(jnp.bfloat16)


def spot(corner_ref, position):
    return corner_ref[position, 0, :1, :1], corner_ref[position, 1, :1, :1]


def cut(own_ref, rim_ref, patch_ref, spot_ref, tile_ref, place_ref, sem, base, count):
    n = patch_ref.shape[2]
    height, width = own_ref.shape[1:]
    copy = pltpu.make_async_copy(spot_ref, place_ref, sem)
    copy.start()
    ends = lax.axis_index("row") == lax.axis_size("row") - 1
    for c in range(2):
        tile_ref[c, : height // 8] = own_ref[c].astype(jnp.float32).reshape(height // 8, 8, width)
        rim = jnp.where(ends, 0.0, rim_ref[c].astype(jnp.float32))
        tile_ref[c, height // 8 :] = rim.reshape(-1, 8, width)
    copy.wait()
    within = lax.broadcasted_iota(jnp.int32, (n // 8, 8, width), 1)
    for p in range(count):
        corner_y, corner_x = place_ref[base + p, 0], place_ref[base + p, 1]
        group = corner_y // 8
        shift = corner_y - group * 8
        rows = []
        for c in range(2):
            turned = pltpu.roll(tile_ref[c, pl.ds(group, n // 8 + 1)], 8 - shift, 1)
            rows.append(jnp.where(within < 8 - shift, turned[:-1], turned[1:]).reshape(n, width))
        rows = jnp.concatenate(rows, 0).astype(jnp.bfloat16)
        both = product(rows, one_hot_columns((width, n), corner_x)).astype(jnp.bfloat16)
        patch_ref[p, 0] = both[:n]
        patch_ref[p, 1] = both[n:]


def pair(ref, p, rows):
    return ref[p, 0, rows].astype(jnp.float32), ref[p, 1, rows].astype(jnp.float32)


def own_kernel(slab_hbm, own_ref, wide_ref, sems):
    parts = [(c, rows) for c in range(own_ref.shape[0]) for rows in chunks(own_ref.shape[1], 64)]
    copies = [
        pltpu.make_async_copy(slab_hbm.at[c, rows], wide_ref.at[c, rows], sems.at[i])
        for i, (c, rows) in enumerate(parts)
    ]
    for copy in copies:
        copy.start()
    for (c, rows), copy in zip(parts, copies):
        copy.wait()
        own_ref[c, rows] = wide_ref[c, rows].astype(jnp.bfloat16)


def prepare_kernel(
    corner_ref, source_ref, phase_ref, table_hbm, slab_hbm, intensity_ref,
    own_ref, table_ref, kernel_ref, vector_ref, spot_ref, *rest,
):
    message_refs, wide_ref, sems = rest[:-2], rest[-2], rest[-1]
    planes = own_ref.shape[0]
    slab_copy = pltpu.make_async_copy(slab_hbm.at[pl.ds(planes, planes)], wide_ref, sems.at[0])
    slab_copy.start()
    copy = pltpu.make_async_copy(table_hbm, table_ref, sems.at[1])
    copy.start()
    for s, message_ref in enumerate(message_refs):
        target = lax.axis_index("row") ^ s
        slot = jnp.int32(-1)
        for k in range(intensity_ref.shape[0]):
            slot = jnp.where(source_ref[k] == target, k, slot)
        chosen = intensity_ref[jnp.maximum(slot, 0)]
        message_ref[...] = jnp.where(slot >= 0, chosen, -1.0).astype(jnp.bfloat16)
    lane = lax.broadcasted_iota(jnp.int32, (1, spot_ref.shape[1]), 1)
    for p in range(vector_ref.shape[0]):
        owner = lax.axis_index("row") ^ p
        for k in range(2):
            vector_ref[p, k] = jnp.full(vector_ref.shape[2:], corner_ref[owner, k], jnp.int32)
        spot_ref[p : p + 1] = jnp.where(lane == 0, corner_ref[owner, 0], corner_ref[owner, 1])
    for rows in chunks(phase_ref.shape[0]):
        kernel_ref[0, rows] = jnp.cos(phase_ref[rows])
        kernel_ref[1, rows] = jnp.sin(phase_ref[rows])
    slab_copy.wait()
    own_ref[...] = wide_ref[...].astype(jnp.bfloat16)
    copy.wait()


def first_kernel(
    spot_ref, own_ref, rim_ref, probe_ref, kernel_ref, table_ref, patch_ref, moved_ref,
    tile_ref, place_ref, sem, field_ref, middle_ref, out_ref,
):
    count, _, n, _ = patch_ref.shape
    base = pl.program_id(0) * count
    cut(own_ref, rim_ref, patch_ref, spot_ref, tile_ref, place_ref, sem, base, count)
    for p in range(count):
        for rows in chunks(n):
            q_re, q_im = probe_ref[0, rows], probe_ref[1, rows]
            o_re, o_im = pair(patch_ref, p, rows)
            put_forward(field_ref, p, rows, q_re * o_re - q_im * o_im, q_re * o_im + q_im * o_re)
    transform(table_ref, field_ref, middle_ref, out_ref, range(count))
    for p in range(count):
        for rows in chunks(n):
            k_re, k_im = kernel_ref[0, rows], kernel_ref[1, rows]
            r, i = get_forward(out_ref, p, rows)
            put_backward(field_ref, p, rows, k_re * r - k_im * i, k_re * i + k_im * r)
    transform(table_ref, field_ref, middle_ref, moved_ref, range(count))


def second_kernel(
    spot_ref, own_ref, rim_ref, moved_ref, table_ref, patch_ref, far_ref,
    tile_ref, place_ref, sem, field_ref, middle_ref,
):
    count, _, n, _ = patch_ref.shape
    base = pl.program_id(0) * count
    cut(own_ref, rim_ref, patch_ref, spot_ref, tile_ref, place_ref, sem, base, count)
    for p in range(count):
        for rows in chunks(n):
            m_re, m_im = get_backward(moved_ref, p, rows)
            o_re, o_im = pair(patch_ref, p, rows)
            put_forward(field_ref, p, rows, m_re * o_re - m_im * o_im, m_re * o_im + m_im * o_re)
    transform(table_ref, field_ref, middle_ref, far_ref, range(count))


def third_kernel(probe_ref, kernel_ref, table_ref, zero_ref, one_ref, moved_ref, far_ref, *rest, steps):
    measured_refs = rest[:-8]
    grad_ref, keep_ref, send_ref, probe_grad_ref, measured_ref = rest[-8:-3]
    field_ref, middle_ref, out_ref = rest[-3:]
    count, _, n, _ = zero_ref.shape
    base = pl.program_id(0) * count if steps > 1 else 0

    def start():
        for s, ref in enumerate(measured_refs):
            measured_ref[s] = ref[...]
        probe_grad_ref[...] = jnp.zeros_like(probe_grad_ref)

    if steps > 1:
        pl.when(pl.program_id(0) == 0)(start)

    for p in range(count):
        for rows in chunks(n):
            f_re, f_im = get_forward(far_ref, p, rows)
            measured = measured_ref[base + p, rows] if steps > 1 else measured_refs[p][rows]
            measured = measured.astype(jnp.float32)
            misfit = jnp.where(measured < 0.0, 0.0, f_re * f_re + f_im * f_im - measured)
            put_backward(field_ref, p, rows, misfit * f_re, misfit * f_im)
    transform(table_ref, field_ref, middle_ref, out_ref, range(count))
    for p in range(count):
        for rows in chunks(n):
            b_re, b_im = get_backward(out_ref, p, rows)
            m_re, m_im = get_backward(moved_ref, p, rows)
            o_re, o_im = pair(one_ref, p, rows)
            grad_ref[2, base + p, rows] = (m_re * b_re + m_im * b_im).astype(jnp.bfloat16)
            grad_ref[3, base + p, rows] = (m_re * b_im - m_im * b_re).astype(jnp.bfloat16)
            put_forward(field_ref, p, rows, o_re * b_re + o_im * b_im, o_re * b_im - o_im * b_re)
    transform(table_ref, field_ref, middle_ref, out_ref, range(count))
    for p in range(count):
        for rows in chunks(n):
            k_re, k_im = kernel_ref[0, rows], kernel_ref[1, rows]
            r, i = get_forward(out_ref, p, rows)
            put_backward(field_ref, p, rows, k_re * r + k_im * i, k_re * i - k_im * r)
    transform(table_ref, field_ref, middle_ref, out_ref, range(count))
    for rows in chunks(n):
        total_re, total_im = (probe_grad_ref[0, rows], probe_grad_ref[1, rows]) if steps > 1 else (0.0, 0.0)
        q_re, q_im = probe_ref[0, rows], probe_ref[1, rows]
        for p in range(count):
            b_re, b_im = get_backward(out_ref, p, rows)
            o_re, o_im = pair(zero_ref, p, rows)
            grad_ref[0, base + p, rows] = (q_re * b_re + q_im * b_im).astype(jnp.bfloat16)
            grad_ref[1, base + p, rows] = (q_re * b_im - q_im * b_re).astype(jnp.bfloat16)
            total_re += o_re * b_re + o_im * b_im
            total_im += o_re * b_im - o_im * b_re
        probe_grad_ref[0, rows] = total_re
        probe_grad_ref[1, rows] = total_im

    def end():
        core = lax.axis_index("row") % 2
        keep_ref[...] = probe_grad_ref[core]
        send_ref[...] = probe_grad_ref[1 - core].astype(jnp.bfloat16)

    if steps > 1:
        pl.when(pl.program_id(0) == steps - 1)(end)
    else:
        end()


def placed(corner_ref, grad_ref, tall_ref, rows, width, first_row, first_plane):
    planes = tall_ref.shape[0]
    _, positions, n, _ = grad_ref.shape
    moves = []
    for p in range(positions):
        corner_y, corner_x = spot(corner_ref, p)
        moves.append(one_hot_rows((n, width), corner_x))
        every = jnp.concatenate([grad_ref[first_plane + plane, p] for plane in range(planes)], 1)
        tall = product(one_hot_columns((rows, n), corner_y - first_row), every).astype(jnp.bfloat16)
        for plane in range(planes):
            tall_ref[plane, :, p * n : (p + 1) * n] = tall[:, plane * n : (plane + 1) * n]
    moves = jnp.concatenate(moves, 0)
    for plane in range(planes):
        yield plane, product(tall_ref[plane], moves)


def place_rim_kernel(corner_ref, grad_ref, rim_ref, tall_ref, *, height, first_plane):
    rows, width = rim_ref.shape[1:]
    for plane, total in placed(corner_ref, grad_ref, tall_ref, rows, width, height, first_plane):
        rim_ref[plane] = total.astype(jnp.bfloat16)


def place_kernel(corner_ref, grad_ref, slab_ref, part_ref, tall_ref):
    rows, width = part_ref.shape[1:]
    for plane, total in placed(corner_ref, grad_ref, tall_ref, rows, width, 0, 0):
        part_ref[plane] = slab_ref[plane] - step_object * total


def in_hbm(array):
    return pltpu.with_memory_space_constraint(array, pltpu.HBM)


def finish_kernel(part_ref, *rest):
    rim_refs, (out_hbm, sums_ref, sems) = rest[:-3], rest[-3:]
    each, rim_rows, _ = rim_refs[0].shape
    parts = [(c, rows) for c in range(part_ref.shape[0]) for rows in chunks(part_ref.shape[1], 128)]
    copies = []
    step = jnp.where(lax.axis_index("row") == 0, 0.0, step_object)
    for i, (c, rows) in enumerate(parts):
        value = part_ref[c, rows]
        if rows.start < rim_rows:
            value -= step * rim_refs[c // each][c % each, rows].astype(jnp.float32)
        sums_ref[c, rows] = value
        copies.append(pltpu.make_async_copy(sums_ref.at[c, rows], out_hbm.at[c, rows], sems.at[i]))
        copies[-1].start()
    for copy in copies:
        copy.wait()


def whole(shape):
    return pl.BlockSpec(shape, lambda *_: (0,) * len(shape))


def per_position(shape):
    return pl.BlockSpec(shape, lambda i, *_: (i,) + (0,) * (len(shape) - 1))


def half_sum_kernel(keep_ref, other_ref, mine_ref, *rest):
    send_refs, total_ref = rest[:-1], rest[-1]
    chip = lax.axis_index("row") // 2
    piece = mine_ref.shape[0]
    total_ref[...] = keep_ref[...] + other_ref[...].astype(jnp.float32)
    mine_ref[...] = total_ref[pl.ds(pl.multiple_of(chip * piece, piece), piece)]
    for s, send_ref in enumerate(send_refs, 1):
        rows = pl.ds(pl.multiple_of((chip ^ s) * piece, piece), piece)
        send_ref[...] = total_ref[rows].astype(jnp.bfloat16)


def row_sum_kernel(mine_ref, *rest):
    other_refs, total_ref, send_ref = rest[:-2], rest[-2], rest[-1]
    total = mine_ref[...]
    for other_ref in other_refs:
        total += other_ref[...].astype(jnp.float32)
    total_ref[...] = total
    send_ref[...] = total.astype(jnp.bfloat16)


def full_sum_kernel(mine_ref, *rest):
    other_refs, total_ref = rest[:-1], rest[-1]
    total = mine_ref[...]
    for other_ref in other_refs:
        total += other_ref[...].astype(jnp.float32)
    total_ref[...] = total.astype(jnp.bfloat16)


def gather_kernel(mine_ref, *rest):
    other_refs, half_ref = rest[:-1], rest[-1]
    chip = lax.axis_index("row") // 2
    piece = mine_ref.shape[0]
    for s, ref in enumerate((mine_ref,) + other_refs):
        half_ref[pl.ds(pl.multiple_of((chip ^ s) * piece, piece), piece)] = ref[...]


def probe_kernel(probe_ref, mine_ref, other_ref, out_ref, *, scale):
    core = lax.axis_index("row") % 2
    out_ref[core] = probe_ref[core] - scale * mine_ref[...].astype(jnp.float32)
    out_ref[1 - core] = probe_ref[1 - core] - scale * other_ref[...].astype(jnp.float32)


def small_call(body, arrays, out_shape, name, scratch=()):
    return pl.pallas_call(
        body,
        in_specs=[pl.BlockSpec(memory_space=pltpu.VMEM)] * len(arrays),
        out_specs=[pl.BlockSpec(memory_space=pltpu.VMEM)] * len(out_shape),
        out_shape=out_shape,
        scratch_shapes=scratch,
        compiler_params=pltpu.CompilerParams(vmem_limit_bytes=SMALL_VMEM),
        cost_estimate=pl.CostEstimate(flops=SMALL_FLOPS, bytes_accessed=2**18, transcendentals=0),
        name=name,
    )(*arrays)


def probe_sum(keep, send, rim_grads, part):
    n = keep.shape[0]
    row_count, col_count = lax.axis_size("row"), lax.axis_size("col")
    chips = row_count // 2
    shape = (n // chips, n)
    wide, narrow = jax.ShapeDtypeStruct(shape, jnp.float32), jax.ShapeDtypeStruct(shape, jnp.bfloat16)
    other = permute_pairs(send, "row", lambda i: i ^ 1)
    other, rim_grads[0] = lax.optimization_barrier((other, rim_grads[0]))
    rim_grads = [around(rim_grad, "row", 1) for rim_grad in rim_grads]
    mine, *sends = small_call(
        half_sum_kernel, [keep, other], [wide] + [narrow] * (chips - 1), "half_sum", [pltpu.VMEM((n, n), jnp.float32)]
    )
    others = [permute_pairs(sends[s - 1], "row", lambda i: i ^ (2 * s)) for s in range(1, chips)]
    total, send = small_call(row_sum_kernel, [mine, *others], [wide, narrow], "row_sum")
    steps = [1] + list(range(col_count - 1, 1, -1)) if col_count > 1 else []
    others = [permute_pairs(send, "col", lambda i: i ^ s) for s in steps]
    others, part = lax.optimization_barrier((others, part))
    (total,) = small_call(full_sum_kernel, [total, *others], [narrow], "full_sum")
    others = [permute_pairs(total, "row", lambda i: i ^ (2 * s)) for s in range(1, chips)]
    half = jax.ShapeDtypeStruct((n, n), jnp.bfloat16)
    (mine,) = small_call(gather_kernel, [total, *others], [half], "gather_half")
    return mine, permute_pairs(mine, "row", lambda i: i ^ 1), rim_grads, part


def per_device(object_slab, probe_field, prop_phase, intensities, corners, slot_source):
    slice_count, pair_count, height, width = object_slab.shape
    n = probe_field.shape[-1]
    row_count = lax.axis_size("row")
    col_count = lax.axis_size("col")
    slot_count = intensities.shape[0]
    me = lax.axis_index("row")

    planes = slice_count * pair_count
    slab = object_slab.reshape(planes, height, width)
    sources = slot_source.reshape(slot_count)
    smem = pl.BlockSpec(memory_space=pltpu.SMEM)
    hbm = pl.BlockSpec(memory_space=pltpu.HBM)
    vmem = pl.BlockSpec(memory_space=pltpu.VMEM)
    small = row_count <= POSITIONS_AT_ONCE

    def kept(shape, kind):
        return pltpu.VMEM(shape, kind) if small else jax.ShapeDtypeStruct(shape, kind)

    def near(array):
        return pltpu.with_memory_space_constraint(array, pltpu.VMEM) if small else array

    tile = (pair_count, height, width)
    spot_shape = (-(-row_count // 8) * 8, 128)
    own_zero = pl.pallas_call(
        own_kernel,
        in_specs=[hbm],
        out_specs=vmem,
        out_shape=kept(tile, jnp.bfloat16),
        scratch_shapes=[
            pltpu.VMEM(tile, jnp.float32),
            pltpu.SemaphoreType.DMA((pair_count * len(chunks(height, 64)),)),
        ],
        compiler_params=pltpu.CompilerParams(vmem_limit_bytes=SMALL_VMEM),
        name="own_zero",
    )(in_hbm(slab))
    rim_zero = around(own_zero[:, :n], "row", -1)
    own_one, table, kernel, vectors, spots, *messages = pl.pallas_call(
        prepare_kernel,
        in_specs=[smem, smem, vmem, hbm, hbm, vmem],
        out_specs=[vmem] * (5 + row_count),
        out_shape=[
            kept(tile, jnp.bfloat16),
            kept((2 * n, 2 * n), jnp.bfloat16),
            kept((2, n, n), jnp.float32),
            kept((row_count, 2, 8, 128), jnp.int32),
            kept(spot_shape, jnp.int32),
        ]
        + [kept((n, n), jnp.bfloat16)] * row_count,
        scratch_shapes=[pltpu.VMEM(tile, jnp.float32), pltpu.SemaphoreType.DMA((2,))],
        compiler_params=pltpu.CompilerParams(vmem_limit_bytes=SMALL_VMEM),
        name="prepare",
    )(corners.reshape(row_count, 2), sources, prop_phase, in_hbm(dft_table(n)), in_hbm(slab), intensities)
    rim_one = around(own_one[:, :n], "row", -1)
    measured = {0: messages[0]}
    late = [s for s in range(1, row_count) if s >= LATE_FROM]
    for s in range(1, row_count):
        if s not in late:
            measured[s] = permute_pairs(messages[s], "row", lambda i: i ^ s)

    count = min(POSITIONS_AT_ONCE, row_count)
    plane = (2, n, n)
    positions = (row_count, 2, n, n)
    block = per_position((count, 2, n, n))
    own_block, rim_block, tables = whole(tile), whole((pair_count, n, width)), whole((2 * n, 2 * n))
    spot_block, vector_block = whole(spot_shape), whole((row_count, 2, 8, 128))
    cutting = [
        pltpu.VMEM((pair_count, (height + n) // 8, 8, width), jnp.float32),
        pltpu.SMEM(spot_shape, jnp.int32),
        pltpu.SemaphoreType.DMA,
    ]
    wide = (row_count, n, 2 * n)
    wide_block = per_position((count, n, 2 * n))
    work = [
        pltpu.VMEM((count, 2 * n, n), jnp.bfloat16),
        pltpu.VMEM((count, n, 2 * n), jnp.bfloat16),
        pltpu.VMEM((count, n, 2 * n), jnp.float32),
    ]
    unit = 2 * n * n * n

    def call(body, in_specs, out_specs, out_shape, units, name, scratch=(), steps=row_count // count):
        return pl.pallas_call(
            body,
            grid=(steps,),
            in_specs=in_specs,
            out_specs=out_specs,
            scratch_shapes=scratch,
            out_shape=out_shape,
            compiler_params=pltpu.CompilerParams(vmem_limit_bytes=LARGE_VMEM),
            cost_estimate=pl.CostEstimate(
                flops=row_count * units * unit, bytes_accessed=2**21, transcendentals=0
            ),
            name=name,
        )

    patch_zero, moved = call(
        first_kernel,
        [spot_block, own_block, rim_block, whole(plane), whole(plane), tables],
        [block, wide_block],
        [kept(positions, jnp.bfloat16), kept(wide, jnp.float32)],
        28,
        "moved",
        scratch=cutting + work,
    )(near(spots), near(own_zero), near(rim_zero), probe_field, near(kernel), near(table))
    moved, waiting = lax.optimization_barrier((moved, [messages[s] for s in late]))
    for s, message in zip(late, waiting):
        measured[s] = permute_pairs(message, "row", lambda i: i ^ s)
    patch_one, far = call(
        second_kernel,
        [spot_block, own_block, rim_block, wide_block, tables],
        [block, wide_block],
        [kept(positions, jnp.bfloat16), kept(wide, jnp.float32)],
        20,
        "far",
        scratch=cutting + work[:2],
    )(near(spots), near(own_one), near(rim_one), near(moved), near(table))
    grad_shape = (planes, row_count, n, n)
    grads, keep, send = call(
        functools.partial(third_kernel, steps=row_count // count),
        [whole(plane), whole(plane), tables, block, block, wide_block, wide_block] + [whole((n, n))] * row_count,
        [whole(grad_shape), whole((n, n)), whole((n, n))],
        [
            kept(grad_shape, jnp.bfloat16),
            kept((n, n), jnp.float32),
            kept((n, n), jnp.bfloat16),
        ],
        24,
        "gradients",
        scratch=[pltpu.VMEM(plane, jnp.float32), pltpu.VMEM((row_count, n, n), jnp.bfloat16)] + work,
    )(
        probe_field, near(kernel), near(table), near(patch_zero), near(patch_one), near(moved), near(far),
        *[near(measured[s]) for s in range(row_count)],
    )
    rim_grads = []
    for piece in range(slice_count):
        rim_grads += call(
            functools.partial(place_rim_kernel, height=height, first_plane=piece * pair_count),
            [vector_block, whole(grad_shape)],
            [whole((pair_count, n, width))],
            [kept((pair_count, n, width), jnp.bfloat16)],
            6,
            "place_rim",
            scratch=[pltpu.VMEM((pair_count, n, row_count * n), jnp.bfloat16)],
            steps=1,
        )(near(vectors), near(grads))
    (part,) = call(
        place_kernel,
        [vector_block, whole(grad_shape), whole((planes, height, width))],
        [whole((planes, height, width))],
        [kept((planes, height, width), jnp.float32)],
        12,
        "place",
        scratch=[pltpu.VMEM((planes, height, row_count * n), jnp.bfloat16)],
        steps=1,
    )(near(vectors), near(grads), slab)

    mine, other, rim_grads, part = probe_sum(keep, send, rim_grads, part)
    updated_slab = pl.pallas_call(
        finish_kernel,
        in_specs=[vmem] * (1 + slice_count),
        out_specs=hbm,
        out_shape=pltpu.HBM((planes, height, width), jnp.float32),
        scratch_shapes=[
            pltpu.VMEM((planes, height, width), jnp.float32),
            pltpu.SemaphoreType.DMA((planes * len(chunks(height, 128)),)),
        ],
        compiler_params=pltpu.CompilerParams(vmem_limit_bytes=SMALL_VMEM),
        name="finish",
    )(near(part), *[near(rim) for rim in rim_grads]).reshape(object_slab.shape)
    other, updated_slab = lax.optimization_barrier((other, updated_slab))
    (updated_probe,) = small_call(
        functools.partial(probe_kernel, scale=step_probe / (row_count * col_count * slot_count)),
        [probe_field, mine, other],
        [jax.ShapeDtypeStruct(probe_field.shape, jnp.float32)],
        "update_probe",
    )
    return (updated_slab, updated_probe)


def solution(mesh):
    placed = (
        P(None, None, ("groups", "row"), "col"),
        P("groups", None, None),
        P(),
        P(("groups", "row"), "col", None),
        P(("groups", "row"), "col", None),
        P(("groups", "row"), "col"),
    )
    return jax.shard_map(
        per_device,
        mesh=mesh,
        in_specs=placed,
        out_specs=(P(None, None, ("groups", "row"), "col"), P("groups", None, None)),
        check_vma=False,
    )
```

```python
import functools

import jax
import jax.numpy as jnp
import ml_dtypes
import numpy as np
from jax import lax
from jax.experimental import pallas as pl
from jax.experimental.pallas import tpu as pltpu
from jax.sharding import PartitionSpec as P

step_object = 0.05
step_probe = 0.5
SMALL_FLOPS = 1500000000
LATE_FROM = 99
SMALL_VMEM = 8 * 1024 * 1024
LARGE_VMEM = 24 * 1024 * 1024
POSITIONS_AT_ONCE = 4


def permute_pairs(block, axis, partner):
    return lax.ppermute(block, axis, [(i, partner(i)) for i in range(lax.axis_size(axis))])


def around(block, axis, distance):
    size = lax.axis_size(axis)
    return lax.ppermute(block, axis, [(i, (i + distance) % size) for i in range(size)])


def dft_table(length):
    index = np.arange(length)
    angles = (index[:, None] * index[None, :] % length) * (2.0 * np.pi / length)
    scale_factor = 1.0 / np.sqrt(length)
    table_re = (np.cos(angles) * scale_factor).astype(np.float32).astype(ml_dtypes.bfloat16)
    table_im = (-np.sin(angles) * scale_factor).astype(np.float32).astype(ml_dtypes.bfloat16)
    return jnp.asarray(np.block([[table_re, -table_im], [table_im, table_re]]))


def product(a, b):
    return jnp.dot(a, b, preferred_element_type=jnp.float32)


def transform(table_ref, field_ref, middle_ref, out_ref, positions):
    n = field_ref.shape[1] // 2
    for p in positions:
        middle = product(table_ref[...], field_ref[p])
        middle_ref[p, :, n:] = middle[:n].astype(jnp.bfloat16)
        middle_ref[p, :, :n] = middle[n:].astype(jnp.bfloat16)
    for p in positions:
        out_ref[p] = product(middle_ref[p], table_ref[...])


def chunks(n, size=32):
    size = min(size, n)
    return [slice(a, a + size) for a in range(0, n, size)]


def put_forward(field_ref, p, rows, re, im):
    n = field_ref.shape[1] // 2
    field_ref[p, rows] = re.astype(jnp.bfloat16)
    field_ref[p, slice(n + rows.start, n + rows.stop)] = im.astype(jnp.bfloat16)


def put_backward(field_ref, p, rows, re, im):
    put_forward(field_ref, p, rows, im, re)


def get_forward(out_ref, p, rows):
    n = out_ref.shape[1]
    return out_ref[p, rows, n:], out_ref[p, rows, :n]


def get_backward(out_ref, p, rows):
    n = out_ref.shape[1]
    return out_ref[p, rows, :n], out_ref[p, rows, n:]


def one_hot_rows(shape, offset):
    rows = lax.broadcasted_iota(jnp.int32, shape, 0)
    columns = lax.broadcasted_iota(jnp.int32, shape, 1)
    return (columns == rows + offset).astype(jnp.bfloat16)


def one_hot_columns(shape, offset):
    rows = lax.broadcasted_iota(jnp.int32, shape, 0)
    columns = lax.broadcasted_iota(jnp.int32, shape, 1)
    return (rows == columns + offset).astype(jnp.bfloat16)


def spot(corner_ref, position):
    return corner_ref[position, 0, :1, :1], corner_ref[position, 1, :1, :1]


def cut(own_ref, rim_ref, patch_ref, spot_ref, tile_ref, place_ref, sem, base, count):
    n = patch_ref.shape[2]
    height, width = own_ref.shape[1:]
    copy = pltpu.make_async_copy(spot_ref, place_ref, sem)
    copy.start()
    ends = lax.axis_index("row") == lax.axis_size("row") - 1
    for c in range(2):
        tile_ref[c, : height // 8] = own_ref[c].astype(jnp.float32).reshape(height // 8, 8, width)
        rim = jnp.where(ends, 0.0, rim_ref[c].astype(jnp.float32))
        tile_ref[c, height // 8 :] = rim.reshape(-1, 8, width)
    copy.wait()
    within = lax.broadcasted_iota(jnp.int32, (n // 8, 8, width), 1)
    for p in range(count):
        corner_y, corner_x = place_ref[base + p, 0], place_ref[base + p, 1]
        group = corner_y // 8
        shift = corner_y - group * 8
        rows = []
        for c in range(2):
            turned = pltpu.roll(tile_ref[c, pl.ds(group, n // 8 + 1)], 8 - shift, 1)
            rows.append(jnp.where(within < 8 - shift, turned[:-1], turned[1:]).reshape(n, width))
        rows = jnp.concatenate(rows, 0).astype(jnp.bfloat16)
        both = product(rows, one_hot_columns((width, n), corner_x)).astype(jnp.bfloat16)
        patch_ref[p, 0] = both[:n]
        patch_ref[p, 1] = both[n:]


def pair(ref, p, rows):
    return ref[p, 0, rows].astype(jnp.float32), ref[p, 1, rows].astype(jnp.float32)


def own_kernel(slab_hbm, own_ref, wide_ref, sems):
    parts = [(c, rows) for c in range(own_ref.shape[0]) for rows in chunks(own_ref.shape[1], 64)]
    copies = [
        pltpu.make_async_copy(slab_hbm.at[c, rows], wide_ref.at[c, rows], sems.at[i])
        for i, (c, rows) in enumerate(parts)
    ]
    for copy in copies:
        copy.start()
    for (c, rows), copy in zip(parts, copies):
        copy.wait()
        own_ref[c, rows] = wide_ref[c, rows].astype(jnp.bfloat16)


def prepare_kernel(
    corner_ref, source_ref, phase_ref, table_hbm, slab_hbm, intensity_ref,
    own_ref, table_ref, kernel_ref, vector_ref, spot_ref, *rest,
):
    message_refs, wide_ref, sems = rest[:-2], rest[-2], rest[-1]
    planes = own_ref.shape[0]
    slab_copy = pltpu.make_async_copy(slab_hbm.at[pl.ds(planes, planes)], wide_ref, sems.at[0])
    slab_copy.start()
    copy = pltpu.make_async_copy(table_hbm, table_ref, sems.at[1])
    copy.start()
    for s, message_ref in enumerate(message_refs):
        target = lax.axis_index("row") ^ s
        slot = jnp.int32(-1)
        for k in range(intensity_ref.shape[0]):
            slot = jnp.where(source_ref[k] == target, k, slot)
        chosen = intensity_ref[jnp.maximum(slot, 0)]
        message_ref[...] = jnp.where(slot >= 0, chosen, -1.0).astype(jnp.bfloat16)
    lane = lax.broadcasted_iota(jnp.int32, (1, spot_ref.shape[1]), 1)
    for p in range(vector_ref.shape[0]):
        owner = lax.axis_index("row") ^ p
        for k in range(2):
            vector_ref[p, k] = jnp.full(vector_ref.shape[2:], corner_ref[owner, k], jnp.int32)
        spot_ref[p : p + 1] = jnp.where(lane == 0, corner_ref[owner, 0], corner_ref[owner, 1])
    for rows in chunks(phase_ref.shape[0]):
        kernel_ref[0, rows] = jnp.cos(phase_ref[rows])
        kernel_ref[1, rows] = jnp.sin(phase_ref[rows])
    slab_copy.wait()
    own_ref[...] = wide_ref[...].astype(jnp.bfloat16)
    copy.wait()


def first_kernel(
    spot_ref, own_ref, rim_ref, probe_ref, kernel_ref, table_ref, patch_ref, moved_ref,
    tile_ref, place_ref, sem, field_ref, middle_ref, out_ref,
):
    count, _, n, _ = patch_ref.shape
    base = pl.program_id(0) * count
    cut(own_ref, rim_ref, patch_ref, spot_ref, tile_ref, place_ref, sem, base, count)
    for p in range(count):
        for rows in chunks(n):
            q_re, q_im = probe_ref[0, rows], probe_ref[1, rows]
            o_re, o_im = pair(patch_ref, p, rows)
            put_forward(field_ref, p, rows, q_re * o_re - q_im * o_im, q_re * o_im + q_im * o_re)
    transform(table_ref, field_ref, middle_ref, out_ref, range(count))
    for p in range(count):
        for rows in chunks(n):
            k_re, k_im = kernel_ref[0, rows], kernel_ref[1, rows]
            r, i = get_forward(out_ref, p, rows)
            put_backward(field_ref, p, rows, k_re * r - k_im * i, k_re * i + k_im * r)
    transform(table_ref, field_ref, middle_ref, moved_ref, range(count))


def second_kernel(
    spot_ref, own_ref, rim_ref, moved_ref, table_ref, patch_ref, far_ref,
    tile_ref, place_ref, sem, field_ref, middle_ref,
):
    count, _, n, _ = patch_ref.shape
    base = pl.program_id(0) * count
    cut(own_ref, rim_ref, patch_ref, spot_ref, tile_ref, place_ref, sem, base, count)
    for p in range(count):
        for rows in chunks(n):
            m_re, m_im = get_backward(moved_ref, p, rows)
            o_re, o_im = pair(patch_ref, p, rows)
            put_forward(field_ref, p, rows, m_re * o_re - m_im * o_im, m_re * o_im + m_im * o_re)
    transform(table_ref, field_ref, middle_ref, far_ref, range(count))


def third_kernel(probe_ref, kernel_ref, table_ref, zero_ref, one_ref, moved_ref, far_ref, *rest, steps):
    measured_refs = rest[:-8]
    grad_ref, keep_ref, send_ref, probe_grad_ref, measured_ref = rest[-8:-3]
    field_ref, middle_ref, out_ref = rest[-3:]
    count, _, n, _ = zero_ref.shape
    base = pl.program_id(0) * count if steps > 1 else 0

    def start():
        for s, ref in enumerate(measured_refs):
            measured_ref[s] = ref[...]
        probe_grad_ref[...] = jnp.zeros_like(probe_grad_ref)

    if steps > 1:
        pl.when(pl.program_id(0) == 0)(start)

    for p in range(count):
        for rows in chunks(n):
            f_re, f_im = get_forward(far_ref, p, rows)
            measured = measured_ref[base + p, rows] if steps > 1 else measured_refs[p][rows]
            measured = measured.astype(jnp.float32)
            misfit = jnp.where(measured < 0.0, 0.0, f_re * f_re + f_im * f_im - measured)
            put_backward(field_ref, p, rows, misfit * f_re, misfit * f_im)
    transform(table_ref, field_ref, middle_ref, out_ref, range(count))
    for p in range(count):
        for rows in chunks(n):
            b_re, b_im = get_backward(out_ref, p, rows)
            m_re, m_im = get_backward(moved_ref, p, rows)
            o_re, o_im = pair(one_ref, p, rows)
            grad_ref[2, base + p, rows] = (m_re * b_re + m_im * b_im).astype(jnp.bfloat16)
            grad_ref[3, base + p, rows] = (m_re * b_im - m_im * b_re).astype(jnp.bfloat16)
            put_forward(field_ref, p, rows, o_re * b_re + o_im * b_im, o_re * b_im - o_im * b_re)
    transform(table_ref, field_ref, middle_ref, out_ref, range(count))
    for p in range(count):
        for rows in chunks(n):
            k_re, k_im = kernel_ref[0, rows], kernel_ref[1, rows]
            r, i = get_forward(out_ref, p, rows)
            put_backward(field_ref, p, rows, k_re * r + k_im * i, k_re * i - k_im * r)
    transform(table_ref, field_ref, middle_ref, out_ref, range(count))
    for rows in chunks(n):
        total_re, total_im = (probe_grad_ref[0, rows], probe_grad_ref[1, rows]) if steps > 1 else (0.0, 0.0)
        q_re, q_im = probe_ref[0, rows], probe_ref[1, rows]
        for p in range(count):
            b_re, b_im = get_backward(out_ref, p, rows)
            o_re, o_im = pair(zero_ref, p, rows)
            grad_ref[0, base + p, rows] = (q_re * b_re + q_im * b_im).astype(jnp.bfloat16)
            grad_ref[1, base + p, rows] = (q_re * b_im - q_im * b_re).astype(jnp.bfloat16)
            total_re += o_re * b_re + o_im * b_im
            total_im += o_re * b_im - o_im * b_re
        probe_grad_ref[0, rows] = total_re
        probe_grad_ref[1, rows] = total_im

    def end():
        core = lax.axis_index("row") % 2
        keep_ref[...] = probe_grad_ref[core]
        send_ref[...] = probe_grad_ref[1 - core].astype(jnp.bfloat16)

    if steps > 1:
        pl.when(pl.program_id(0) == steps - 1)(end)
    else:
        end()


def placed(corner_ref, grad_ref, tall_ref, rows, width, first_row, first_plane):
    planes = tall_ref.shape[0]
    _, positions, n, _ = grad_ref.shape
    moves = []
    for p in range(positions):
        corner_y, corner_x = spot(corner_ref, p)
        moves.append(one_hot_rows((n, width), corner_x))
        every = jnp.concatenate([grad_ref[first_plane + plane, p] for plane in range(planes)], 1)
        tall = product(one_hot_columns((rows, n), corner_y - first_row), every).astype(jnp.bfloat16)
        for plane in range(planes):
            tall_ref[plane, :, p * n : (p + 1) * n] = tall[:, plane * n : (plane + 1) * n]
    moves = jnp.concatenate(moves, 0)
    for plane in range(planes):
        yield plane, product(tall_ref[plane], moves)


def place_rim_kernel(corner_ref, grad_ref, rim_ref, tall_ref, *, height, first_plane):
    rows, width = rim_ref.shape[1:]
    for plane, total in placed(corner_ref, grad_ref, tall_ref, rows, width, height, first_plane):
        rim_ref[plane] = total.astype(jnp.bfloat16)


def place_kernel(corner_ref, grad_ref, slab_ref, part_ref, tall_ref):
    rows, width = part_ref.shape[1:]
    for plane, total in placed(corner_ref, grad_ref, tall_ref, rows, width, 0, 0):
        part_ref[plane] = slab_ref[plane] - step_object * total


def in_hbm(array):
    return pltpu.with_memory_space_constraint(array, pltpu.HBM)


def finish_kernel(part_ref, rim_ref, *rest, first_plane):
    out_hbm, sums_ref, sems = rest[-3:]
    parts = [(c, rows) for c in range(rim_ref.shape[0]) for rows in chunks(part_ref.shape[1], 128)]
    copies = []
    step = jnp.where(lax.axis_index("row") == 0, 0.0, step_object)
    for i, (c, rows) in enumerate(parts):
        value = part_ref[first_plane + c, rows]
        if rows.start < rim_ref.shape[1]:
            value -= step * rim_ref[c, rows].astype(jnp.float32)
        sums_ref[c, rows] = value
        copies.append(pltpu.make_async_copy(sums_ref.at[c, rows], out_hbm.at[first_plane + c, rows], sems.at[i]))
        copies[-1].start()
    for copy in copies:
        copy.wait()


def whole(shape):
    return pl.BlockSpec(shape, lambda *_: (0,) * len(shape))


def per_position(shape):
    return pl.BlockSpec(shape, lambda i, *_: (i,) + (0,) * (len(shape) - 1))


def half_sum_kernel(keep_ref, other_ref, mine_ref, *rest):
    send_refs, total_ref = rest[:-1], rest[-1]
    chip = lax.axis_index("row") // 2
    piece = mine_ref.shape[0]
    total_ref[...] = keep_ref[...] + other_ref[...].astype(jnp.float32)
    mine_ref[...] = total_ref[pl.ds(pl.multiple_of(chip * piece, piece), piece)]
    for s, send_ref in enumerate(send_refs, 1):
        rows = pl.ds(pl.multiple_of((chip ^ s) * piece, piece), piece)
        send_ref[...] = total_ref[rows].astype(jnp.bfloat16)


def row_sum_kernel(mine_ref, *rest):
    other_refs, total_ref, send_ref = rest[:-2], rest[-2], rest[-1]
    total = mine_ref[...]
    for other_ref in other_refs:
        total += other_ref[...].astype(jnp.float32)
    total_ref[...] = total
    send_ref[...] = total.astype(jnp.bfloat16)


def full_sum_kernel(mine_ref, *rest):
    other_refs, total_ref = rest[:-1], rest[-1]
    total = mine_ref[...]
    for other_ref in other_refs:
        total += other_ref[...].astype(jnp.float32)
    total_ref[...] = total.astype(jnp.bfloat16)


def gather_kernel(mine_ref, *rest):
    other_refs, half_ref = rest[:-1], rest[-1]
    chip = lax.axis_index("row") // 2
    piece = mine_ref.shape[0]
    for s, ref in enumerate((mine_ref,) + other_refs):
        half_ref[pl.ds(pl.multiple_of((chip ^ s) * piece, piece), piece)] = ref[...]


def probe_kernel(probe_ref, mine_ref, other_ref, out_ref, *, scale):
    core = lax.axis_index("row") % 2
    out_ref[core] = probe_ref[core] - scale * mine_ref[...].astype(jnp.float32)
    out_ref[1 - core] = probe_ref[1 - core] - scale * other_ref[...].astype(jnp.float32)


def small_call(body, arrays, out_shape, name, scratch=()):
    return pl.pallas_call(
        body,
        in_specs=[pl.BlockSpec(memory_space=pltpu.VMEM)] * len(arrays),
        out_specs=[pl.BlockSpec(memory_space=pltpu.VMEM)] * len(out_shape),
        out_shape=out_shape,
        scratch_shapes=scratch,
        compiler_params=pltpu.CompilerParams(vmem_limit_bytes=SMALL_VMEM),
        cost_estimate=pl.CostEstimate(flops=SMALL_FLOPS, bytes_accessed=2**18, transcendentals=0),
        name=name,
    )(*arrays)


def probe_sum(keep, send, rim_grads, part, finish):
    n = keep.shape[0]
    row_count, col_count = lax.axis_size("row"), lax.axis_size("col")
    chips = row_count // 2
    shape = (n // chips, n)
    wide, narrow = jax.ShapeDtypeStruct(shape, jnp.float32), jax.ShapeDtypeStruct(shape, jnp.bfloat16)
    other = permute_pairs(send, "row", lambda i: i ^ 1)
    other, rim_grads[0] = lax.optimization_barrier((other, rim_grads[0]))
    rim_grads = [around(rim_grad, "row", 1) for rim_grad in rim_grads]
    mine, *sends = small_call(
        half_sum_kernel, [keep, other], [wide] + [narrow] * (chips - 1), "half_sum", [pltpu.VMEM((n, n), jnp.float32)]
    )
    others = [permute_pairs(sends[s - 1], "row", lambda i: i ^ (2 * s)) for s in range(1, chips)]
    total, send = small_call(row_sum_kernel, [mine, *others], [wide, narrow], "row_sum")
    steps = [1] + list(range(col_count - 1, 1, -1)) if col_count > 1 else []
    others = [permute_pairs(send, "col", lambda i: i ^ s) for s in steps]
    others, part = lax.optimization_barrier((others, part))
    (total,) = small_call(full_sum_kernel, [total, *others], [narrow], "full_sum")
    others = [permute_pairs(total, "row", lambda i: i ^ (2 * s)) for s in range(1, chips)]
    others, updated = lax.optimization_barrier((others, finish(0, part, rim_grads[0], None)))
    half = jax.ShapeDtypeStruct((n, n), jnp.bfloat16)
    (mine,) = small_call(gather_kernel, [total, *others], [half], "gather_half")
    other = permute_pairs(mine, "row", lambda i: i ^ 1)
    for piece in range(1, len(rim_grads)):
        updated = finish(piece, part, rim_grads[piece], updated)
    other, updated = lax.optimization_barrier((other, updated))
    return mine, other, updated


def per_device(object_slab, probe_field, prop_phase, intensities, corners, slot_source):
    slice_count, pair_count, height, width = object_slab.shape
    n = probe_field.shape[-1]
    row_count = lax.axis_size("row")
    col_count = lax.axis_size("col")
    slot_count = intensities.shape[0]
    me = lax.axis_index("row")

    planes = slice_count * pair_count
    slab = object_slab.reshape(planes, height, width)
    sources = slot_source.reshape(slot_count)
    smem = pl.BlockSpec(memory_space=pltpu.SMEM)
    hbm = pl.BlockSpec(memory_space=pltpu.HBM)
    vmem = pl.BlockSpec(memory_space=pltpu.VMEM)
    small = row_count <= POSITIONS_AT_ONCE

    def kept(shape, kind):
        return pltpu.VMEM(shape, kind) if small else jax.ShapeDtypeStruct(shape, kind)

    def near(array):
        return pltpu.with_memory_space_constraint(array, pltpu.VMEM) if small else array

    tile = (pair_count, height, width)
    spot_shape = (-(-row_count // 8) * 8, 128)
    own_zero = pl.pallas_call(
        own_kernel,
        in_specs=[hbm],
        out_specs=vmem,
        out_shape=kept(tile, jnp.bfloat16),
        scratch_shapes=[
            pltpu.VMEM(tile, jnp.float32),
            pltpu.SemaphoreType.DMA((pair_count * len(chunks(height, 64)),)),
        ],
        compiler_params=pltpu.CompilerParams(vmem_limit_bytes=SMALL_VMEM),
        name="own_zero",
    )(in_hbm(slab))
    rim_zero = around(own_zero[:, :n], "row", -1)
    own_one, table, kernel, vectors, spots, *messages = pl.pallas_call(
        prepare_kernel,
        in_specs=[smem, smem, vmem, hbm, hbm, vmem],
        out_specs=[vmem] * (5 + row_count),
        out_shape=[
            kept(tile, jnp.bfloat16),
            kept((2 * n, 2 * n), jnp.bfloat16),
            kept((2, n, n), jnp.float32),
            kept((row_count, 2, 8, 128), jnp.int32),
            kept(spot_shape, jnp.int32),
        ]
        + [kept((n, n), jnp.bfloat16)] * row_count,
        scratch_shapes=[pltpu.VMEM(tile, jnp.float32), pltpu.SemaphoreType.DMA((2,))],
        compiler_params=pltpu.CompilerParams(vmem_limit_bytes=SMALL_VMEM),
        name="prepare",
    )(corners.reshape(row_count, 2), sources, prop_phase, in_hbm(dft_table(n)), in_hbm(slab), intensities)
    rim_one = around(own_one[:, :n], "row", -1)
    measured = {0: messages[0]}
    late = [s for s in range(1, row_count) if s >= LATE_FROM]
    for s in range(1, row_count):
        if s not in late:
            measured[s] = permute_pairs(messages[s], "row", lambda i: i ^ s)

    count = min(POSITIONS_AT_ONCE, row_count)
    plane = (2, n, n)
    positions = (row_count, 2, n, n)
    block = per_position((count, 2, n, n))
    own_block, rim_block, tables = whole(tile), whole((pair_count, n, width)), whole((2 * n, 2 * n))
    spot_block, vector_block = whole(spot_shape), whole((row_count, 2, 8, 128))
    cutting = [
        pltpu.VMEM((pair_count, (height + n) // 8, 8, width), jnp.float32),
        pltpu.SMEM(spot_shape, jnp.int32),
        pltpu.SemaphoreType.DMA,
    ]
    wide = (row_count, n, 2 * n)
    wide_block = per_position((count, n, 2 * n))
    work = [
        pltpu.VMEM((count, 2 * n, n), jnp.bfloat16),
        pltpu.VMEM((count, n, 2 * n), jnp.bfloat16),
        pltpu.VMEM((count, n, 2 * n), jnp.float32),
    ]
    unit = 2 * n * n * n

    def call(body, in_specs, out_specs, out_shape, units, name, scratch=(), steps=row_count // count):
        return pl.pallas_call(
            body,
            grid=(steps,),
            in_specs=in_specs,
            out_specs=out_specs,
            scratch_shapes=scratch,
            out_shape=out_shape,
            compiler_params=pltpu.CompilerParams(vmem_limit_bytes=LARGE_VMEM),
            cost_estimate=pl.CostEstimate(
                flops=row_count * units * unit, bytes_accessed=2**21, transcendentals=0
            ),
            name=name,
        )

    patch_zero, moved = call(
        first_kernel,
        [spot_block, own_block, rim_block, whole(plane), whole(plane), tables],
        [block, wide_block],
        [kept(positions, jnp.bfloat16), kept(wide, jnp.float32)],
        28,
        "moved",
        scratch=cutting + work,
    )(near(spots), near(own_zero), near(rim_zero), probe_field, near(kernel), near(table))
    moved, waiting = lax.optimization_barrier((moved, [messages[s] for s in late]))
    for s, message in zip(late, waiting):
        measured[s] = permute_pairs(message, "row", lambda i: i ^ s)
    patch_one, far = call(
        second_kernel,
        [spot_block, own_block, rim_block, wide_block, tables],
        [block, wide_block],
        [kept(positions, jnp.bfloat16), kept(wide, jnp.float32)],
        20,
        "far",
        scratch=cutting + work[:2],
    )(near(spots), near(own_one), near(rim_one), near(moved), near(table))
    grad_shape = (planes, row_count, n, n)
    grads, keep, send = call(
        functools.partial(third_kernel, steps=row_count // count),
        [whole(plane), whole(plane), tables, block, block, wide_block, wide_block] + [whole((n, n))] * row_count,
        [whole(grad_shape), whole((n, n)), whole((n, n))],
        [
            kept(grad_shape, jnp.bfloat16),
            kept((n, n), jnp.float32),
            kept((n, n), jnp.bfloat16),
        ],
        24,
        "gradients",
        scratch=[pltpu.VMEM(plane, jnp.float32), pltpu.VMEM((row_count, n, n), jnp.bfloat16)] + work,
    )(
        probe_field, near(kernel), near(table), near(patch_zero), near(patch_one), near(moved), near(far),
        *[near(measured[s]) for s in range(row_count)],
    )
    rim_grads = []
    for piece in range(slice_count):
        rim_grads += call(
            functools.partial(place_rim_kernel, height=height, first_plane=piece * pair_count),
            [vector_block, whole(grad_shape)],
            [whole((pair_count, n, width))],
            [kept((pair_count, n, width), jnp.bfloat16)],
            6,
            "place_rim",
            scratch=[pltpu.VMEM((pair_count, n, row_count * n), jnp.bfloat16)],
            steps=1,
        )(near(vectors), near(grads))
    (part,) = call(
        place_kernel,
        [vector_block, whole(grad_shape), whole((planes, height, width))],
        [whole((planes, height, width))],
        [kept((planes, height, width), jnp.float32)],
        12,
        "place",
        scratch=[pltpu.VMEM((planes, height, row_count * n), jnp.bfloat16)],
        steps=1,
    )(near(vectors), near(grads), slab)

    def finish(piece, part, rim, updated):
        given = [near(part), near(rim)] + ([] if updated is None else [updated])
        return pl.pallas_call(
            functools.partial(finish_kernel, first_plane=piece * pair_count),
            in_specs=[vmem, vmem] + [hbm] * (len(given) - 2),
            out_specs=hbm,
            out_shape=pltpu.HBM((planes, height, width), jnp.float32),
            scratch_shapes=[
                pltpu.VMEM(tile, jnp.float32),
                pltpu.SemaphoreType.DMA((pair_count * len(chunks(height, 128)),)),
            ],
            input_output_aliases={} if updated is None else {2: 0},
            compiler_params=pltpu.CompilerParams(vmem_limit_bytes=SMALL_VMEM),
            name="finish",
        )(*given)

    mine, other, updated_slab = probe_sum(keep, send, rim_grads, part, finish)
    updated_slab = updated_slab.reshape(object_slab.shape)
    (updated_probe,) = small_call(
        functools.partial(probe_kernel, scale=step_probe / (row_count * col_count * slot_count)),
        [probe_field, mine, other],
        [jax.ShapeDtypeStruct(probe_field.shape, jnp.float32)],
        "update_probe",
    )
    return (updated_slab, updated_probe)


def solution(mesh):
    placed = (
        P(None, None, ("groups", "row"), "col"),
        P("groups", None, None),
        P(),
        P(("groups", "row"), "col", None),
        P(("groups", "row"), "col", None),
        P(("groups", "row"), "col"),
    )
    return jax.shard_map(
        per_device,
        mesh=mesh,
        in_specs=placed,
        out_specs=(P(None, None, ("groups", "row"), "col"), P("groups", None, None)),
        check_vma=False,
    )
```

```python
import functools

import jax
import jax.numpy as jnp
import ml_dtypes
import numpy as np
from jax import lax
from jax.experimental import pallas as pl
from jax.experimental.pallas import tpu as pltpu
from jax.sharding import PartitionSpec as P

step_object = 0.05
step_probe = 0.5
SMALL_FLOPS = 1500000000
LATE_FROM = 99
SMALL_VMEM = 8 * 1024 * 1024
LARGE_VMEM = 24 * 1024 * 1024
POSITIONS_AT_ONCE = 4


def permute_pairs(block, axis, partner):
    return lax.ppermute(block, axis, [(i, partner(i)) for i in range(lax.axis_size(axis))])


def around(block, axis, distance):
    size = lax.axis_size(axis)
    return lax.ppermute(block, axis, [(i, (i + distance) % size) for i in range(size)])


def dft_table(length):
    index = np.arange(length)
    angles = (index[:, None] * index[None, :] % length) * (2.0 * np.pi / length)
    scale_factor = 1.0 / np.sqrt(length)
    table_re = (np.cos(angles) * scale_factor).astype(np.float32).astype(ml_dtypes.bfloat16)
    table_im = (-np.sin(angles) * scale_factor).astype(np.float32).astype(ml_dtypes.bfloat16)
    return jnp.asarray(np.block([[table_re, -table_im], [table_im, table_re]]))


def product(a, b):
    return jnp.dot(a, b, preferred_element_type=jnp.float32)


def transform(table_ref, field_ref, middle_ref, out_ref, positions):
    n = field_ref.shape[1] // 2
    for p in positions:
        middle = product(table_ref[...], field_ref[p])
        middle_ref[p, :, n:] = middle[:n].astype(jnp.bfloat16)
        middle_ref[p, :, :n] = middle[n:].astype(jnp.bfloat16)
    for p in positions:
        out_ref[p] = product(middle_ref[p], table_ref[...])


def chunks(n, size=32):
    size = min(size, n)
    return [slice(a, a + size) for a in range(0, n, size)]


def put_forward(field_ref, p, rows, re, im):
    n = field_ref.shape[1] // 2
    field_ref[p, rows] = re.astype(jnp.bfloat16)
    field_ref[p, slice(n + rows.start, n + rows.stop)] = im.astype(jnp.bfloat16)


def put_backward(field_ref, p, rows, re, im):
    put_forward(field_ref, p, rows, im, re)


def get_forward(out_ref, p, rows):
    n = out_ref.shape[1]
    return out_ref[p, rows, n:], out_ref[p, rows, :n]


def get_backward(out_ref, p, rows):
    n = out_ref.shape[1]
    return out_ref[p, rows, :n], out_ref[p, rows, n:]


def one_hot_rows(shape, offset):
    rows = lax.broadcasted_iota(jnp.int32, shape, 0)
    columns = lax.broadcasted_iota(jnp.int32, shape, 1)
    return (columns == rows + offset).astype(jnp.bfloat16)


def one_hot_columns(shape, offset):
    rows = lax.broadcasted_iota(jnp.int32, shape, 0)
    columns = lax.broadcasted_iota(jnp.int32, shape, 1)
    return (rows == columns + offset).astype(jnp.bfloat16)


def spot(corner_ref, position):
    return corner_ref[position, 0, :1, :1], corner_ref[position, 1, :1, :1]


def cut(own_ref, rim_ref, patch_ref, spot_ref, tile_ref, place_ref, sem, base, count):
    n = patch_ref.shape[2]
    height, width = own_ref.shape[1:]
    copy = pltpu.make_async_copy(spot_ref, place_ref, sem)
    copy.start()
    ends = lax.axis_index("row") == lax.axis_size("row") - 1
    for c in range(2):
        tile_ref[c, : height // 8] = own_ref[c].astype(jnp.float32).reshape(height // 8, 8, width)
        rim = jnp.where(ends, 0.0, rim_ref[c].astype(jnp.float32))
        tile_ref[c, height // 8 :] = rim.reshape(-1, 8, width)
    copy.wait()
    window = min(n + 128, width)
    within = lax.broadcasted_iota(jnp.int32, (n // 8, 8, window), 1)
    for p in range(count):
        corner_y, corner_x = place_ref[base + p, 0], place_ref[base + p, 1]
        group = corner_y // 8
        shift = corner_y - group * 8
        left = pl.multiple_of(jnp.minimum(corner_x // 128 * 128, width - window), 128)
        rows = []
        for c in range(2):
            turned = pltpu.roll(tile_ref[c, pl.ds(group, n // 8 + 1), :, pl.ds(left, window)], 8 - shift, 1)
            rows.append(jnp.where(within < 8 - shift, turned[:-1], turned[1:]).reshape(n, window))
        rows = jnp.concatenate(rows, 0).astype(jnp.bfloat16)
        both = product(rows, one_hot_columns((window, n), corner_x - left)).astype(jnp.bfloat16)
        patch_ref[p, 0] = both[:n]
        patch_ref[p, 1] = both[n:]


def pair(ref, p, rows):
    return ref[p, 0, rows].astype(jnp.float32), ref[p, 1, rows].astype(jnp.float32)


def own_kernel(slab_hbm, own_ref, wide_ref, sems):
    parts = [(c, rows) for c in range(own_ref.shape[0]) for rows in chunks(own_ref.shape[1], 256)]
    copies = [
        pltpu.make_async_copy(slab_hbm.at[c, rows], wide_ref.at[c, rows], sems.at[i])
        for i, (c, rows) in enumerate(parts)
    ]
    for copy in copies:
        copy.start()
    for (c, rows), copy in zip(parts, copies):
        copy.wait()
        own_ref[c, rows] = wide_ref[c, rows].astype(jnp.bfloat16)


def prepare_kernel(
    corner_ref, source_ref, phase_ref, table_hbm, slab_hbm, intensity_ref,
    own_ref, table_ref, kernel_ref, vector_ref, spot_ref, *rest,
):
    message_refs, wide_ref, sems = rest[:-2], rest[-2], rest[-1]
    planes = own_ref.shape[0]
    slab_copy = pltpu.make_async_copy(slab_hbm.at[pl.ds(planes, planes)], wide_ref, sems.at[0])
    slab_copy.start()
    copy = pltpu.make_async_copy(table_hbm, table_ref, sems.at[1])
    copy.start()
    for s, message_ref in enumerate(message_refs):
        target = lax.axis_index("row") ^ s
        slot = jnp.int32(-1)
        for k in range(intensity_ref.shape[0]):
            slot = jnp.where(source_ref[k] == target, k, slot)
        chosen = intensity_ref[jnp.maximum(slot, 0)]
        message_ref[...] = jnp.where(slot >= 0, chosen, -1.0).astype(jnp.bfloat16)
    lane = lax.broadcasted_iota(jnp.int32, (1, spot_ref.shape[1]), 1)
    for p in range(vector_ref.shape[0]):
        owner = lax.axis_index("row") ^ p
        for k in range(2):
            vector_ref[p, k] = jnp.full(vector_ref.shape[2:], corner_ref[owner, k], jnp.int32)
        spot_ref[p : p + 1] = jnp.where(lane == 0, corner_ref[owner, 0], corner_ref[owner, 1])
    for rows in chunks(phase_ref.shape[0]):
        kernel_ref[0, rows] = jnp.cos(phase_ref[rows])
        kernel_ref[1, rows] = jnp.sin(phase_ref[rows])
    slab_copy.wait()
    own_ref[...] = wide_ref[...].astype(jnp.bfloat16)
    copy.wait()


def first_kernel(
    spot_ref, own_ref, rim_ref, probe_ref, kernel_ref, table_ref, patch_ref, moved_ref,
    tile_ref, place_ref, sem, field_ref, middle_ref, out_ref,
):
    count, _, n, _ = patch_ref.shape
    base = pl.program_id(0) * count
    cut(own_ref, rim_ref, patch_ref, spot_ref, tile_ref, place_ref, sem, base, count)
    for p in range(count):
        for rows in chunks(n):
            q_re, q_im = probe_ref[0, rows], probe_ref[1, rows]
            o_re, o_im = pair(patch_ref, p, rows)
            put_forward(field_ref, p, rows, q_re * o_re - q_im * o_im, q_re * o_im + q_im * o_re)
    transform(table_ref, field_ref, middle_ref, out_ref, range(count))
    for p in range(count):
        for rows in chunks(n):
            k_re, k_im = kernel_ref[0, rows], kernel_ref[1, rows]
            r, i = get_forward(out_ref, p, rows)
            put_backward(field_ref, p, rows, k_re * r - k_im * i, k_re * i + k_im * r)
    transform(table_ref, field_ref, middle_ref, moved_ref, range(count))


def second_kernel(
    spot_ref, own_ref, rim_ref, moved_ref, table_ref, patch_ref, far_ref,
    tile_ref, place_ref, sem, field_ref, middle_ref,
):
    count, _, n, _ = patch_ref.shape
    base = pl.program_id(0) * count
    cut(own_ref, rim_ref, patch_ref, spot_ref, tile_ref, place_ref, sem, base, count)
    for p in range(count):
        for rows in chunks(n):
            m_re, m_im = get_backward(moved_ref, p, rows)
            o_re, o_im = pair(patch_ref, p, rows)
            put_forward(field_ref, p, rows, m_re * o_re - m_im * o_im, m_re * o_im + m_im * o_re)
    transform(table_ref, field_ref, middle_ref, far_ref, range(count))


def third_kernel(probe_ref, kernel_ref, table_ref, zero_ref, one_ref, moved_ref, far_ref, *rest, steps):
    measured_refs = rest[:-8]
    grad_ref, keep_ref, send_ref, probe_grad_ref, measured_ref = rest[-8:-3]
    field_ref, middle_ref, out_ref = rest[-3:]
    count, _, n, _ = zero_ref.shape
    base = pl.program_id(0) * count if steps > 1 else 0

    def start():
        for s, ref in enumerate(measured_refs):
            measured_ref[s] = ref[...]
        probe_grad_ref[...] = jnp.zeros_like(probe_grad_ref)

    if steps > 1:
        pl.when(pl.program_id(0) == 0)(start)

    for p in range(count):
        for rows in chunks(n):
            f_re, f_im = get_forward(far_ref, p, rows)
            measured = measured_ref[base + p, rows] if steps > 1 else measured_refs[p][rows]
            measured = measured.astype(jnp.float32)
            misfit = jnp.where(measured < 0.0, 0.0, f_re * f_re + f_im * f_im - measured)
            put_backward(field_ref, p, rows, misfit * f_re, misfit * f_im)
    transform(table_ref, field_ref, middle_ref, out_ref, range(count))
    for p in range(count):
        for rows in chunks(n):
            b_re, b_im = get_backward(out_ref, p, rows)
            m_re, m_im = get_backward(moved_ref, p, rows)
            o_re, o_im = pair(one_ref, p, rows)
            grad_ref[2, base + p, rows] = (m_re * b_re + m_im * b_im).astype(jnp.bfloat16)
            grad_ref[3, base + p, rows] = (m_re * b_im - m_im * b_re).astype(jnp.bfloat16)
            put_forward(field_ref, p, rows, o_re * b_re + o_im * b_im, o_re * b_im - o_im * b_re)
    transform(table_ref, field_ref, middle_ref, out_ref, range(count))
    for p in range(count):
        for rows in chunks(n):
            k_re, k_im = kernel_ref[0, rows], kernel_ref[1, rows]
            r, i = get_forward(out_ref, p, rows)
            put_backward(field_ref, p, rows, k_re * r + k_im * i, k_re * i - k_im * r)
    transform(table_ref, field_ref, middle_ref, out_ref, range(count))
    for rows in chunks(n):
        total_re, total_im = (probe_grad_ref[0, rows], probe_grad_ref[1, rows]) if steps > 1 else (0.0, 0.0)
        q_re, q_im = probe_ref[0, rows], probe_ref[1, rows]
        for p in range(count):
            b_re, b_im = get_backward(out_ref, p, rows)
            o_re, o_im = pair(zero_ref, p, rows)
            grad_ref[0, base + p, rows] = (q_re * b_re + q_im * b_im).astype(jnp.bfloat16)
            grad_ref[1, base + p, rows] = (q_re * b_im - q_im * b_re).astype(jnp.bfloat16)
            total_re += o_re * b_re + o_im * b_im
            total_im += o_re * b_im - o_im * b_re
        probe_grad_ref[0, rows] = total_re
        probe_grad_ref[1, rows] = total_im

    def end():
        core = lax.axis_index("row") % 2
        keep_ref[...] = probe_grad_ref[core]
        send_ref[...] = probe_grad_ref[1 - core].astype(jnp.bfloat16)

    if steps > 1:
        pl.when(pl.program_id(0) == steps - 1)(end)
    else:
        end()


def placed(corner_ref, grad_ref, tall_ref, rows, width, first_row, first_plane):
    planes = tall_ref.shape[0]
    _, positions, n, _ = grad_ref.shape
    moves = []
    for p in range(positions):
        corner_y, corner_x = spot(corner_ref, p)
        moves.append(one_hot_rows((n, width), corner_x))
        every = jnp.concatenate([grad_ref[first_plane + plane, p] for plane in range(planes)], 1)
        tall = product(one_hot_columns((rows, n), corner_y - first_row), every).astype(jnp.bfloat16)
        for plane in range(planes):
            tall_ref[plane, :, p * n : (p + 1) * n] = tall[:, plane * n : (plane + 1) * n]
    moves = jnp.concatenate(moves, 0)
    for plane in range(planes):
        yield plane, product(tall_ref[plane], moves)


def place_rim_kernel(corner_ref, grad_ref, rim_ref, tall_ref, *, height, first_plane):
    rows, width = rim_ref.shape[1:]
    for plane, total in placed(corner_ref, grad_ref, tall_ref, rows, width, height, first_plane):
        rim_ref[plane] = total.astype(jnp.bfloat16)


def place_kernel(corner_ref, grad_ref, slab_ref, part_ref, tall_ref):
    rows, width = part_ref.shape[1:]
    for plane, total in placed(corner_ref, grad_ref, tall_ref, rows, width, 0, 0):
        part_ref[plane] = slab_ref[plane] - step_object * total


def in_hbm(array):
    return pltpu.with_memory_space_constraint(array, pltpu.HBM)


def finish_kernel(part_ref, rim_ref, *rest, first_plane):
    out_hbm, sums_ref, sems = rest[-3:]
    parts = [(c, rows) for c in range(rim_ref.shape[0]) for rows in chunks(part_ref.shape[1], 128)]
    copies = []
    step = jnp.where(lax.axis_index("row") == 0, 0.0, step_object)
    for i, (c, rows) in enumerate(parts):
        value = part_ref[first_plane + c, rows]
        if rows.start < rim_ref.shape[1]:
            value -= step * rim_ref[c, rows].astype(jnp.float32)
        sums_ref[c, rows] = value
        copies.append(pltpu.make_async_copy(sums_ref.at[c, rows], out_hbm.at[first_plane + c, rows], sems.at[i]))
        copies[-1].start()
    for copy in copies:
        copy.wait()


def whole(shape):
    return pl.BlockSpec(shape, lambda *_: (0,) * len(shape))


def per_position(shape):
    return pl.BlockSpec(shape, lambda i, *_: (i,) + (0,) * (len(shape) - 1))


def half_sum_kernel(keep_ref, other_ref, mine_ref, *rest):
    send_refs, total_ref = rest[:-1], rest[-1]
    chip = lax.axis_index("row") // 2
    piece = mine_ref.shape[0]
    total_ref[...] = keep_ref[...] + other_ref[...].astype(jnp.float32)
    mine_ref[...] = total_ref[pl.ds(pl.multiple_of(chip * piece, piece), piece)]
    for s, send_ref in enumerate(send_refs, 1):
        rows = pl.ds(pl.multiple_of((chip ^ s) * piece, piece), piece)
        send_ref[...] = total_ref[rows].astype(jnp.bfloat16)


def row_sum_kernel(mine_ref, *rest):
    other_refs, total_ref, send_ref = rest[:-2], rest[-2], rest[-1]
    total = mine_ref[...]
    for other_ref in other_refs:
        total += other_ref[...].astype(jnp.float32)
    total_ref[...] = total
    send_ref[...] = total.astype(jnp.bfloat16)


def full_sum_kernel(mine_ref, *rest):
    other_refs, total_ref = rest[:-1], rest[-1]
    total = mine_ref[...]
    for other_ref in other_refs:
        total += other_ref[...].astype(jnp.float32)
    total_ref[...] = total.astype(jnp.bfloat16)


def gather_kernel(mine_ref, *rest):
    other_refs, half_ref = rest[:-1], rest[-1]
    chip = lax.axis_index("row") // 2
    piece = mine_ref.shape[0]
    for s, ref in enumerate((mine_ref,) + other_refs):
        half_ref[pl.ds(pl.multiple_of((chip ^ s) * piece, piece), piece)] = ref[...]


def probe_kernel(probe_ref, mine_ref, other_ref, out_hbm, sums_ref, sems, *, scale):
    core = lax.axis_index("row") % 2
    copies = []
    for half, (plane, ref) in enumerate([(core, mine_ref), (1 - core, other_ref)]):
        for i, rows in enumerate(chunks(ref.shape[0], 128)):
            sums_ref[plane, rows] = probe_ref[plane, rows] - scale * ref[rows].astype(jnp.float32)
            sem = sems.at[half, i]
            copies.append(pltpu.make_async_copy(sums_ref.at[plane, rows], out_hbm.at[plane, rows], sem))
            copies[-1].start()
    for copy in copies:
        copy.wait()


def small_call(body, arrays, out_shape, name, scratch=()):
    return pl.pallas_call(
        body,
        in_specs=[pl.BlockSpec(memory_space=pltpu.VMEM)] * len(arrays),
        out_specs=[pl.BlockSpec(memory_space=pltpu.VMEM)] * len(out_shape),
        out_shape=out_shape,
        scratch_shapes=scratch,
        compiler_params=pltpu.CompilerParams(vmem_limit_bytes=SMALL_VMEM),
        cost_estimate=pl.CostEstimate(flops=SMALL_FLOPS, bytes_accessed=2**18, transcendentals=0),
        name=name,
    )(*arrays)


def probe_sum(keep, send, rim_grads, part, finish):
    n = keep.shape[0]
    row_count, col_count = lax.axis_size("row"), lax.axis_size("col")
    chips = row_count // 2
    shape = (n // chips, n)
    wide, narrow = jax.ShapeDtypeStruct(shape, jnp.float32), jax.ShapeDtypeStruct(shape, jnp.bfloat16)
    other = permute_pairs(send, "row", lambda i: i ^ 1)
    other, rim_grads[0] = lax.optimization_barrier((other, rim_grads[0]))
    rim_grads = [around(rim_grad, "row", 1) for rim_grad in rim_grads]
    mine, *sends = small_call(
        half_sum_kernel, [keep, other], [wide] + [narrow] * (chips - 1), "half_sum", [pltpu.VMEM((n, n), jnp.float32)]
    )
    others = [permute_pairs(sends[s - 1], "row", lambda i: i ^ (2 * s)) for s in range(1, chips)]
    total, send = small_call(row_sum_kernel, [mine, *others], [wide, narrow], "row_sum")
    steps = [1] + list(range(col_count - 1, 1, -1)) if col_count > 1 else []
    others = [permute_pairs(send, "col", lambda i: i ^ s) for s in steps]
    others, part = lax.optimization_barrier((others, part))
    (total,) = small_call(full_sum_kernel, [total, *others], [narrow], "full_sum")
    others = [permute_pairs(total, "row", lambda i: i ^ (2 * s)) for s in range(1, chips)]
    others, updated = lax.optimization_barrier((others, finish(0, part, rim_grads[0], None)))
    half = jax.ShapeDtypeStruct((n, n), jnp.bfloat16)
    (mine,) = small_call(gather_kernel, [total, *others], [half], "gather_half")
    other = permute_pairs(mine, "row", lambda i: i ^ 1)
    for piece in range(1, len(rim_grads)):
        updated = finish(piece, part, rim_grads[piece], updated)
    other, updated = lax.optimization_barrier((other, updated))
    return mine, other, updated


def per_device(object_slab, probe_field, prop_phase, intensities, corners, slot_source):
    slice_count, pair_count, height, width = object_slab.shape
    n = probe_field.shape[-1]
    row_count = lax.axis_size("row")
    col_count = lax.axis_size("col")
    slot_count = intensities.shape[0]
    me = lax.axis_index("row")

    planes = slice_count * pair_count
    slab = object_slab.reshape(planes, height, width)
    sources = slot_source.reshape(slot_count)
    smem = pl.BlockSpec(memory_space=pltpu.SMEM)
    hbm = pl.BlockSpec(memory_space=pltpu.HBM)
    vmem = pl.BlockSpec(memory_space=pltpu.VMEM)
    small = row_count <= POSITIONS_AT_ONCE

    def kept(shape, kind):
        return pltpu.VMEM(shape, kind) if small else jax.ShapeDtypeStruct(shape, kind)

    def near(array):
        return pltpu.with_memory_space_constraint(array, pltpu.VMEM) if small else array

    tile = (pair_count, height, width)
    spot_shape = (-(-row_count // 8) * 8, 128)
    own_zero = pl.pallas_call(
        own_kernel,
        in_specs=[hbm],
        out_specs=vmem,
        out_shape=kept(tile, jnp.bfloat16),
        scratch_shapes=[
            pltpu.VMEM(tile, jnp.float32),
            pltpu.SemaphoreType.DMA((pair_count * len(chunks(height, 256)),)),
        ],
        compiler_params=pltpu.CompilerParams(vmem_limit_bytes=SMALL_VMEM),
        name="own_zero",
    )(in_hbm(slab))
    rim_zero = around(own_zero[:, :n], "row", -1)
    own_one, table, kernel, vectors, spots, *messages = pl.pallas_call(
        prepare_kernel,
        in_specs=[smem, smem, vmem, hbm, hbm, vmem],
        out_specs=[vmem] * (5 + row_count),
        out_shape=[
            kept(tile, jnp.bfloat16),
            kept((2 * n, 2 * n), jnp.bfloat16),
            kept((2, n, n), jnp.float32),
            kept((row_count, 2, 8, 128), jnp.int32),
            kept(spot_shape, jnp.int32),
        ]
        + [kept((n, n), jnp.bfloat16)] * row_count,
        scratch_shapes=[pltpu.VMEM(tile, jnp.float32), pltpu.SemaphoreType.DMA((2,))],
        compiler_params=pltpu.CompilerParams(vmem_limit_bytes=SMALL_VMEM),
        name="prepare",
    )(corners.reshape(row_count, 2), sources, prop_phase, in_hbm(dft_table(n)), in_hbm(slab), intensities)
    rim_one = around(own_one[:, :n], "row", -1)
    measured = {0: messages[0]}
    late = [s for s in range(1, row_count) if s >= LATE_FROM]
    for s in range(1, row_count):
        if s not in late:
            measured[s] = permute_pairs(messages[s], "row", lambda i: i ^ s)

    count = min(POSITIONS_AT_ONCE, row_count)
    plane = (2, n, n)
    positions = (row_count, 2, n, n)
    block = per_position((count, 2, n, n))
    own_block, rim_block, tables = whole(tile), whole((pair_count, n, width)), whole((2 * n, 2 * n))
    spot_block, vector_block = whole(spot_shape), whole((row_count, 2, 8, 128))
    cutting = [
        pltpu.VMEM((pair_count, (height + n) // 8, 8, width), jnp.float32),
        pltpu.SMEM(spot_shape, jnp.int32),
        pltpu.SemaphoreType.DMA,
    ]
    wide = (row_count, n, 2 * n)
    wide_block = per_position((count, n, 2 * n))
    work = [
        pltpu.VMEM((count, 2 * n, n), jnp.bfloat16),
        pltpu.VMEM((count, n, 2 * n), jnp.bfloat16),
        pltpu.VMEM((count, n, 2 * n), jnp.float32),
    ]
    unit = 2 * n * n * n

    def call(body, in_specs, out_specs, out_shape, units, name, scratch=(), steps=row_count // count):
        return pl.pallas_call(
            body,
            grid=(steps,),
            in_specs=in_specs,
            out_specs=out_specs,
            scratch_shapes=scratch,
            out_shape=out_shape,
            compiler_params=pltpu.CompilerParams(vmem_limit_bytes=LARGE_VMEM),
            cost_estimate=pl.CostEstimate(
                flops=row_count * units * unit, bytes_accessed=2**21, transcendentals=0
            ),
            name=name,
        )

    patch_zero, moved = call(
        first_kernel,
        [spot_block, own_block, rim_block, whole(plane), whole(plane), tables],
        [block, wide_block],
        [kept(positions, jnp.bfloat16), kept(wide, jnp.float32)],
        28,
        "moved",
        scratch=cutting + work,
    )(near(spots), near(own_zero), near(rim_zero), near(probe_field), near(kernel), near(table))
    moved, waiting = lax.optimization_barrier((moved, [messages[s] for s in late]))
    for s, message in zip(late, waiting):
        measured[s] = permute_pairs(message, "row", lambda i: i ^ s)
    patch_one, far = call(
        second_kernel,
        [spot_block, own_block, rim_block, wide_block, tables],
        [block, wide_block],
        [kept(positions, jnp.bfloat16), kept(wide, jnp.float32)],
        20,
        "far",
        scratch=cutting + work[:2],
    )(near(spots), near(own_one), near(rim_one), near(moved), near(table))
    grad_shape = (planes, row_count, n, n)
    grads, keep, send = call(
        functools.partial(third_kernel, steps=row_count // count),
        [whole(plane), whole(plane), tables, block, block, wide_block, wide_block] + [whole((n, n))] * row_count,
        [whole(grad_shape), whole((n, n)), whole((n, n))],
        [
            kept(grad_shape, jnp.bfloat16),
            kept((n, n), jnp.float32),
            kept((n, n), jnp.bfloat16),
        ],
        24,
        "gradients",
        scratch=[pltpu.VMEM(plane, jnp.float32), pltpu.VMEM((row_count, n, n), jnp.bfloat16)] + work,
    )(
        near(probe_field), near(kernel), near(table), near(patch_zero), near(patch_one), near(moved), near(far),
        *[near(measured[s]) for s in range(row_count)],
    )
    rim_grads = []
    for piece in range(slice_count):
        rim_grads += call(
            functools.partial(place_rim_kernel, height=height, first_plane=piece * pair_count),
            [vector_block, whole(grad_shape)],
            [whole((pair_count, n, width))],
            [kept((pair_count, n, width), jnp.bfloat16)],
            6,
            "place_rim",
            scratch=[pltpu.VMEM((pair_count, n, row_count * n), jnp.bfloat16)],
            steps=1,
        )(near(vectors), near(grads))
    (part,) = call(
        place_kernel,
        [vector_block, whole(grad_shape), whole((planes, height, width))],
        [whole((planes, height, width))],
        [kept((planes, height, width), jnp.float32)],
        12,
        "place",
        scratch=[pltpu.VMEM((planes, height, row_count * n), jnp.bfloat16)],
        steps=1,
    )(near(vectors), near(grads), slab)

    def finish(piece, part, rim, updated):
        given = [near(part), near(rim)] + ([] if updated is None else [updated])
        return pl.pallas_call(
            functools.partial(finish_kernel, first_plane=piece * pair_count),
            in_specs=[vmem, vmem] + [hbm] * (len(given) - 2),
            out_specs=hbm,
            out_shape=pltpu.HBM((planes, height, width), jnp.float32),
            scratch_shapes=[
                pltpu.VMEM(tile, jnp.float32),
                pltpu.SemaphoreType.DMA((pair_count * len(chunks(height, 128)),)),
            ],
            input_output_aliases={} if updated is None else {2: 0},
            compiler_params=pltpu.CompilerParams(vmem_limit_bytes=SMALL_VMEM),
            name="finish",
        )(*given)

    mine, other, updated_slab = probe_sum(keep, send, rim_grads, part, finish)
    updated_slab = updated_slab.reshape(object_slab.shape)
    updated_probe = pl.pallas_call(
        functools.partial(probe_kernel, scale=step_probe / (row_count * col_count * slot_count)),
        in_specs=[vmem] * 3,
        out_specs=hbm,
        out_shape=pltpu.HBM(probe_field.shape, jnp.float32),
        scratch_shapes=[
            pltpu.VMEM(probe_field.shape, jnp.float32),
            pltpu.SemaphoreType.DMA((2, len(chunks(n, 128)))),
        ],
        compiler_params=pltpu.CompilerParams(vmem_limit_bytes=SMALL_VMEM),
        name="update_probe",
    )(near(probe_field), mine, other)
    return (updated_slab, updated_probe)


def solution(mesh):
    placed = (
        P(None, None, ("groups", "row"), "col"),
        P("groups", None, None),
        P(),
        P(("groups", "row"), "col", None),
        P(("groups", "row"), "col", None),
        P(("groups", "row"), "col"),
    )
    return jax.shard_map(
        per_device,
        mesh=mesh,
        in_specs=placed,
        out_specs=(P(None, None, ("groups", "row"), "col"), P("groups", None, None)),
        check_vma=False,
    )
```

```python
import functools

import jax
import jax.numpy as jnp
import ml_dtypes
import numpy as np
from jax import lax
from jax.experimental import pallas as pl
from jax.experimental.pallas import tpu as pltpu
from jax.sharding import PartitionSpec as P

step_object = 0.05
step_probe = 0.5
SMALL_FLOPS = 1500000000
LATE_FROM = 99
SMALL_VMEM = 8 * 1024 * 1024
LARGE_VMEM = 24 * 1024 * 1024
POSITIONS_AT_ONCE = 4


def permute_pairs(block, axis, partner):
    return lax.ppermute(block, axis, [(i, partner(i)) for i in range(lax.axis_size(axis))])


def around(block, axis, distance):
    size = lax.axis_size(axis)
    return lax.ppermute(block, axis, [(i, (i + distance) % size) for i in range(size)])


def dft_table(length):
    index = np.arange(length)
    angles = (index[:, None] * index[None, :] % length) * (2.0 * np.pi / length)
    scale_factor = 1.0 / np.sqrt(length)
    table_re = (np.cos(angles) * scale_factor).astype(np.float32).astype(ml_dtypes.bfloat16)
    table_im = (-np.sin(angles) * scale_factor).astype(np.float32).astype(ml_dtypes.bfloat16)
    return jnp.asarray(np.block([[table_re, -table_im], [table_im, table_re]]))


def product(a, b):
    return jnp.dot(a, b, preferred_element_type=jnp.float32)


def transform(table_ref, field_ref, middle_ref, out_ref, positions):
    n = field_ref.shape[1] // 2
    for p in positions:
        middle = product(table_ref[...], field_ref[p])
        middle_ref[p, :, n:] = middle[:n].astype(jnp.bfloat16)
        middle_ref[p, :, :n] = middle[n:].astype(jnp.bfloat16)
    for p in positions:
        out_ref[p] = product(middle_ref[p], table_ref[...])


def chunks(n, size=32):
    size = min(size, n)
    return [slice(a, a + size) for a in range(0, n, size)]


def put_forward(field_ref, p, rows, re, im):
    n = field_ref.shape[1] // 2
    field_ref[p, rows] = re.astype(jnp.bfloat16)
    field_ref[p, slice(n + rows.start, n + rows.stop)] = im.astype(jnp.bfloat16)


def put_backward(field_ref, p, rows, re, im):
    put_forward(field_ref, p, rows, im, re)


def get_forward(out_ref, p, rows):
    n = out_ref.shape[1]
    return out_ref[p, rows, n:], out_ref[p, rows, :n]


def get_backward(out_ref, p, rows):
    n = out_ref.shape[1]
    return out_ref[p, rows, :n], out_ref[p, rows, n:]


def one_hot_rows(shape, offset):
    rows = lax.broadcasted_iota(jnp.int32, shape, 0)
    columns = lax.broadcasted_iota(jnp.int32, shape, 1)
    return (columns == rows + offset).astype(jnp.bfloat16)


def one_hot_columns(shape, offset):
    rows = lax.broadcasted_iota(jnp.int32, shape, 0)
    columns = lax.broadcasted_iota(jnp.int32, shape, 1)
    return (rows == columns + offset).astype(jnp.bfloat16)


def spot(corner_ref, position):
    return corner_ref[position, 0, :1, :1], corner_ref[position, 1, :1, :1]


def cut(own_ref, rim_ref, patch_ref, spot_ref, tile_ref, place_ref, sem, base, count):
    n = patch_ref.shape[2]
    height, width = own_ref.shape[1:]
    copy = pltpu.make_async_copy(spot_ref, place_ref, sem)
    copy.start()
    ends = lax.axis_index("row") == lax.axis_size("row") - 1
    for c in range(2):
        tile_ref[c, : height // 8] = own_ref[c].astype(jnp.float32).reshape(height // 8, 8, width)
        rim = jnp.where(ends, 0.0, rim_ref[c].astype(jnp.float32))
        tile_ref[c, height // 8 :] = rim.reshape(-1, 8, width)
    copy.wait()
    within = lax.broadcasted_iota(jnp.int32, (n // 8, 8, width), 1)
    for p in range(count):
        corner_y, corner_x = place_ref[base + p, 0], place_ref[base + p, 1]
        group = corner_y // 8
        shift = corner_y - group * 8
        rows = []
        for c in range(2):
            turned = pltpu.roll(tile_ref[c, pl.ds(group, n // 8 + 1)], 8 - shift, 1)
            rows.append(jnp.where(within < 8 - shift, turned[:-1], turned[1:]).reshape(n, width))
        rows = jnp.concatenate(rows, 0).astype(jnp.bfloat16)
        both = product(rows, one_hot_columns((width, n), corner_x)).astype(jnp.bfloat16)
        patch_ref[p, 0] = both[:n]
        patch_ref[p, 1] = both[n:]


def pair(ref, p, rows):
    return ref[p, 0, rows].astype(jnp.float32), ref[p, 1, rows].astype(jnp.float32)


def own_kernel(slab_hbm, own_ref, wide_ref, sems):
    parts = [(c, rows) for c in range(own_ref.shape[0]) for rows in chunks(own_ref.shape[1], 256)]
    copies = [
        pltpu.make_async_copy(slab_hbm.at[c, rows], wide_ref.at[c, rows], sems.at[i])
        for i, (c, rows) in enumerate(parts)
    ]
    for copy in copies:
        copy.start()
    for (c, rows), copy in zip(parts, copies):
        copy.wait()
        own_ref[c, rows] = wide_ref[c, rows].astype(jnp.bfloat16)


def prepare_kernel(
    corner_ref, source_ref, phase_ref, table_hbm, slab_hbm, intensity_ref,
    own_ref, table_ref, kernel_ref, vector_ref, spot_ref, *rest,
):
    message_refs, wide_ref, sems = rest[:-2], rest[-2], rest[-1]
    planes = own_ref.shape[0]
    slab_copy = pltpu.make_async_copy(slab_hbm.at[pl.ds(planes, planes)], wide_ref, sems.at[0])
    slab_copy.start()
    copy = pltpu.make_async_copy(table_hbm, table_ref, sems.at[1])
    copy.start()
    for s, message_ref in enumerate(message_refs):
        target = lax.axis_index("row") ^ s
        slot = jnp.int32(-1)
        for k in range(intensity_ref.shape[0]):
            slot = jnp.where(source_ref[k] == target, k, slot)
        chosen = intensity_ref[jnp.maximum(slot, 0)]
        message_ref[...] = jnp.where(slot >= 0, chosen, -1.0).astype(jnp.bfloat16)
    lane = lax.broadcasted_iota(jnp.int32, (1, spot_ref.shape[1]), 1)
    for p in range(vector_ref.shape[0]):
        owner = lax.axis_index("row") ^ p
        for k in range(2):
            vector_ref[p, k] = jnp.full(vector_ref.shape[2:], corner_ref[owner, k], jnp.int32)
        spot_ref[p : p + 1] = jnp.where(lane == 0, corner_ref[owner, 0], corner_ref[owner, 1])
    for rows in chunks(phase_ref.shape[0]):
        kernel_ref[0, rows] = jnp.cos(phase_ref[rows])
        kernel_ref[1, rows] = jnp.sin(phase_ref[rows])
    slab_copy.wait()
    own_ref[...] = wide_ref[...].astype(jnp.bfloat16)
    copy.wait()


def first_kernel(
    spot_ref, own_ref, rim_ref, probe_ref, kernel_ref, table_ref, patch_ref, moved_ref,
    tile_ref, place_ref, sem, field_ref, middle_ref, out_ref,
):
    count, _, n, _ = patch_ref.shape
    base = pl.program_id(0) * count
    cut(own_ref, rim_ref, patch_ref, spot_ref, tile_ref, place_ref, sem, base, count)
    for p in range(count):
        for rows in chunks(n):
            q_re, q_im = probe_ref[0, rows], probe_ref[1, rows]
            o_re, o_im = pair(patch_ref, p, rows)
            put_forward(field_ref, p, rows, q_re * o_re - q_im * o_im, q_re * o_im + q_im * o_re)
    transform(table_ref, field_ref, middle_ref, out_ref, range(count))
    for p in range(count):
        for rows in chunks(n):
            k_re, k_im = kernel_ref[0, rows], kernel_ref[1, rows]
            r, i = get_forward(out_ref, p, rows)
            put_backward(field_ref, p, rows, k_re * r - k_im * i, k_re * i + k_im * r)
    transform(table_ref, field_ref, middle_ref, moved_ref, range(count))


def second_kernel(
    spot_ref, own_ref, rim_ref, moved_ref, table_ref, patch_ref, far_ref,
    tile_ref, place_ref, sem, field_ref, middle_ref,
):
    count, _, n, _ = patch_ref.shape
    base = pl.program_id(0) * count
    cut(own_ref, rim_ref, patch_ref, spot_ref, tile_ref, place_ref, sem, base, count)
    for p in range(count):
        for rows in chunks(n):
            m_re, m_im = get_backward(moved_ref, p, rows)
            o_re, o_im = pair(patch_ref, p, rows)
            put_forward(field_ref, p, rows, m_re * o_re - m_im * o_im, m_re * o_im + m_im * o_re)
    transform(table_ref, field_ref, middle_ref, far_ref, range(count))


def third_kernel(probe_ref, kernel_ref, table_ref, zero_ref, one_ref, moved_ref, far_ref, *rest, steps):
    measured_refs = rest[:-8]
    grad_ref, keep_ref, send_ref, probe_grad_ref, measured_ref = rest[-8:-3]
    field_ref, middle_ref, out_ref = rest[-3:]
    count, _, n, _ = zero_ref.shape
    base = pl.program_id(0) * count if steps > 1 else 0

    def start():
        for s, ref in enumerate(measured_refs):
            measured_ref[s] = ref[...]
        probe_grad_ref[...] = jnp.zeros_like(probe_grad_ref)

    if steps > 1:
        pl.when(pl.program_id(0) == 0)(start)

    for p in range(count):
        for rows in chunks(n):
            f_re, f_im = get_forward(far_ref, p, rows)
            measured = measured_ref[base + p, rows] if steps > 1 else measured_refs[p][rows]
            measured = measured.astype(jnp.float32)
            misfit = jnp.where(measured < 0.0, 0.0, f_re * f_re + f_im * f_im - measured)
            put_backward(field_ref, p, rows, misfit * f_re, misfit * f_im)
    transform(table_ref, field_ref, middle_ref, out_ref, range(count))
    for p in range(count):
        for rows in chunks(n):
            b_re, b_im = get_backward(out_ref, p, rows)
            m_re, m_im = get_backward(moved_ref, p, rows)
            o_re, o_im = pair(one_ref, p, rows)
            grad_ref[2, base + p, rows] = (m_re * b_re + m_im * b_im).astype(jnp.bfloat16)
            grad_ref[3, base + p, rows] = (m_re * b_im - m_im * b_re).astype(jnp.bfloat16)
            put_forward(field_ref, p, rows, o_re * b_re + o_im * b_im, o_re * b_im - o_im * b_re)
    transform(table_ref, field_ref, middle_ref, out_ref, range(count))
    for p in range(count):
        for rows in chunks(n):
            k_re, k_im = kernel_ref[0, rows], kernel_ref[1, rows]
            r, i = get_forward(out_ref, p, rows)
            put_backward(field_ref, p, rows, k_re * r + k_im * i, k_re * i - k_im * r)
    transform(table_ref, field_ref, middle_ref, out_ref, range(count))
    for rows in chunks(n):
        total_re, total_im = (probe_grad_ref[0, rows], probe_grad_ref[1, rows]) if steps > 1 else (0.0, 0.0)
        q_re, q_im = probe_ref[0, rows], probe_ref[1, rows]
        for p in range(count):
            b_re, b_im = get_backward(out_ref, p, rows)
            o_re, o_im = pair(zero_ref, p, rows)
            grad_ref[0, base + p, rows] = (q_re * b_re + q_im * b_im).astype(jnp.bfloat16)
            grad_ref[1, base + p, rows] = (q_re * b_im - q_im * b_re).astype(jnp.bfloat16)
            total_re += o_re * b_re + o_im * b_im
            total_im += o_re * b_im - o_im * b_re
        probe_grad_ref[0, rows] = total_re
        probe_grad_ref[1, rows] = total_im

    def end():
        core = lax.axis_index("row") % 2
        keep_ref[...] = probe_grad_ref[core]
        send_ref[...] = probe_grad_ref[1 - core].astype(jnp.bfloat16)

    if steps > 1:
        pl.when(pl.program_id(0) == steps - 1)(end)
    else:
        end()


def placed(corner_ref, grad_ref, tall_ref, rows, width, first_row, first_plane):
    planes = tall_ref.shape[0]
    _, positions, n, _ = grad_ref.shape
    moves = []
    for p in range(positions):
        corner_y, corner_x = spot(corner_ref, p)
        moves.append(one_hot_rows((n, width), corner_x))
        every = jnp.concatenate([grad_ref[first_plane + plane, p] for plane in range(planes)], 1)
        tall = product(one_hot_columns((rows, n), corner_y - first_row), every).astype(jnp.bfloat16)
        for plane in range(planes):
            tall_ref[plane, :, p * n : (p + 1) * n] = tall[:, plane * n : (plane + 1) * n]
    moves = jnp.concatenate(moves, 0)
    for plane in range(planes):
        yield plane, product(tall_ref[plane], moves)


def place_rim_kernel(corner_ref, grad_ref, rim_ref, tall_ref, *, height, first_plane):
    rows, width = rim_ref.shape[1:]
    for plane, total in placed(corner_ref, grad_ref, tall_ref, rows, width, height, first_plane):
        rim_ref[plane] = total.astype(jnp.bfloat16)


def place_kernel(corner_ref, grad_ref, slab_ref, part_ref, tall_ref):
    rows, width = part_ref.shape[1:]
    for plane, total in placed(corner_ref, grad_ref, tall_ref, rows, width, 0, 0):
        part_ref[plane] = slab_ref[plane] - step_object * total


def in_hbm(array):
    return pltpu.with_memory_space_constraint(array, pltpu.HBM)


def finish_kernel(part_ref, rim_ref, *rest, first_plane):
    out_hbm, sums_ref, sems = rest[-3:]
    parts = [(c, rows) for c in range(rim_ref.shape[0]) for rows in chunks(part_ref.shape[1], 128)]
    copies = []
    step = jnp.where(lax.axis_index("row") == 0, 0.0, step_object)
    for i, (c, rows) in enumerate(parts):
        value = part_ref[first_plane + c, rows]
        if rows.start < rim_ref.shape[1]:
            value -= step * rim_ref[c, rows].astype(jnp.float32)
        sums_ref[c, rows] = value
        copies.append(pltpu.make_async_copy(sums_ref.at[c, rows], out_hbm.at[first_plane + c, rows], sems.at[i]))
        copies[-1].start()
    for copy in copies:
        copy.wait()


def whole(shape):
    return pl.BlockSpec(shape, lambda *_: (0,) * len(shape))


def per_position(shape):
    return pl.BlockSpec(shape, lambda i, *_: (i,) + (0,) * (len(shape) - 1))


def half_sum_kernel(keep_ref, other_ref, mine_ref, *rest):
    send_refs, total_ref = rest[:-1], rest[-1]
    chip = lax.axis_index("row") // 2
    piece = mine_ref.shape[0]
    total_ref[...] = keep_ref[...] + other_ref[...].astype(jnp.float32)
    mine_ref[...] = total_ref[pl.ds(pl.multiple_of(chip * piece, piece), piece)]
    for s, send_ref in enumerate(send_refs, 1):
        rows = pl.ds(pl.multiple_of((chip ^ s) * piece, piece), piece)
        send_ref[...] = total_ref[rows].astype(jnp.bfloat16)


def row_sum_kernel(mine_ref, *rest):
    other_refs, total_ref, send_ref = rest[:-2], rest[-2], rest[-1]
    total = mine_ref[...]
    for other_ref in other_refs:
        total += other_ref[...].astype(jnp.float32)
    total_ref[...] = total
    send_ref[...] = total.astype(jnp.bfloat16)


def full_sum_kernel(mine_ref, *rest):
    other_refs, total_ref = rest[:-1], rest[-1]
    total = mine_ref[...]
    for other_ref in other_refs:
        total += other_ref[...].astype(jnp.float32)
    total_ref[...] = total.astype(jnp.bfloat16)


def gather_kernel(mine_ref, *rest):
    other_refs, half_ref = rest[:-1], rest[-1]
    chip = lax.axis_index("row") // 2
    piece = mine_ref.shape[0]
    for s, ref in enumerate((mine_ref,) + other_refs):
        half_ref[pl.ds(pl.multiple_of((chip ^ s) * piece, piece), piece)] = ref[...]


def probe_kernel(probe_ref, mine_ref, other_ref, out_ref, *, scale):
    core = lax.axis_index("row") % 2
    out_ref[core] = probe_ref[core] - scale * mine_ref[...].astype(jnp.float32)
    out_ref[1 - core] = probe_ref[1 - core] - scale * other_ref[...].astype(jnp.float32)


def small_call(body, arrays, out_shape, name, scratch=()):
    return pl.pallas_call(
        body,
        in_specs=[pl.BlockSpec(memory_space=pltpu.VMEM)] * len(arrays),
        out_specs=[pl.BlockSpec(memory_space=pltpu.VMEM)] * len(out_shape),
        out_shape=out_shape,
        scratch_shapes=scratch,
        compiler_params=pltpu.CompilerParams(vmem_limit_bytes=SMALL_VMEM),
        cost_estimate=pl.CostEstimate(flops=SMALL_FLOPS, bytes_accessed=2**18, transcendentals=0),
        name=name,
    )(*arrays)


def probe_sum(keep, send, rim_grads, part, finish):
    n = keep.shape[0]
    row_count, col_count = lax.axis_size("row"), lax.axis_size("col")
    chips = row_count // 2
    shape = (n // chips, n)
    wide, narrow = jax.ShapeDtypeStruct(shape, jnp.float32), jax.ShapeDtypeStruct(shape, jnp.bfloat16)
    other = permute_pairs(send, "row", lambda i: i ^ 1)
    other, rim_grads[0] = lax.optimization_barrier((other, rim_grads[0]))
    rim_grads = [around(rim_grad, "row", 1) for rim_grad in rim_grads]
    mine, *sends = small_call(
        half_sum_kernel, [keep, other], [wide] + [narrow] * (chips - 1), "half_sum", [pltpu.VMEM((n, n), jnp.float32)]
    )
    others = [permute_pairs(sends[s - 1], "row", lambda i: i ^ (2 * s)) for s in range(1, chips)]
    total, send = small_call(row_sum_kernel, [mine, *others], [wide, narrow], "row_sum")
    steps = [1] + list(range(col_count - 1, 1, -1)) if col_count > 1 else []
    others = [permute_pairs(send, "col", lambda i: i ^ s) for s in steps]
    others, part = lax.optimization_barrier((others, part))
    (total,) = small_call(full_sum_kernel, [total, *others], [narrow], "full_sum")
    others = [permute_pairs(total, "row", lambda i: i ^ (2 * s)) for s in range(1, chips)]
    others, updated = lax.optimization_barrier((others, finish(0, part, rim_grads[0], None)))
    half = jax.ShapeDtypeStruct((n, n), jnp.bfloat16)
    (mine,) = small_call(gather_kernel, [total, *others], [half], "gather_half")
    other = permute_pairs(mine, "row", lambda i: i ^ 1)
    for piece in range(1, len(rim_grads)):
        updated = finish(piece, part, rim_grads[piece], updated)
    other, updated = lax.optimization_barrier((other, updated))
    return mine, other, updated


def per_device(object_slab, probe_field, prop_phase, intensities, corners, slot_source):
    slice_count, pair_count, height, width = object_slab.shape
    n = probe_field.shape[-1]
    row_count = lax.axis_size("row")
    col_count = lax.axis_size("col")
    slot_count = intensities.shape[0]
    me = lax.axis_index("row")

    planes = slice_count * pair_count
    slab = object_slab.reshape(planes, height, width)
    sources = slot_source.reshape(slot_count)
    smem = pl.BlockSpec(memory_space=pltpu.SMEM)
    hbm = pl.BlockSpec(memory_space=pltpu.HBM)
    vmem = pl.BlockSpec(memory_space=pltpu.VMEM)
    small = row_count <= POSITIONS_AT_ONCE

    def kept(shape, kind):
        return pltpu.VMEM(shape, kind) if small else jax.ShapeDtypeStruct(shape, kind)

    def near(array):
        return pltpu.with_memory_space_constraint(array, pltpu.VMEM) if small else array

    tile = (pair_count, height, width)
    spot_shape = (-(-row_count // 8) * 8, 128)
    own_zero = pl.pallas_call(
        own_kernel,
        in_specs=[hbm],
        out_specs=vmem,
        out_shape=kept(tile, jnp.bfloat16),
        scratch_shapes=[
            pltpu.VMEM(tile, jnp.float32),
            pltpu.SemaphoreType.DMA((pair_count * len(chunks(height, 256)),)),
        ],
        compiler_params=pltpu.CompilerParams(vmem_limit_bytes=SMALL_VMEM),
        name="own_zero",
    )(in_hbm(slab))
    rim_zero = around(own_zero[:, :n], "row", -1)
    own_one, table, kernel, vectors, spots, *messages = pl.pallas_call(
        prepare_kernel,
        in_specs=[smem, smem, vmem, hbm, hbm, vmem],
        out_specs=[vmem] * (5 + row_count),
        out_shape=[
            kept(tile, jnp.bfloat16),
            kept((2 * n, 2 * n), jnp.bfloat16),
            kept((2, n, n), jnp.float32),
            kept((row_count, 2, 8, 128), jnp.int32),
            kept(spot_shape, jnp.int32),
        ]
        + [kept((n, n), jnp.bfloat16)] * row_count,
        scratch_shapes=[pltpu.VMEM(tile, jnp.float32), pltpu.SemaphoreType.DMA((2,))],
        compiler_params=pltpu.CompilerParams(vmem_limit_bytes=SMALL_VMEM),
        name="prepare",
    )(corners.reshape(row_count, 2), sources, prop_phase, in_hbm(dft_table(n)), in_hbm(slab), intensities)
    rim_one = around(own_one[:, :n], "row", -1)
    measured = {0: messages[0]}
    late = [s for s in range(1, row_count) if s >= LATE_FROM]
    for s in range(1, row_count):
        if s not in late:
            measured[s] = permute_pairs(messages[s], "row", lambda i: i ^ s)

    count = min(POSITIONS_AT_ONCE, row_count)
    plane = (2, n, n)
    positions = (row_count, 2, n, n)
    block = per_position((count, 2, n, n))
    own_block, rim_block, tables = whole(tile), whole((pair_count, n, width)), whole((2 * n, 2 * n))
    spot_block, vector_block = whole(spot_shape), whole((row_count, 2, 8, 128))
    cutting = [
        pltpu.VMEM((pair_count, (height + n) // 8, 8, width), jnp.float32),
        pltpu.SMEM(spot_shape, jnp.int32),
        pltpu.SemaphoreType.DMA,
    ]
    wide = (row_count, n, 2 * n)
    wide_block = per_position((count, n, 2 * n))
    work = [
        pltpu.VMEM((count, 2 * n, n), jnp.bfloat16),
        pltpu.VMEM((count, n, 2 * n), jnp.bfloat16),
        pltpu.VMEM((count, n, 2 * n), jnp.float32),
    ]
    unit = 2 * n * n * n

    def call(body, in_specs, out_specs, out_shape, units, name, scratch=(), steps=row_count // count):
        return pl.pallas_call(
            body,
            grid=(steps,),
            in_specs=in_specs,
            out_specs=out_specs,
            scratch_shapes=scratch,
            out_shape=out_shape,
            compiler_params=pltpu.CompilerParams(vmem_limit_bytes=LARGE_VMEM),
            cost_estimate=pl.CostEstimate(
                flops=row_count * units * unit, bytes_accessed=2**21, transcendentals=0
            ),
            name=name,
        )

    patch_zero, moved = call(
        first_kernel,
        [spot_block, own_block, rim_block, whole(plane), whole(plane), tables],
        [block, wide_block],
        [kept(positions, jnp.bfloat16), kept(wide, jnp.float32)],
        28,
        "moved",
        scratch=cutting + work,
    )(near(spots), near(own_zero), near(rim_zero), probe_field, near(kernel), near(table))
    moved, waiting = lax.optimization_barrier((moved, [messages[s] for s in late]))
    for s, message in zip(late, waiting):
        measured[s] = permute_pairs(message, "row", lambda i: i ^ s)
    patch_one, far = call(
        second_kernel,
        [spot_block, own_block, rim_block, wide_block, tables],
        [block, wide_block],
        [kept(positions, jnp.bfloat16), kept(wide, jnp.float32)],
        20,
        "far",
        scratch=cutting + work[:2],
    )(near(spots), near(own_one), near(rim_one), near(moved), near(table))
    grad_shape = (planes, row_count, n, n)
    grads, keep, send = call(
        functools.partial(third_kernel, steps=row_count // count),
        [whole(plane), whole(plane), tables, block, block, wide_block, wide_block] + [whole((n, n))] * row_count,
        [whole(grad_shape), whole((n, n)), whole((n, n))],
        [
            kept(grad_shape, jnp.bfloat16),
            kept((n, n), jnp.float32),
            kept((n, n), jnp.bfloat16),
        ],
        24,
        "gradients",
        scratch=[pltpu.VMEM(plane, jnp.float32), pltpu.VMEM((row_count, n, n), jnp.bfloat16)] + work,
    )(
        probe_field, near(kernel), near(table), near(patch_zero), near(patch_one), near(moved), near(far),
        *[near(measured[s]) for s in range(row_count)],
    )
    rim_grads = []
    for piece in range(slice_count):
        rim_grads += call(
            functools.partial(place_rim_kernel, height=height, first_plane=piece * pair_count),
            [vector_block, whole(grad_shape)],
            [whole((pair_count, n, width))],
            [kept((pair_count, n, width), jnp.bfloat16)],
            6,
            "place_rim",
            scratch=[pltpu.VMEM((pair_count, n, row_count * n), jnp.bfloat16)],
            steps=1,
        )(near(vectors), near(grads))
    (part,) = call(
        place_kernel,
        [vector_block, whole(grad_shape), whole((planes, height, width))],
        [whole((planes, height, width))],
        [kept((planes, height, width), jnp.float32)],
        12,
        "place",
        scratch=[pltpu.VMEM((planes, height, row_count * n), jnp.bfloat16)],
        steps=1,
    )(near(vectors), near(grads), slab)

    def finish(piece, part, rim, updated):
        given = [near(part), near(rim)] + ([] if updated is None else [updated])
        return pl.pallas_call(
            functools.partial(finish_kernel, first_plane=piece * pair_count),
            in_specs=[vmem, vmem] + [hbm] * (len(given) - 2),
            out_specs=hbm,
            out_shape=pltpu.HBM((planes, height, width), jnp.float32),
            scratch_shapes=[
                pltpu.VMEM(tile, jnp.float32),
                pltpu.SemaphoreType.DMA((pair_count * len(chunks(height, 128)),)),
            ],
            input_output_aliases={} if updated is None else {2: 0},
            compiler_params=pltpu.CompilerParams(vmem_limit_bytes=SMALL_VMEM),
            name="finish",
        )(*given)

    mine, other, updated_slab = probe_sum(keep, send, rim_grads, part, finish)
    updated_slab = updated_slab.reshape(object_slab.shape)
    (updated_probe,) = small_call(
        functools.partial(probe_kernel, scale=step_probe / (row_count * col_count * slot_count)),
        [probe_field, mine, other],
        [jax.ShapeDtypeStruct(probe_field.shape, jnp.float32)],
        "update_probe",
    )
    return (updated_slab, updated_probe)


def solution(mesh):
    placed = (
        P(None, None, ("groups", "row"), "col"),
        P("groups", None, None),
        P(),
        P(("groups", "row"), "col", None),
        P(("groups", "row"), "col", None),
        P(("groups", "row"), "col"),
    )
    return jax.shard_map(
        per_device,
        mesh=mesh,
        in_specs=placed,
        out_specs=(P(None, None, ("groups", "row"), "col"), P("groups", None, None)),
        check_vma=False,
    )
```
